128 devices in a mesh: dp: 16 (over z, y_lo, core), ctx: 8 (over y_hi, x).
Axes of the slice: x: 4, y: 4 (y_hi: 2, y_lo: 2; y = y_hi * 2 + y_lo), z: 4, core: 2. Of those that a mesh axis runs over, the one named last changes fastest.
Arguments:
- tokens: bfloat16 [32, 1024, 1024], P('dp', 'ctx'), may hold values from -6 to 6
- segments: int32 [32, 1024], P('dp'), may hold values from 0 to 254, as said below
- ln_gain: bfloat16 [1024], P('dp'), may hold values from 0.5 to 1.5
- ln_bias: bfloat16 [1024], P('dp'), may hold values from -3 to 3
- w_qkv: bfloat16 [1024, 3072], P('dp'), may hold values from -0.1875 to 0.1875
- b_qkv: bfloat16 [3072], P('dp'), may hold values from -4 to 4
- w_out: bfloat16 [1024, 1024], P('dp'), may hold values from -3 to 3
- b_out: bfloat16 [1024], P('dp'), may hold values from -4 to 4
- w_up: bfloat16 [1024, 4096], P('dp'), may hold values from -0.1875 to 0.1875
- b_up: bfloat16 [4096], P('dp'), may hold values from -4 to 4
- w_down: bfloat16 [4096, 1024], P('dp'), may hold values from -0.09375 to 0.09375
- b_down: bfloat16 [1024], P('dp'), may hold values from -4 to 4
- out_grad: bfloat16 [32, 1024, 1024], P('dp', 'ctx'), may hold values from -6 to 6
Outputs:
- mixed: bfloat16 [32, 1024, 1024], P('dp', 'ctx')
- grad_tokens: bfloat16 [32, 1024, 1024], P('dp', 'ctx')
- grad_ln_gain: float32 [1024], P('dp')
- grad_ln_bias: float32 [1024], P('dp')
- grad_w_qkv: float32 [1024, 3072], P('dp')
- grad_b_qkv: float32 [3072], P('dp')
- grad_w_out: float32 [1024, 1024], P('dp')
- grad_b_out: float32 [1024], P('dp')
- grad_w_up: float32 [1024, 4096], P('dp')
- grad_b_up: float32 [4096], P('dp')
- grad_w_down: float32 [4096, 1024], P('dp')
- grad_b_down: float32 [1024], P('dp')
The draws below stay inside these ranges and needn't reach their ends.
Inputs may be any that keep to these rules, and one draw needn't show every extreme that they name: `segments`: in every sequence the document numbers start at 0, never fall and rise by one where a document begins; one document of each sequence begins within its first 128 positions and ends within its last 128; documents other than that one lie within the first or the last 128 positions.
All inputs are finite; a program needn't handle non-finite values.
Results may differ from the reference program's by a relative error of at most 0.02.
Values may be sent and summed in bfloat16 or wider, within the bound.
No kernel may reach another device: no remote copies, remote signals or barrier semaphores. Data moves between devices by JAX's collectives and lax.ppermute only.
A program may use at most 192 MiB of HBM per device.

```python
import jax
import jax.numpy as jnp
from jax import lax

D = 1024
HEADS = 16
HEAD_DIM = 64
ROTARY = 32
FF = 4096
SEQ_LEN = 1024
TOK_DEV = 128
SEQS = 32


def draw_segments(key, part):
    key = jax.random.fold_in(key, 11)
    first_key, last_key, cut_key, pick_key = jax.random.split(key, 4)
    chosen = jax.random.randint(pick_key, (), 0, SEQS)
    rows = jnp.arange(SEQS, dtype=jnp.int32)[:, None]
    forced = rows == chosen
    opening = jax.random.randint(first_key, (SEQS, 1), 1, TOK_DEV)
    closing = jax.random.randint(last_key, (SEQS, 1), SEQ_LEN - TOK_DEV + 1, SEQ_LEN)
    opening = jnp.where(forced, TOK_DEV - 1, opening)
    closing = jnp.where(forced, SEQ_LEN - TOK_DEV + 1, closing)
    places = jnp.arange(1, SEQ_LEN, dtype=jnp.int32)[None, :]
    extra = (jax.random.randint(cut_key, (SEQS, SEQ_LEN - 1), 0, 8) == 0) | forced
    outside = (places < opening) | (places > closing)
    starts = (places == opening) | (places == closing) | outside & extra
    counted = jnp.cumsum(starts.astype(jnp.int32), axis=1)
    return jnp.concatenate([jnp.zeros((SEQS, 1), jnp.int32), counted], axis=1)


def block_scale(stream_key, dims, cuts, least, high):
    factor_of, own = 1.0, jax.random.fold_in(stream_key, 6)
    for position, shards_of in cuts:
        draws = jnp.exp(jax.random.uniform(jax.random.fold_in(own, position), (shards_of,), jnp.float32, least / len(cuts), high / len(cuts)))
        factor_of = factor_of * jnp.repeat(draws, dims[position] // shards_of).reshape([-1 if axis == position else 1 for axis in range(len(dims))])
    return factor_of


def scatter_about(key, extent, spread, most, cuts=(), held_as=jnp.bfloat16):
    drawn = jax.random.normal(key, extent, jnp.float32) * spread
    if len(cuts) > 0:
        drawn = block_scale(key, extent, cuts, -0.22, 0.18) * drawn
    return jnp.clip(drawn, min=-most, max=most).astype(held_as)


def setup_inputs(seed: int = 0) -> dict:
    keys = jax.random.split(jax.random.key(seed), 14)
    return {
        "tokens": scatter_about(keys[0], (SEQS, SEQ_LEN, D), 1.0, 6.0, ((0, 16), (1, 8))),
        "segments": draw_segments(jax.random.fold_in(keys[13], 71), 0),
        "ln_gain": jnp.clip(1.0 + 0.1 * jax.random.normal(keys[2], (D,), jnp.float32), 0.5, 1.5).astype(jnp.bfloat16),
        "ln_bias": scatter_about(keys[3], (D,), 0.2, 3.0, ((0, 16),)),
        "w_qkv": scatter_about(keys[4], (D, 3 * D), D ** -0.5, 0.1875, ((0, 16),)),
        "b_qkv": scatter_about(keys[5], (3 * D,), 0.3, 4.0, ((0, 16),)),
        "w_out": scatter_about(keys[6], (D, D), (max(2, D // 256)) ** -0.5, 3.0, ((0, 16),)),
        "b_out": scatter_about(keys[7], (D,), 0.3, 4.0, ((0, 16),)),
        "w_up": scatter_about(keys[8], (D, FF), D ** -0.5, 0.1875, ((0, 16),)),
        "b_up": scatter_about(keys[9], (FF,), 0.3, 4.0, ((0, 16),)),
        "w_down": scatter_about(keys[10], (FF, D), FF ** -0.5, 0.09375, ((0, 16),)),
        "b_down": scatter_about(keys[11], (D,), 0.3, 4.0, ((0, 16),)),
        "out_grad": scatter_about(keys[12], (SEQS, SEQ_LEN, D), 1.0, 6.0, ((0, 16), (1, 8))),
    }


norm_epsilon = 1e-05
masked_score = -1e+30

@jax.custom_vjp
def low(v):
    return lax.optimization_barrier(v.astype(jnp.bfloat16)).astype(jnp.float32)

@jax.custom_vjp
def low_back(v):
    return v

def low_keep(v):
    return (low(v), None)

def low_pass(kept, grad):
    return (grad,)

def back_keep(v):
    return (v, None)

def back_low(kept, grad):
    return (low(grad),)
low.defvjp(low_keep, low_pass)
low_back.defvjp(back_keep, back_low)

def product(left, right):
    return jnp.dot(left, right, preferred_element_type=jnp.float32, precision=lax.Precision.HIGHEST)

def rotate(field_rows, positions, forward):
    row_count = field_rows.shape[0]
    shaped = field_rows.reshape(row_count, HEADS, HEAD_DIM)
    half_width = ROTARY // 2
    frequency = 10000.0 ** (-2.0 * jnp.arange(half_width, dtype=jnp.float32) / ROTARY)
    angles = positions.astype(jnp.float32)[:, None] * frequency[None, :]
    cosine = jnp.cos(angles)[:, None, :]
    sine_part = jnp.sin(angles)[:, None, :]
    first_half = shaped[:, :, :half_width]
    second_half = shaped[:, :, half_width:ROTARY]
    remainder = shaped[:, :, ROTARY:]
    if forward:
        new_first = first_half * cosine - second_half * sine_part
        new_second = second_half * cosine + first_half * sine_part
    else:
        new_first = first_half * cosine + second_half * sine_part
        new_second = second_half * cosine - first_half * sine_part
    joined = jnp.concatenate([new_first, new_second, remainder], axis=2)
    return joined.reshape(row_count, HEADS * HEAD_DIM)

def layer_forward(inputs, segment_ids, ln_gain, ln_bias, w_qkv, b_qkv, w_out, b_out, w_up, b_up, w_down, b_down):
    seq_length = inputs.shape[0]
    width = inputs.shape[1]
    center = inputs - lax.optimization_barrier(jnp.mean(inputs, axis=1, keepdims=True))
    inverse = lax.rsqrt(lax.optimization_barrier(jnp.mean(center * center, axis=1, keepdims=True)) + norm_epsilon)
    hidden = low(center * inverse * ln_gain + ln_bias)
    projected = low_back(product(hidden, w_qkv) + b_qkv)
    positions = jnp.arange(seq_length, dtype=jnp.int32)
    queries = low(rotate(projected[:, :width], positions, True))
    key_rows = low(rotate(projected[:, width:2 * width], positions, True))
    value_rows = low(projected[:, 2 * width:])
    query_heads = queries.reshape(seq_length, HEADS, HEAD_DIM)
    key_heads = key_rows.reshape(seq_length, HEADS, HEAD_DIM)
    value_heads = value_rows.reshape(seq_length, HEADS, HEAD_DIM)
    scores = jnp.einsum('qhd,khd->hqk', query_heads, key_heads, precision=lax.Precision.HIGHEST)
    scores = low_back(scores * HEAD_DIM ** (-0.5))
    allowed = (positions[None, :] <= positions[:, None]) & (segment_ids[None, :] == segment_ids[:, None])
    scores = jnp.where(allowed[None, :, :], scores, masked_score)
    row_max = lax.optimization_barrier(jnp.max(scores, axis=2, keepdims=True))
    log_total = row_max + jnp.log(lax.optimization_barrier(jnp.sum(jnp.exp(scores - row_max), axis=2, keepdims=True)))
    probs = low(jnp.exp(scores - log_total))
    mixed_heads = jnp.einsum('hqk,khd->qhd', probs, value_heads, precision=lax.Precision.HIGHEST)
    attended = low(low_back(mixed_heads.reshape(seq_length, width)))
    up_proj = low_back(product(hidden, w_up) + b_up)
    activated = low(jax.nn.gelu(up_proj, approximate=False))
    return inputs + product(attended, w_out) + b_out + product(activated, w_down) + b_down

def reference(tokens, segments, ln_gain, ln_bias, w_qkv, b_qkv, w_out, b_out, w_up, b_up, w_down, b_down, out_grad):
    params = (ln_gain.astype(jnp.float32), ln_bias.astype(jnp.float32), w_qkv.astype(jnp.float32), b_qkv.astype(jnp.float32), w_out.astype(jnp.float32), b_out.astype(jnp.float32), w_up.astype(jnp.float32), b_up.astype(jnp.float32), w_down.astype(jnp.float32), b_down.astype(jnp.float32))

    def one_sequence(running, pieces):
        inputs, segment_ids, cotangent = pieces

        def closed(input_rows, gain, lbias, wqkv, bqkv, wout, bout, wup, bup, wdown, bdown):
            return layer_forward(input_rows, segment_ids, gain, lbias, wqkv, bqkv, wout, bout, wup, bup, wdown, bdown)
        result, pullback = jax.vjp(closed, inputs.astype(jnp.float32), *params)
        grads = pullback(cotangent.astype(jnp.float32))
        updated = tuple((total + addend for total, addend in zip(running, grads[1:])))
        return (updated, (result.astype(jnp.bfloat16), grads[0].astype(jnp.bfloat16)))
    start = tuple((jnp.zeros(param.shape, jnp.float32) for param in params))
    sums, outputs = lax.scan(one_sequence, start, (tokens, segments, out_grad))
    return (outputs[0], outputs[1], sums[0], sums[1], sums[2], sums[3], sums[4], sums[5], sums[6], sums[7], sums[8], sums[9])
```

```python
import functools

import jax
import jax.numpy as jnp
from jax import lax
from jax.experimental import pallas as pl
from jax.experimental.pallas import tpu as pltpu
from jax.sharding import Mesh
from jax.sharding import PartitionSpec as P

HEAD_DIM = 64
ROTARY = 32
HALF = ROTARY // 2
SEQ = 1024
D = 1024
PAIR = 128
FFD = 512
QKV = 3 * PAIR
IN_COLS = QKV + FFD
OUT_ROWS = PAIR + FFD
QB = 256

norm_epsilon = 1e-05
masked_score = -1e30
f32 = jnp.float32
bf16 = jnp.bfloat16
NT = (((1,), (1,)), ((), ()))
NN = (((1,), (0,)), ((), ()))
VMEM_LIMIT = 48 * 1024 * 1024


def dot(a, b, dims=NN):
    return lax.dot_general(a, b, dims, preferred_element_type=f32)


def call(kernel, name, grid, in_specs, out_specs, out_shape, scratch=(), prefetch=0, flops=0, nbytes=0):
    return pl.pallas_call(
        kernel,
        name=name,
        grid_spec=pltpu.PrefetchScalarGridSpec(
            num_scalar_prefetch=prefetch,
            grid=grid,
            in_specs=in_specs,
            out_specs=out_specs,
            scratch_shapes=scratch,
        ),
        out_shape=out_shape,
        compiler_params=pltpu.CompilerParams(
            dimension_semantics=("arbitrary",) * len(grid), vmem_limit_bytes=VMEM_LIMIT
        ),
        cost_estimate=pl.CostEstimate(flops=flops, bytes_accessed=nbytes, transcendentals=0),
    )


def shift(x, axis, count, by):
    return lax.ppermute(x, axis, [(i, (i + by) % count) for i in range(count)])


def add(a, b):
    return (a.astype(f32) + b.astype(f32)).astype(bf16)


def halves(a):
    n = a.shape[0] // 2
    return a[:n], a[n:]


def gather_ctx(own):
    other = shift(own, "yh", 2, 1)
    blocks = []
    for step, mine in ((0, own), (1, other)):
        left = shift(mine, "x", 4, 1)
        right = shift(mine, "x", 4, -1)
        far0 = shift(halves(left)[0], "x", 4, 1)
        far1 = shift(halves(right)[1], "x", 4, -1)
        blocks += [(step, 0, None, mine), (step, 3, None, left), (step, 1, None, right)]
        blocks += [(step, 2, 0, far0), (step, 2, 1, far1)]
    return blocks


def place(blocks, out, put):
    x = lax.axis_index("x")
    yh = lax.axis_index("yh")
    for step, dx, half, block in blocks:
        index = ((yh + step) % 2) * 4 + (x + dx) % 4
        out = put(out, block, half, index)
    return out


def gather_positions(own):
    def put(out, block, half, index):
        return lax.dynamic_update_slice(out, block[:, None], (half or 0, index, 0, 0))

    return place(gather_ctx(own), jnp.zeros((2, 8) + own.shape[1:], own.dtype), put)


def gather_shards(own):
    def put(out, block, half, index):
        return lax.dynamic_update_slice(out, block[None], (index, 32 * (half or 0), 0))

    return place(gather_ctx(own), jnp.zeros((8,) + own.shape, own.dtype), put)


def scatter_x(far, right, left):
    a = shift(far[0], "x", 4, 1)
    b = shift(far[1], "x", 4, -1)
    to_right = jnp.stack([add(right[0], a), right[1]])
    to_left = jnp.stack([left[0], add(left[1], b)])
    return shift(to_right, "x", 4, 1), shift(to_left, "x", 4, -1)


def scatter_positions(parts):
    c, d = scatter_x(parts[0], parts[1], parts[2])
    other = (parts[3].astype(f32) + c.astype(f32) + d.astype(f32)).astype(bf16)
    e = shift(other, "yh", 2, 1)
    c, d = scatter_x(parts[4], parts[5], parts[6])
    return parts[7].astype(f32) + c.astype(f32) + d.astype(f32) + e.astype(f32)


def dest_order():
    x = lax.axis_index("x")
    yh = lax.axis_index("yh")
    order = [((yh + step) % 2) * 4 + (x + dx) % 4 for step in (1, 0) for dx in (2, 1, 3, 0)]
    return jnp.stack(order).astype(jnp.int32)


def scatter_owners(parts):
    z = lax.axis_index("z")
    yl = lax.axis_index("yl")
    c = lax.axis_index("c")
    p = parts.reshape((4, 2, 2) + parts.shape[1:])
    mine = lax.dynamic_index_in_dim(p, c, 2, keepdims=False)
    other = lax.dynamic_index_in_dim(p, 1 - c, 2, keepdims=False)
    p = add(mine, shift(other, "c", 2, 1))

    def block(k):
        return lax.dynamic_index_in_dim(p, (z + k) % 4, 0, keepdims=False)

    far, right, left = block(2), block(1), block(3)
    a = shift(far[0], "z", 4, 1)
    b = shift(far[1], "z", 4, -1)
    to_right = jnp.stack([add(right[0], a), right[1]])
    to_left = jnp.stack([left[0], add(left[1], b)])
    from_left = shift(to_right, "z", 4, 1)
    from_right = shift(to_left, "z", 4, -1)
    r = (block(0).astype(f32) + from_left.astype(f32) + from_right.astype(f32)).astype(bf16)
    mine = lax.dynamic_index_in_dim(r, yl, 0, keepdims=False)
    other = lax.dynamic_index_in_dim(r, 1 - yl, 0, keepdims=False)
    return mine.astype(f32) + shift(other, "yl", 2, 1).astype(f32)


ALL = ("z", "yl", "c", "yh", "x")


def out_pairs(back):
    pairs = []
    for j in range(8):
        for b in range(2):
            for k in range(8):
                pairs.append(((2 * j + b) * 8 + k, (8 * b + k) * 8 + j))
    return [(t, s) for s, t in pairs] if back else pairs


def turn(v, cosine, sine_a, sine_b):
    return v * cosine + pltpu.roll(v, PAIR - HALF, 1) * sine_a + pltpu.roll(v, HALF, 1) * sine_b


def assemble_kernel(g0, g1, g2, g3, g4, out_ref):
    for i in range(16):
        b, k = i // 8, i % 8
        rows = pl.ds(64 * i, 64)
        cols = pl.ds(128 * k, 128)
        out_ref[pl.ds(64 * b, 64), cols] = g0[rows, :]
        for m, g in enumerate((g1, g2, g3, g4)):
            out_ref[pl.ds(PAIR + 256 * b + 64 * m, 64), cols] = g[rows, :]


def project_kernel(x_ref, gain_ref, lbias_ref, w_ref, b_ref, cos_ref, sa_ref, sb_ref, hid_ref, qkv_ref, act_ref, dgelu_ref):
    x = x_ref[...].astype(f32)
    center = x - jnp.mean(x, axis=1, keepdims=True)
    inverse = lax.rsqrt(jnp.mean(center * center, axis=1, keepdims=True) + norm_epsilon)
    hidden = (center * inverse * gain_ref[...] + lbias_ref[...]).astype(bf16)
    hid_ref[...] = hidden
    proj = dot(hidden, w_ref[...]) + b_ref[...]
    cosine, sa, sb = cos_ref[...], sa_ref[...], sb_ref[...]
    qkv_ref[:, 0:PAIR] = turn(proj[:, 0:PAIR], cosine, sa, sb).astype(bf16)
    qkv_ref[:, PAIR : 2 * PAIR] = turn(proj[:, PAIR : 2 * PAIR], cosine, sa, sb).astype(bf16)
    qkv_ref[:, 2 * PAIR : QKV] = proj[:, 2 * PAIR : QKV].astype(bf16)
    up = proj[:, QKV:]
    cdf = 0.5 * (1.0 + lax.erf(up * 0.7071067811865476))
    density = jnp.exp(-0.5 * up * up) * 0.3989422804014327
    act_ref[...] = (up * cdf).astype(bf16)
    dgelu_ref[...] = (cdf + up * density).astype(bf16)


def head_lanes(h):
    lane = lax.broadcasted_iota(jnp.int32, (1, PAIR), 1)
    return (lane < HEAD_DIM) if h == 0 else (lane >= HEAD_DIM)


def allowed_mask(seg_row_ref, seg_col_ref, b, keys):
    key_pos = lax.broadcasted_iota(jnp.int32, (keys, QB), 0)
    query_pos = lax.broadcasted_iota(jnp.int32, (keys, QB), 1) + b * QB
    same = seg_col_ref[0, 0:keys, :] == seg_row_ref[0, :, b * QB : (b + 1) * QB]
    return (key_pos <= query_pos) & same


def attend_kernel(qkv_ref, seg_row_ref, seg_col_ref, att_ref, lse_ref):
    value_t = qkv_ref[:, 2 * PAIR : QKV].astype(f32).T.astype(bf16)
    for b in range(SEQ // QB):
        keys = (b + 1) * QB
        rows = slice(b * QB, (b + 1) * QB)
        allowed = allowed_mask(seg_row_ref, seg_col_ref, b, keys)
        query = qkv_ref[rows, 0:PAIR]
        mixed = []
        for h in range(2):
            q = jnp.where(head_lanes(h), query * 0.125, jnp.zeros_like(query))
            s = jnp.where(allowed, dot(qkv_ref[0:keys, PAIR : 2 * PAIR], q, NT), masked_score)
            top = jnp.max(s, axis=0, keepdims=True)
            e = jnp.exp(s - top)
            total = jnp.sum(e, axis=0, keepdims=True)
            p = (e * (1.0 / total)).astype(bf16)
            lse_ref[0, h : h + 1, rows] = top + jnp.log(total)
            mixed.append(dot(value_t[h * HEAD_DIM : (h + 1) * HEAD_DIM, 0:keys], p))
        att_ref[rows, :] = jnp.concatenate(mixed, axis=0).T.astype(bf16)


def attend_back_kernel(
    qkv_ref, da_ref, lse_ref, seg_row_ref, seg_col_ref, cos_ref, sa_ref, sb_ref, out_ref, sum_ref, dk_ref, dv_ref
):
    key_t = qkv_ref[:, PAIR : 2 * PAIR].astype(f32).T.astype(bf16)
    dk_ref[...] = jnp.zeros_like(dk_ref)
    dv_ref[...] = jnp.zeros_like(dv_ref)
    sums = jnp.zeros((1, PAIR), f32)
    for b in range(SEQ // QB):
        keys = (b + 1) * QB
        rows = slice(b * QB, (b + 1) * QB)
        allowed = allowed_mask(seg_row_ref, seg_col_ref, b, keys)
        query = qkv_ref[rows, 0:PAIR]
        grad = da_ref[rows, :]
        dq = []
        for h in range(2):
            q = jnp.where(head_lanes(h), query * 0.125, jnp.zeros_like(query))
            g = jnp.where(head_lanes(h), grad, jnp.zeros_like(grad))
            s = jnp.where(allowed, dot(qkv_ref[0:keys, PAIR : 2 * PAIR], q, NT), masked_score)
            soft = jnp.exp(s - lse_ref[0, h : h + 1, rows])
            dp = dot(qkv_ref[0:keys, 2 * PAIR : QKV], g, NT)
            t = soft * dp
            inner = jnp.sum(t, axis=0, keepdims=True)
            ds = (t - soft * inner).astype(bf16)
            dv_ref[0:keys, :] += dot(soft.astype(bf16), g)
            dk_ref[0:keys, :] += dot(ds, q)
            dq.append(dot(key_t[h * HEAD_DIM : (h + 1) * HEAD_DIM, 0:keys], ds))
        dq = jnp.concatenate(dq, axis=0).T * 0.125
        dq = turn(dq, cos_ref[rows, :], -sa_ref[rows, :], -sb_ref[rows, :]).astype(bf16)
        out_ref[rows, 0:PAIR] = dq
        sums += jnp.sum(dq.astype(f32), axis=0, keepdims=True)
    dk = turn(dk_ref[...], cos_ref[...], -sa_ref[...], -sb_ref[...]).astype(bf16)
    dv = dv_ref[...].astype(bf16)
    out_ref[:, PAIR : 2 * PAIR] = dk
    out_ref[:, 2 * PAIR : QKV] = dv
    sum_ref[0, :, 0:PAIR] = sums
    sum_ref[0, :, PAIR : 2 * PAIR] = jnp.sum(dk.astype(f32), axis=0, keepdims=True)
    sum_ref[0, :, 2 * PAIR : QKV] = jnp.sum(dv.astype(f32), axis=0, keepdims=True)


def mix_kernel(order_ref, att_ref, act_ref, w_ref, out_ref):
    for s in range(2):
        part = dot(att_ref[s, 0], w_ref[0:PAIR, :]) + dot(act_ref[s, 0], w_ref[PAIR:, :])
        out_ref[0, s] = part.astype(bf16)


def back_out_kernel(g_ref, w_ref, dgelu_ref, da_ref, dup_ref, sum_ref):
    @pl.when(pl.program_id(0) == 0)
    def _():
        sum_ref[...] = jnp.zeros_like(sum_ref)

    r = dot(g_ref[...], w_ref[...], NT)
    da_ref[...] = r[:, 0:PAIR].astype(bf16)
    dup = (r[:, PAIR:] * dgelu_ref[...].astype(f32)).astype(bf16)
    dup_ref[...] = dup
    sum_ref[...] += jnp.sum(dup.astype(f32), axis=0, keepdims=True)


def back_in_kernel(order_ref, dqkv_ref, dup_ref, w_ref, x_ref, out_ref, sum_ref):
    @pl.when(pl.program_id(0) == 0)
    def _():
        sum_ref[...] = jnp.zeros_like(sum_ref)

    for s in range(2):
        grad = dot(dqkv_ref[s, 0], w_ref[:, 0:QKV], NT) + dot(dup_ref[s, 0], w_ref[:, QKV:], NT)
        out_ref[0, s] = grad.astype(bf16)
        x = x_ref[s, 0].astype(f32)
        center = x - jnp.mean(x, axis=1, keepdims=True)
        inverse = lax.rsqrt(jnp.mean(center * center, axis=1, keepdims=True) + norm_epsilon)
        sum_ref[0:1, :] += jnp.sum(grad * (center * inverse), axis=0, keepdims=True)
        sum_ref[1:2, :] += jnp.sum(grad, axis=0, keepdims=True)


def shape(dims, dtype):
    return jax.ShapeDtypeStruct(dims, dtype)


def rotary_tables():
    frequency = 10000.0 ** (-2.0 * jnp.arange(HALF, dtype=f32) / ROTARY)
    angles = jnp.arange(SEQ, dtype=f32)[:, None] * frequency[None, :]
    cosine, sine = jnp.cos(angles), jnp.sin(angles)
    one = jnp.ones((SEQ, HEAD_DIM - ROTARY), f32)
    zero = jnp.zeros((SEQ, HEAD_DIM - ROTARY), f32)
    none = jnp.zeros((SEQ, HALF), f32)
    cos = jnp.concatenate([cosine, cosine, one] * 2, axis=1)
    sine_a = jnp.concatenate([-sine, none, zero] * 2, axis=1)
    sine_b = jnp.concatenate([none, sine, zero] * 2, axis=1)
    return cos, sine_a, sine_b


def cols(a, start, size):
    return lax.dynamic_slice_in_dim(a, start, size, axis=1)


def body(tokens, segments, ln_gain, ln_bias, w_qkv, b_qkv, w_out, b_out, w_up, b_up, w_down, b_down, out_grad):
    j = lax.axis_index("yh") * 4 + lax.axis_index("x")
    order = dest_order()

    piece = jnp.concatenate(
        [cols(w_out, 128 * j, 128)] + [cols(w_down, 128 * j, 128)[64 * m : 64 * m + 64] for m in range(4)], axis=1
    )
    piece = lax.ppermute(piece, ALL, out_pairs(False))
    small = jnp.concatenate([ln_gain, ln_bias, b_qkv, b_out, b_up, b_down, jnp.zeros((64,), bf16)])
    small = jnp.pad(small.reshape(6, 128), ((0, 58), (0, 0)))
    shard = jnp.concatenate(
        [cols(w_qkv, D * t + 128 * j, 128) for t in range(3)] + [cols(w_up, FFD * j, FFD), piece, small], axis=1
    )
    gathered = lax.all_gather(shard, ("z", "yl", "c"), axis=0, tiled=True)

    x_all = gather_positions(tokens)
    g_all = gather_positions(out_grad)

    vec = gathered[:, IN_COLS + OUT_ROWS :].reshape(16, 64, 128)[:, :6].reshape(16, 768).astype(f32)
    gain = vec[:, 0:64].reshape(1, D)
    lbias = vec[:, 64:128].reshape(1, D)
    bqkv = vec[:, 128:320].reshape(1, 3 * D)
    bout = vec[:, 320:384].reshape(D)
    bup = vec[:, 384:640].reshape(1, 8 * FFD)
    bdown = vec[:, 640:704].reshape(D)
    b_in = jnp.concatenate([cols(bqkv, D * t + 128 * j, 128) for t in range(3)] + [cols(bup, FFD * j, FFD)], axis=1)
    cos, sine_a, sine_b = rotary_tables()
    seg_row = segments[:, None, :]
    seg_col = segments[:, :, None]

    whole = lambda dims: pl.BlockSpec(dims, lambda i, *_: (0,) * len(dims))
    rows = lambda n, size=256: pl.BlockSpec((size, n), lambda i, *_: (i, 0))
    table = pl.BlockSpec((256, PAIR), lambda i, *_: (i % 4, 0))
    tokens_n = 2 * SEQ

    w_mix = call(
        assemble_kernel,
        "assemble",
        (1,),
        [pl.BlockSpec((D, 128), functools.partial(lambda m, i: (0, m), 7 + m)) for m in range(5)],
        whole((OUT_ROWS, D)),
        shape((OUT_ROWS, D), bf16),
        nbytes=2 * 2 * OUT_ROWS * D,
    )(*[gathered] * 5)

    hidden, qkv, activated, dgelu = call(
        project_kernel,
        "project",
        (8,),
        [rows(D), whole((1, D)), whole((1, D)), whole((D, IN_COLS)), whole((1, IN_COLS)), table, table, table],
        [rows(D), rows(QKV), rows(FFD), rows(FFD)],
        [shape((tokens_n, n), bf16) for n in (D, QKV, FFD, FFD)],
        flops=2 * tokens_n * D * IN_COLS,
        nbytes=16 * 1024 * 1024,
    )(x_all.reshape(tokens_n, D), gain, lbias, gathered, b_in, cos, sine_a, sine_b)

    seg_row_spec = pl.BlockSpec((1, 1, SEQ), lambda i: (i, 0, 0))
    seg_col_spec = pl.BlockSpec((1, SEQ, 1), lambda i: (i, 0, 0))
    lse_spec = pl.BlockSpec((1, 2, SEQ), lambda i: (i, 0, 0))
    attended, lse = call(
        attend_kernel,
        "attend",
        (2,),
        [rows(QKV, SEQ), seg_row_spec, seg_col_spec],
        [rows(PAIR, SEQ), lse_spec],
        [shape((tokens_n, PAIR), bf16), shape((2, 2, SEQ), f32)],
        flops=4 * 4 * SEQ * SEQ * 128,
        nbytes=4 * 1024 * 1024,
    )(qkv, seg_row, seg_col)

    placed = lambda n: pl.BlockSpec((2, 1, 128, n), lambda i, order: (0, order[i], 0, 0))
    part_spec = pl.BlockSpec((1, 2, 128, D), lambda i, order: (i, 0, 0, 0))
    parts = call(
        mix_kernel,
        "mix",
        (8,),
        [placed(PAIR), placed(FFD), whole((OUT_ROWS, D))],
        part_spec,
        shape((8, 2, 128, D), bf16),
        prefetch=1,
        flops=2 * tokens_n * D * OUT_ROWS,
        nbytes=8 * 1024 * 1024,
    )(order, attended.reshape(2, 8, 128, PAIR), activated.reshape(2, 8, 128, FFD), w_mix)
    mixed = tokens.astype(f32) + scatter_positions(parts) + (bout + bdown)
    mixed = mixed.astype(bf16)

    g_rows = g_all.reshape(tokens_n, D)
    grad_attended, grad_up, up_sums = call(
        back_out_kernel,
        "back_out",
        (8,),
        [rows(D), whole((OUT_ROWS, D)), rows(FFD)],
        [rows(PAIR), rows(FFD), whole((1, FFD))],
        [shape((tokens_n, PAIR), bf16), shape((tokens_n, FFD), bf16), shape((1, FFD), f32)],
        flops=2 * tokens_n * D * OUT_ROWS,
        nbytes=10 * 1024 * 1024,
    )(g_rows, w_mix, dgelu)

    TN = (((0,), (0,)), ((), ()))
    grad_out = dot(attended, g_rows, TN).astype(bf16)
    grad_down = dot(activated, g_rows, TN).astype(bf16)
    out_parts = jnp.concatenate(
        [
            grad_out.reshape(2, 64, 8, 128).transpose(0, 2, 1, 3).reshape(16, 64, 128),
            grad_down.reshape(2, 4, 64, 8, 128).transpose(0, 3, 2, 1, 4).reshape(16, 64, FFD),
        ],
        axis=2,
    )
    out_owned = lax.ppermute(scatter_owners(out_parts).astype(bf16), ALL, out_pairs(True))
    out_full = gather_shards(out_owned)

    up_parts = dot(hidden, grad_up, TN).astype(bf16).reshape(16, 64, FFD)
    up_full = gather_shards(scatter_owners(up_parts).astype(bf16))

    grad_qkv, qkv_sums = call(
        attend_back_kernel,
        "attend_back",
        (2,),
        [
            rows(QKV, SEQ),
            rows(PAIR, SEQ),
            lse_spec,
            seg_row_spec,
            seg_col_spec,
            whole((SEQ, PAIR)),
            whole((SEQ, PAIR)),
            whole((SEQ, PAIR)),
        ],
        [rows(QKV, SEQ), pl.BlockSpec((1, 1, QKV), lambda i: (i, 0, 0))],
        [shape((tokens_n, QKV), bf16), shape((2, 1, QKV), f32)],
        scratch=[pltpu.VMEM((SEQ, PAIR), f32), pltpu.VMEM((SEQ, PAIR), f32)],
        flops=10 * 4 * SEQ * SEQ * 128,
        nbytes=8 * 1024 * 1024,
    )(qkv, grad_attended, lse, seg_row, seg_col, cos, sine_a, sine_b)

    parts, ln_sums = call(
        back_in_kernel,
        "back_in",
        (8,),
        [placed(QKV), placed(FFD), whole((D, IN_COLS)), placed(D)],
        [part_spec, whole((2, D))],
        [shape((8, 2, 128, D), bf16), shape((2, D), f32)],
        prefetch=1,
        flops=2 * tokens_n * D * IN_COLS,
        nbytes=14 * 1024 * 1024,
    )(order, grad_qkv.reshape(2, 8, 128, QKV), grad_up.reshape(2, 8, 128, FFD), gathered, x_all)

    sums = jnp.sum(qkv_sums, axis=0)
    grad_bqkv = jnp.zeros((1, 3 * D), f32)
    for t in range(3):
        grad_bqkv = lax.dynamic_update_slice(grad_bqkv, sums[:, 128 * t : 128 * t + 128], (0, D * t + 128 * j))
    grad_bup = lax.dynamic_update_slice(jnp.zeros((1, 8 * FFD), f32), up_sums, (0, FFD * j))
    g_sum = jnp.sum(out_grad.astype(f32), axis=(0, 1))
    vec = jnp.concatenate(
        [
            ln_sums[0].reshape(16, 64),
            ln_sums[1].reshape(16, 64),
            grad_bqkv.reshape(16, 192),
            g_sum.reshape(16, 64),
            grad_bup.reshape(16, 256),
            jnp.zeros((16, 128), f32),
        ],
        axis=1,
    ).astype(bf16)
    vec = jnp.pad(vec.reshape(16, 6, 128), ((0, 0), (0, 58), (0, 0)))
    qkv_parts = jnp.concatenate([dot(hidden, grad_qkv, TN).astype(bf16).reshape(16, 64, QKV), vec], axis=2)
    qkv_full = gather_shards(scatter_owners(qkv_parts).astype(bf16))

    grad_hidden = scatter_positions(parts)
    x = tokens.astype(f32)
    center = x - jnp.mean(x, axis=2, keepdims=True)
    inverse = lax.rsqrt(jnp.mean(center * center, axis=2, keepdims=True) + norm_epsilon)
    normed = center * inverse
    n = grad_hidden * gain
    grad_tokens = out_grad.astype(f32) + inverse * (
        n - jnp.mean(n, axis=2, keepdims=True) - normed * jnp.mean(n * normed, axis=2, keepdims=True)
    )
    grad_tokens = grad_tokens.astype(bf16)

    def side_by_side(a):
        return a.transpose(1, 0, 2).reshape(a.shape[1], -1).astype(f32)

    grad_w_qkv = jnp.concatenate([side_by_side(qkv_full[:, :, 128 * t : 128 * t + 128]) for t in range(3)], axis=1)
    grad_w_up = side_by_side(up_full)
    grad_w_out = side_by_side(out_full[:, :, 0:128])
    grad_w_down = out_full[:, :, 128:].reshape(8, 64, 4, 128).transpose(2, 1, 0, 3).reshape(256, D).astype(f32)
    vec = jnp.sum(qkv_full[:, 0:6, QKV:].astype(f32), axis=0).reshape(768)
    return (
        mixed,
        grad_tokens,
        vec[0:64],
        vec[64:128],
        grad_w_qkv,
        vec[128:320],
        grad_w_out,
        vec[320:384],
        grad_w_up,
        vec[384:640],
        grad_w_down,
        vec[320:384],
    )


def solution(mesh):
    fine = Mesh(mesh.devices.reshape(4, 2, 2, 2, 4), ALL)
    dp = ("z", "yl", "c")
    ctx = ("yh", "x")
    in_specs = (
        P(dp, ctx, None),
        P(dp, None),
        P(dp),
        P(dp),
        P(dp, None),
        P(dp),
        P(dp, None),
        P(dp),
        P(dp, None),
        P(dp),
        P(dp, None),
        P(dp),
        P(dp, ctx, None),
    )
    out_specs = (
        P(dp, ctx, None),
        P(dp, ctx, None),
        P(dp),
        P(dp),
        P(dp, None),
        P(dp),
        P(dp, None),
        P(dp),
        P(dp, None),
        P(dp),
        P(dp, None),
        P(dp),
    )
    return jax.shard_map(body, mesh=fine, in_specs=in_specs, out_specs=out_specs, check_vma=False)
```

```python
import functools

import jax
import jax.numpy as jnp
from jax import lax
from jax.experimental import pallas as pl
from jax.experimental.pallas import tpu as pltpu
from jax.sharding import Mesh
from jax.sharding import PartitionSpec as P

HEAD_DIM = 64
ROTARY = 32
HALF = ROTARY // 2
SEQ = 1024
D = 1024
PAIR = 128
FFD = 512
QKV = 3 * PAIR
IN_COLS = QKV + FFD
OUT_ROWS = PAIR + FFD
QB = 256

norm_epsilon = 1e-05
masked_score = -1e30
f32 = jnp.float32
bf16 = jnp.bfloat16
NT = (((1,), (1,)), ((), ()))
NN = (((1,), (0,)), ((), ()))
VMEM_LIMIT = 52 * 1024 * 1024
TN = (((0,), (0,)), ((), ()))
SHARD = IN_COLS + OUT_ROWS + 128
SCALE = 0.3
COST = dict(shard=2, piece=1, project=13, attend=11, assemble=3, mix=6, back_out=9, attend_back=13, back_in=14, fold=2, token_grad=3, chunk=4, pair_sum=3, owner_sum=2, finish=3)


def dot(a, b, dims=NN):
    return lax.dot_general(a, b, dims, preferred_element_type=f32)


def call(kernel, name, grid, in_specs, out_specs, out_shape, scratch=(), prefetch=0, alias=None):
    return pl.pallas_call(
        kernel,
        name=name,
        grid_spec=pltpu.PrefetchScalarGridSpec(
            num_scalar_prefetch=prefetch,
            grid=grid,
            in_specs=in_specs,
            out_specs=out_specs,
            scratch_shapes=scratch,
        ),
        out_shape=out_shape,
        input_output_aliases=alias or {},
        compiler_params=pltpu.CompilerParams(
            dimension_semantics=("arbitrary",) * len(grid), vmem_limit_bytes=VMEM_LIMIT
        ),
        cost_estimate=pl.CostEstimate(flops=int(COST.get(name, 1) * 1e9 * SCALE), bytes_accessed=int(COST.get(name, 1) * 1000000 * SCALE), transcendentals=0),
    )


ALL = ("z", "yl", "c", "yh", "x")


def shift(x, axis, by):
    count = lax.axis_size(axis)
    return lax.ppermute(x, axis, [(i, (i + by) % count) for i in range(count)])


def after(x, *others):
    return lax.optimization_barrier((x,) + others)[0]


def add(a, b):
    return (a.astype(f32) + b.astype(f32)).astype(bf16)


def block_of():
    at = jnp.arange(8, dtype=jnp.int32)
    same = (at // 4) == lax.axis_index("yh")
    step = (at % 4 - lax.axis_index("x")) % 4
    kind = jnp.where(step == 0, 3, jnp.where(step == 1, 1, jnp.where(step == 2, 0, 2)))
    return (jnp.where(same, 4, 0) + kind).astype(jnp.int32)


def out_pairs(back):
    pairs = []
    for j in range(8):
        for b in range(2):
            for k in range(8):
                pairs.append(((2 * j + b) * 8 + k, (8 * b + k) * 8 + j))
    return [(t, s) for s, t in pairs] if back else pairs


def turn(v, cosine, sine_a, sine_b):
    return v * cosine + pltpu.roll(v, PAIR - HALF, 1) * sine_a + pltpu.roll(v, HALF, 1) * sine_b


def norm(x):
    center = x - jnp.mean(x, axis=1, keepdims=True)
    inverse = lax.rsqrt(jnp.mean(center * center, axis=1, keepdims=True) + norm_epsilon)
    return center * inverse, inverse


def piece_kernel(place_ref, out_ref, down_ref, piece_ref):
    piece_ref[:, 0:128] = out_ref[...]
    for m in range(4):
        piece_ref[:, 128 + 128 * m : 256 + 128 * m] = down_ref[64 * m : 64 * m + 64, :]


def spread(row, size, offset):
    n = row.shape[1]
    v = lax.broadcasted_iota(jnp.int32, (n, size), 0)
    t = lax.broadcasted_iota(jnp.int32, (n, size), 1)
    return dot(row, jnp.where(offset(t) == v, 1.0, 0.0).astype(bf16))


def shard_kernel(place_ref, q_ref, k_ref, v_ref, up_ref, gain_ref, lbias_ref, bqkv_ref, bout_ref, bup_ref, bdown_ref, shard_ref):
    j, i = place_ref[0], place_ref[1]
    shard_ref[:, 0:128] = q_ref[...]
    shard_ref[:, 128:256] = k_ref[...]
    shard_ref[:, 256:384] = v_ref[...]
    shard_ref[:, QKV:IN_COLS] = up_ref[...]
    rows = []
    for ref in (gain_ref, lbias_ref, bout_ref, bdown_ref):
        rows.append(spread(ref[...], D, lambda t: t - 64 * i))
    rows.append(spread(bqkv_ref[...], QKV, lambda t: (t // 128) * D + 128 * j + t % 128 - 192 * i))
    rows.append(spread(bup_ref[...], FFD, lambda t: t + FFD * j - 256 * i))
    row = jnp.concatenate(rows, axis=1)
    count = row.shape[1] // 128
    table = jnp.concatenate([row[:, 128 * r : 128 * r + 128] for r in range(count)] + [jnp.zeros((64 - count, 128), f32)], axis=0)
    shard_ref[:, IN_COLS:] = table.astype(bf16)


def assemble_kernel(g0, g1, g2, g3, g4, out_ref, turned_ref):
    for i in range(16):
        b, k = i // 8, i % 8
        rows = pl.ds(64 * i, 64)
        at = pl.ds(128 * k, 128)
        for m, g_ref in enumerate((g0, g1, g2, g3, g4)):
            row = 64 * b if m == 0 else PAIR + 256 * b + 64 * (m - 1)
            out_ref[pl.ds(row, 64), at] = g_ref[rows, :]
    turned_ref[...] = out_ref[...].T


def token_blocks(refs):
    own, other, left, right, left3, right3, far0, far1 = refs
    return [
        ((far0, 0), (far1, 0)),
        ((right3, 0), (right3, 1)),
        ((left3, 0), (left3, 1)),
        ((other, 0), (other, 1)),
        ((left3, 2), (right3, 2)),
        ((right, 0), (right, 1)),
        ((left, 0), (left, 1)),
        ((own, 0), (own, 1)),
    ]


def grad_blocks(refs):
    own, other, left, right, far_own, far_other = refs
    return [
        ((far_other, 0), (far_other, 1)),
        ((right, 2), (right, 3)),
        ((left, 2), (left, 3)),
        ((other, 0), (other, 1)),
        ((far_own, 0), (far_own, 1)),
        ((right, 0), (right, 1)),
        ((left, 0), (left, 1)),
        ((own, 0), (own, 1)),
    ]


def load_pair(back_ref, blocks, hold_ref):
    for half in range(2):
        want = back_ref[2 * pl.program_id(0) + half]
        for block, pair in enumerate(blocks):

            @pl.when(want == block)
            def _(pair=pair):
                for s, (ref, row) in enumerate(pair):
                    hold_ref[256 * s + 128 * half : 256 * s + 128 * half + 128, :] = ref[row]


def project_kernel(back_ref, *refs):
    token_refs, refs = refs[:8], refs[8:]
    w_ref, vec_ref, cos_ref, sa_ref, sb_ref = refs[:5]
    hid_ref, qkv_ref, act_ref, dgelu_ref, small_ref, hold_ref = refs[5:]

    @pl.when(pl.program_id(0) == 0)
    def _():
        total = vec_ref[0:64, :].astype(f32)
        for i in range(1, 16):
            total = total + vec_ref[64 * i : 64 * i + 64, :].astype(f32)
        small_ref[...] = jnp.concatenate([total[r : r + 1, :] for r in range(39)], axis=1)

    load_pair(back_ref, token_blocks(token_refs), hold_ref)
    gain, lbias = small_ref[:, 0:D], small_ref[:, D : 2 * D]
    bias = small_ref[:, 4 * D :]
    cosine, sa, sb = cos_ref[...], sa_ref[...], sb_ref[...]
    for s in range(2):
        normed, _ = norm(hold_ref[256 * s : 256 * s + 256, :].astype(f32))
        hidden = (normed * gain + lbias).astype(bf16)
        proj = dot(hidden, w_ref[...]) + bias
        hid_ref[s] = hidden
        qkv_ref[s, :, 0:PAIR] = turn(proj[:, 0:PAIR], cosine, sa, sb).astype(bf16)
        qkv_ref[s, :, PAIR : 2 * PAIR] = turn(proj[:, PAIR : 2 * PAIR], cosine, sa, sb).astype(bf16)
        qkv_ref[s, :, 2 * PAIR : QKV] = proj[:, 2 * PAIR : QKV].astype(bf16)
        up = proj[:, QKV:]
        cdf = 0.5 * (1.0 + lax.erf(up * 0.7071067811865476))
        density = jnp.exp(-0.5 * up * up) * 0.3989422804014327
        act_ref[s] = (up * cdf).astype(bf16)
        dgelu_ref[s] = (cdf + up * density).astype(bf16)


def head_lanes(h):
    lane = lax.broadcasted_iota(jnp.int32, (1, PAIR), 1)
    return (lane < HEAD_DIM) if h == 0 else (lane >= HEAD_DIM)


def allowed_mask(seg_row_ref, seg_col_ref, b, keys):
    key_pos = lax.broadcasted_iota(jnp.int32, (keys, QB), 0)
    query_pos = lax.broadcasted_iota(jnp.int32, (keys, QB), 1) + b * QB
    same = seg_col_ref[0, 0:keys, :] == seg_row_ref[0, :, b * QB : (b + 1) * QB]
    return (key_pos <= query_pos) & same


def attend_kernel(qkv_ref, seg_row_ref, seg_col_ref, att_ref, lse_ref):
    value_t = qkv_ref[:, 2 * PAIR : QKV].astype(f32).T.astype(bf16)
    for b in range(SEQ // QB):
        keys = (b + 1) * QB
        rows = slice(b * QB, (b + 1) * QB)
        allowed = allowed_mask(seg_row_ref, seg_col_ref, b, keys)
        query = qkv_ref[rows, 0:PAIR]
        mixed = []
        for h in range(2):
            q = jnp.where(head_lanes(h), query * 0.125, jnp.zeros_like(query))
            s = jnp.where(allowed, dot(qkv_ref[0:keys, PAIR : 2 * PAIR], q, NT), masked_score)
            top = jnp.max(s, axis=0, keepdims=True)
            e = jnp.exp(s - top)
            total = jnp.sum(e, axis=0, keepdims=True)
            p = (e * (1.0 / total)).astype(bf16)
            lse_ref[0, h : h + 1, rows] = top + jnp.log(total)
            mixed.append(dot(value_t[h * HEAD_DIM : (h + 1) * HEAD_DIM, 0:keys], p))
        att_ref[rows, :] = jnp.concatenate(mixed, axis=0).T.astype(bf16)


def attend_back_kernel(
    qkv_ref, da_ref, lse_ref, seg_row_ref, seg_col_ref, cos_ref, sa_ref, sb_ref, out_ref, sum_ref, dk_ref, dv_ref
):
    key_t = qkv_ref[:, PAIR : 2 * PAIR].astype(f32).T.astype(bf16)
    dk_ref[...] = jnp.zeros_like(dk_ref)
    dv_ref[...] = jnp.zeros_like(dv_ref)
    sums = jnp.zeros((1, PAIR), f32)
    for b in range(SEQ // QB):
        keys = (b + 1) * QB
        rows = slice(b * QB, (b + 1) * QB)
        allowed = allowed_mask(seg_row_ref, seg_col_ref, b, keys)
        query = qkv_ref[rows, 0:PAIR]
        grad = da_ref[rows, :]
        dq = []
        for h in range(2):
            q = jnp.where(head_lanes(h), query * 0.125, jnp.zeros_like(query))
            g = jnp.where(head_lanes(h), grad, jnp.zeros_like(grad))
            s = jnp.where(allowed, dot(qkv_ref[0:keys, PAIR : 2 * PAIR], q, NT), masked_score)
            soft = jnp.exp(s - lse_ref[0, h : h + 1, rows])
            dp = dot(qkv_ref[0:keys, 2 * PAIR : QKV], g, NT)
            t = soft * dp
            inner = jnp.sum(t, axis=0, keepdims=True)
            ds = (t - soft * inner).astype(bf16)
            dv_ref[0:keys, :] += dot(soft.astype(bf16), g)
            dk_ref[0:keys, :] += dot(ds, q)
            dq.append(dot(key_t[h * HEAD_DIM : (h + 1) * HEAD_DIM, 0:keys], ds))
        dq = jnp.concatenate(dq, axis=0).T * 0.125
        dq = turn(dq, cos_ref[rows, :], -sa_ref[rows, :], -sb_ref[rows, :]).astype(bf16)
        out_ref[rows, 0:PAIR] = dq
        sums += jnp.sum(dq.astype(f32), axis=0, keepdims=True)
    dk = turn(dk_ref[...], cos_ref[...], -sa_ref[...], -sb_ref[...]).astype(bf16)
    dv = dv_ref[...].astype(bf16)
    out_ref[:, PAIR : 2 * PAIR] = dk
    out_ref[:, 2 * PAIR : QKV] = dv
    sum_ref[0, :, 0:PAIR] = sums
    sum_ref[0, :, PAIR : 2 * PAIR] = jnp.sum(dk.astype(f32), axis=0, keepdims=True)
    sum_ref[0, :, 2 * PAIR : QKV] = jnp.sum(dv.astype(f32), axis=0, keepdims=True)


def mix_kernel(att_ref, act_ref, w_ref, out_ref):
    left = jnp.concatenate([att_ref[...], act_ref[...]], axis=1)
    part = dot(left, w_ref[...]).astype(bf16)
    out_ref[:, 0] = part.reshape(4, 128, D)


def back_out_kernel(back_ref, *refs):
    grad_refs, refs = refs[:6], refs[6:]
    w_ref, dgelu_ref, da_ref, dup_ref, g_ref, sum_ref, hold_ref = refs

    @pl.when(pl.program_id(0) == 0)
    def _():
        sum_ref[...] = jnp.zeros_like(sum_ref)

    load_pair(back_ref, grad_blocks(grad_refs), hold_ref)
    g = hold_ref[...]
    r = dot(g, w_ref[...])
    for s in range(2):
        part = slice(256 * s, 256 * s + 256)
        g_ref[s] = g[part]
        da_ref[s] = r[part, 0:PAIR].astype(bf16)
        dup = (r[part, PAIR:] * dgelu_ref[s].astype(f32)).astype(bf16)
        dup_ref[s] = dup
        sum_ref[...] += jnp.sum(dup.astype(f32), axis=0, keepdims=True)


def back_in_kernel(back_ref, *refs):
    token_refs, refs = refs[:8], refs[8:]
    dqkv_ref, dup_ref, w_ref = refs[:3]
    to_right, to_left, *outs = refs[3:11]
    sum_ref, hold_ref = refs[11:]

    @pl.when(pl.program_id(0) == 0)
    def _():
        sum_ref[...] = jnp.zeros_like(sum_ref)

    load_pair(back_ref, token_blocks(token_refs), hold_ref)
    left = [jnp.concatenate([dqkv_ref[s], dup_ref[s]], axis=1) for s in range(2)]
    grad = dot(jnp.concatenate(left, axis=0), w_ref[...], NT)
    low = grad.astype(bf16)
    for half in range(2):
        at = back_ref[2 * pl.program_id(0) + half]
        parts = [low[256 * s + 128 * half : 256 * s + 128 * half + 128] for s in range(2)]
        for block in range(8):

            @pl.when(at == block)
            def _(block=block, parts=parts):
                group, kind = block // 4, block % 4
                if kind == 0:
                    to_right[group] = parts[0]
                    to_left[group] = parts[1]
                else:
                    ref = outs[3 * group + kind - 1]
                    for s in range(2):
                        ref[s] = parts[s]

    normed, _ = norm(hold_ref[...].astype(f32))
    sum_ref[0:1, :] += jnp.sum(grad * normed, axis=0, keepdims=True)
    sum_ref[1:2, :] += jnp.sum(grad, axis=0, keepdims=True)


def fold_kernel(a_ref, b_ref, r0, l0, r1, l1, r0o, l0o, r1o, l1o):
    for g, (r, l, ro, lo) in enumerate(((r0, l0, r0o, l0o), (r1, l1, r1o, l1o))):
        ro[0] = add(r[0], a_ref[g])
        lo[0] = add(l[0], b_ref[g])


def token_grad_kernel(x_ref, g_ref, c_ref, a_ref, b_ref, e_ref, gain_ref, out_ref):
    for s in range(2):
        grad = c_ref[s].astype(f32) + a_ref[s].astype(f32) + b_ref[s].astype(f32) + e_ref[s].astype(f32)
        normed, inverse = norm(x_ref[s].astype(f32))
        n = grad * gain_ref[...]
        inner = n - jnp.mean(n, axis=1, keepdims=True) - normed * jnp.mean(n * normed, axis=1, keepdims=True)
        out_ref[s] = (g_ref[s].astype(f32) + inverse * inner).astype(bf16)


def chunk_kernel(place_ref, out_ref, down_ref, up_ref, qkv_ref, vec_ref, mine_ref, other_ref):
    for c in range(2):

        @pl.when(place_ref[2] == c)
        def _(c=c):
            for i in range(16):
                ref, at = (mine_ref if i % 2 == c else other_ref), i // 2
                b, cols = i // 8, slice(128 * (i % 8), 128 * (i % 8) + 128)
                ref[at, :, 0:128] = out_ref[64 * b : 64 * b + 64, cols]
                for m in range(4):
                    row = 256 * b + 64 * m
                    ref[at, :, 128 + 128 * m : 256 + 128 * m] = down_ref[row : row + 64, cols]
                ref[at, :, OUT_ROWS : OUT_ROWS + FFD] = up_ref[64 * i : 64 * i + 64, :]
                ref[at, :, OUT_ROWS + FFD : SHARD - 128] = qkv_ref[64 * i : 64 * i + 64, :]
                ref[at, :, SHARD - 128 :] = vec_ref[...]


def pair_sum_kernel(mine_ref, got_ref, out_ref):
    out_ref[...] = add(mine_ref[...], got_ref[...])


def owner_sum_kernel(got_ref, out_ref, rest_ref):
    total = got_ref[0].astype(f32)
    for k in range(1, 8):
        total = total + got_ref[k].astype(f32)
    out_ref[...] = total[:, 0:OUT_ROWS].astype(bf16)
    rest_ref[...] = total[:, OUT_ROWS:].astype(bf16)


def finish_kernel(got_ref, qkv_ref, up_ref, out_ref, down_ref, vec_ref, bias_ref):
    out_got, rest_got = got_ref, got_ref.at[:, :, OUT_ROWS:]
    total = jnp.zeros((64, 128), f32)
    for k in range(8):
        at = slice(128 * k, 128 * k + 128)
        out_ref[:, at] = out_got[k, :, 0:128].astype(f32)
        for m in range(4):
            down_ref[64 * m : 64 * m + 64, at] = out_got[k, :, 128 + 128 * m : 256 + 128 * m].astype(f32)
        up_ref[:, FFD * k : FFD * k + FFD] = rest_got[k, :, 0:FFD].astype(f32)
        for t in range(3):
            start = FFD + 128 * t
            qkv_ref[:, D * t + 128 * k : D * t + 128 * k + 128] = rest_got[k, :, start : start + 128].astype(f32)
        last = rest_got[k, :, FFD + QKV :].astype(f32)
        bias_ref[k] = last
        total = total + last
    vec_ref[...] = total


def shape(dims, dtype):
    return jax.ShapeDtypeStruct(dims, dtype)


def rotary_tables():
    frequency = 10000.0 ** (-2.0 * jnp.arange(HALF, dtype=f32) / ROTARY)
    angles = jnp.arange(SEQ, dtype=f32)[:, None] * frequency[None, :]
    cosine, sine = jnp.cos(angles), jnp.sin(angles)
    one = jnp.ones((SEQ, HEAD_DIM - ROTARY), f32)
    zero = jnp.zeros((SEQ, HEAD_DIM - ROTARY), f32)
    none = jnp.zeros((SEQ, HALF), f32)
    cos = jnp.concatenate([cosine, cosine, one] * 2, axis=1)
    sine_a = jnp.concatenate([-sine, none, zero] * 2, axis=1)
    sine_b = jnp.concatenate([none, sine, zero] * 2, axis=1)
    return cos, sine_a, sine_b


def whole(dims):
    return pl.BlockSpec(dims, lambda i, *_: (0,) * len(dims))


def body(tokens, segments, ln_gain, ln_bias, w_qkv, b_qkv, w_out, b_out, w_up, b_up, w_down, b_down, out_grad):
    j = lax.axis_index("yh") * 4 + lax.axis_index("x")
    i = lax.axis_index("z") * 4 + lax.axis_index("yl") * 2 + lax.axis_index("c")
    place = [j, i, lax.axis_index("c"), lax.axis_index("z"), lax.axis_index("yl")]
    place = jnp.stack(place).astype(jnp.int32)
    back = block_of()
    tokens_n = 2 * SEQ

    rows = lambda n, size=512: pl.BlockSpec((size, n), lambda i, *_: (i, 0))
    at_j = lambda dims, base=0: pl.BlockSpec(dims, lambda i, place: (0, base + place[0]))
    pairs = lambda n: pl.BlockSpec((2, 256, n), lambda i, *_: (0, i, 0))
    flat = lambda a: a.reshape(tokens_n, -1)
    line = lambda a: a.reshape(1, -1)

    shard = call(
        shard_kernel,
        "shard",
        (1,),
        [at_j((64, 128)), at_j((64, 128), 8), at_j((64, 128), 16), at_j((64, FFD))]
        + [whole((1, n)) for n in (64, 64, 192, 64, 256, 64)],
        whole((64, IN_COLS + 128)),
        shape((64, IN_COLS + 128), bf16),
        prefetch=1,
    )(place, w_qkv, w_qkv, w_qkv, w_up, *[line(a) for a in (ln_gain, ln_bias, b_qkv, b_out, b_up, b_down)])
    w_in = lax.all_gather(shard, ("z", "yl", "c"), axis=0, tiled=True)

    other = shift(tokens, "yh", 1)
    left = shift(tokens, "x", 1)
    right = shift(tokens, "x", -1)
    g_other = shift(out_grad, "yh", 1)
    left3 = shift(jnp.concatenate([other, left[0:1]]), "x", 1)
    right3 = shift(jnp.concatenate([other, right[1:2]]), "x", -1)
    piece = call(
        piece_kernel,
        "piece",
        (1,),
        [at_j((64, 128)), at_j((256, 128))],
        whole((64, OUT_ROWS)),
        shape((64, OUT_ROWS), bf16),
        prefetch=1,
    )(place, w_out, w_down)
    piece = lax.ppermute(after(piece, left, right, other), ALL, out_pairs(False))
    far0 = shift(left3[0:1], "x", 1)
    far1 = shift(right3[1:2], "x", -1)
    token_refs = (tokens, other, left, right, left3, right3, far0, far1)
    token_specs = [whole(a.shape) for a in token_refs]
    pieces = lax.all_gather(piece, ("z", "yl", "c"), axis=0, tiled=True)

    g_both = after(jnp.concatenate([out_grad, g_other]), far0, far1)
    g_left = shift(g_both, "x", 1)
    g_right = shift(g_both, "x", -1)

    cos, sine_a, sine_b = rotary_tables()
    seg_row = segments[:, None, :]
    seg_col = segments[:, :, None]
    table = whole((SEQ, PAIR))

    hidden, qkv, activated, dgelu, small = call(
        project_kernel,
        "project",
        (4,),
        token_specs
        + [whole((D, IN_COLS)), pl.BlockSpec((D, 128), lambda i, *_: (0, 7))]
        + [pl.BlockSpec((256, PAIR), lambda i, *_: (i, 0))] * 3,
        [pairs(n) for n in (D, QKV, FFD, FFD)] + [whole((1, 39 * 128))],
        [shape((2, SEQ, n), bf16) for n in (D, QKV, FFD, FFD)] + [shape((1, 39 * 128), f32)],
        scratch=[pltpu.VMEM((512, D), bf16)],
        prefetch=1,
    )(back, *token_refs, w_in, w_in, cos, sine_a, sine_b)

    far_own, far_other = after(g_left, qkv)[0:2], after(g_right, qkv)[2:4]
    far_own, far_other = shift(far_own, "x", 1), shift(far_other, "x", -1)
    grad_refs = (out_grad, g_other, g_left, g_right, far_own, far_other)

    seg_row_spec = pl.BlockSpec((1, 1, SEQ), lambda i: (i, 0, 0))
    seg_col_spec = pl.BlockSpec((1, SEQ, 1), lambda i: (i, 0, 0))
    lse_spec = pl.BlockSpec((1, 2, SEQ), lambda i: (i, 0, 0))
    attended, lse = call(
        attend_kernel,
        "attend",
        (2,),
        [rows(QKV, SEQ), seg_row_spec, seg_col_spec],
        [rows(PAIR, SEQ), lse_spec],
        [shape((tokens_n, PAIR), bf16), shape((2, 2, SEQ), f32)],
    )(flat(qkv), seg_row, seg_col)

    w_mix, w_mix_turned = call(
        assemble_kernel,
        "assemble",
        (1,),
        [pl.BlockSpec((D, 128), functools.partial(lambda m, i: (0, m), m)) for m in range(5)],
        [whole((OUT_ROWS, D)), whole((D, OUT_ROWS))],
        [shape((OUT_ROWS, D), bf16), shape((D, OUT_ROWS), bf16)],
    )(*[pieces] * 5)
    parts = call(
        mix_kernel,
        "mix",
        (4,),
        [rows(PAIR), rows(FFD), whole((OUT_ROWS, D))],
        pl.BlockSpec((4, 1, 128, D), lambda i: (i % 2, i // 2, 0, 0)),
        shape((8, 2, 128, D), bf16),
    )(attended, flat(activated), w_mix)
    summed = lax.psum_scatter(parts, ("yh", "x"), scatter_dimension=0, tiled=True)[0]
    mixed = tokens.astype(f32) + summed.astype(f32) + (small[0, 2 * D : 3 * D] + small[0, 3 * D : 4 * D])
    mixed = mixed.astype(bf16)

    grad_attended, grad_up, g_rows, up_sums = call(
        back_out_kernel,
        "back_out",
        (4,),
        [whole(a.shape) for a in grad_refs] + [whole((D, OUT_ROWS)), pairs(FFD)],
        [pairs(PAIR), pairs(FFD), pairs(D), whole((1, FFD))],
        [shape((2, SEQ, n), bf16) for n in (PAIR, FFD, D)] + [shape((1, FFD), f32)],
        scratch=[pltpu.VMEM((512, D), bf16)],
        prefetch=1,
    )(after(back, parts), *grad_refs, w_mix_turned, dgelu)

    grad_qkv, qkv_sums = call(
        attend_back_kernel,
        "attend_back",
        (2,),
        [rows(QKV, SEQ), rows(PAIR, SEQ), lse_spec, seg_row_spec, seg_col_spec, table, table, table],
        [rows(QKV, SEQ), pl.BlockSpec((1, 1, QKV), lambda i: (i, 0, 0))],
        [shape((tokens_n, QKV), bf16), shape((2, 1, QKV), f32)],
        scratch=[pltpu.VMEM((SEQ, PAIR), f32), pltpu.VMEM((SEQ, PAIR), f32)],
    )(flat(qkv), flat(grad_attended), lse, seg_row, seg_col, cos, sine_a, sine_b)

    block = shape((2, 128, D), bf16)
    *sent, ln_sums = call(
        back_in_kernel,
        "back_in",
        (4,),
        token_specs + [pairs(QKV), pairs(FFD), whole((D, IN_COLS))],
        [whole((2, 128, D))] * 8 + [whole((2, D))],
        [block] * 8 + [shape((2, D), f32)],
        scratch=[pltpu.VMEM((512, D), bf16)],
        prefetch=1,
    )(back, *token_refs, grad_qkv.reshape(2, SEQ, QKV), grad_up, w_in)

    to_right, to_left, right0, left0, own0, right1, left1, own1 = sent
    a = shift(to_right, "x", 1)
    b = shift(to_left, "x", -1)
    first = pl.BlockSpec((1, 128, D), lambda i: (0, 0, 0))
    second = pl.BlockSpec((1, 128, D), lambda i: (1, 0, 0))
    right0, left0, right1, left1 = call(
        fold_kernel,
        "fold",
        (1,),
        [whole((2, 128, D))] * 2 + [first, second, first, second],
        [first, second, first, second],
        [block] * 4,
        alias={2: 0, 3: 1, 4: 2, 5: 3},
    )(a, b, right0, left0, right1, left1)
    from_left0 = shift(right0, "x", 1)
    from_right0 = shift(left0, "x", -1)
    from_left1 = shift(right1, "x", 1)
    from_right1 = shift(left1, "x", -1)
    total = own0.astype(f32) + from_left0.astype(f32) + from_right0.astype(f32)
    from_other = shift(total.astype(bf16), "yh", 1)
    grad_tokens = call(
        token_grad_kernel,
        "token_grad",
        (1,),
        [whole((2, 128, D))] * 6 + [pl.BlockSpec((1, D), lambda i: (0, 0))],
        whole((2, 128, D)),
        block,
    )(tokens, out_grad, own1, from_left1, from_right1, from_other, small)

    g_rows = after(flat(g_rows), to_right)
    hidden = after(flat(hidden), to_right)
    grad_out = dot(attended, g_rows, TN).astype(bf16)
    grad_down = dot(flat(activated), g_rows, TN).astype(bf16)
    grad_w_up = dot(hidden, flat(grad_up), TN).astype(bf16)
    grad_w_qkv = dot(hidden, grad_qkv, TN).astype(bf16)
    g_sum = jnp.sum(out_grad.astype(f32), axis=(0, 1))
    vec = [ln_sums.reshape(16, 128), g_sum.reshape(8, 128), jnp.sum(qkv_sums, axis=0).reshape(3, 128), up_sums.reshape(4, 128)]
    vec = jnp.pad(jnp.concatenate(vec).astype(bf16), ((0, 33), (0, 0)))
    halves = shape((8, 64, SHARD), bf16)
    own_half, other_half = call(
        chunk_kernel,
        "chunk",
        (1,),
        [whole((PAIR, D)), whole((FFD, D)), whole((D, FFD)), whole((D, QKV)), whole((64, 128))],
        [whole(halves.shape)] * 2,
        [halves] * 2,
        prefetch=1,
    )(place, after(grad_out, a, b), grad_down, grad_w_up, grad_w_qkv, vec)
    got = shift(other_half, "c", 1)
    quarter = pl.BlockSpec((2, 64, SHARD), lambda i: (i, 0, 0))
    chip_half = call(pair_sum_kernel, "pair_sum", (4,), [quarter] * 2, quarter, halves)(own_half, got)
    got = lax.all_to_all(after(chip_half, right0, left0), ("z", "yl"), 0, 0, tiled=True)
    out_owned, rest_owned = call(
        owner_sum_kernel,
        "owner_sum",
        (1,),
        [whole(halves.shape)],
        [whole((64, OUT_ROWS)), whole((64, SHARD - OUT_ROWS))],
        [shape((64, OUT_ROWS), bf16), shape((64, SHARD - OUT_ROWS), bf16)],
    )(got)
    out_owned = lax.ppermute(out_owned, ALL, out_pairs(True))

    def spread_ctx(a):
        return lax.all_to_all(jnp.broadcast_to(a[None], (8,) + a.shape), ("yh", "x"), 0, 0, tiled=True)

    both = spread_ctx(after(jnp.concatenate([out_owned, rest_owned], axis=1), grad_tokens))
    grad_w_qkv, grad_w_up, grad_w_out, grad_w_down, vec, bias = call(
        finish_kernel,
        "finish",
        (1,),
        [whole((8, 64, SHARD))],
        [whole((64, 3 * D)), whole((64, 4 * D)), whole((64, D)), whole((256, D)), whole((64, 128)), whole((8, 64, 128))],
        [shape(dims, f32) for dims in ((64, 3 * D), (64, 4 * D), (64, D), (256, D), (64, 128), (8, 64, 128))],
    )(both)
    grad_bqkv = bias[:, 24:27].transpose(1, 0, 2)
    grad_bup = bias[:, 27:31]
    mine = lambda a, size: lax.dynamic_slice_in_dim(a.reshape(-1), size * i, size)
    grad_bqkv = bias[:, 24:27].transpose(1, 0, 2)
    grad_bup = bias[:, 27:31]
    grad_bout = mine(vec[16:24], 64)
    return (
        mixed,
        grad_tokens,
        mine(vec[0:8], 64),
        mine(vec[8:16], 64),
        grad_w_qkv,
        mine(grad_bqkv, 192),
        grad_w_out,
        grad_bout,
        grad_w_up,
        mine(grad_bup, 256),
        grad_w_down,
        grad_bout,
    )


def solution(mesh):
    fine = Mesh(mesh.devices.reshape(4, 2, 2, 2, 4), ALL)
    dp = ("z", "yl", "c")
    ctx = ("yh", "x")
    in_specs = (
        P(dp, ctx, None),
        P(dp, None),
        P(dp),
        P(dp),
        P(dp, None),
        P(dp),
        P(dp, None),
        P(dp),
        P(dp, None),
        P(dp),
        P(dp, None),
        P(dp),
        P(dp, ctx, None),
    )
    out_specs = (
        P(dp, ctx, None),
        P(dp, ctx, None),
        P(dp),
        P(dp),
        P(dp, None),
        P(dp),
        P(dp, None),
        P(dp),
        P(dp, None),
        P(dp),
        P(dp, None),
        P(dp),
    )
    return jax.shard_map(body, mesh=fine, in_specs=in_specs, out_specs=out_specs, check_vma=False)
```

```python
import functools

import jax
import jax.numpy as jnp
import numpy as np
from jax import lax
from jax.experimental import pallas as pl
from jax.experimental.pallas import tpu as pltpu
from jax.sharding import Mesh
from jax.sharding import PartitionSpec as P

HEAD_DIM = 64
ROTARY = 32
HALF = ROTARY // 2
SEQ = 1024
D = 1024
PAIR = 128
FFD = 512
QKV = 3 * PAIR
IN_COLS = QKV + FFD
OUT_ROWS = PAIR + FFD
QB = 256

norm_epsilon = 1e-05
masked_score = -1e30
f32 = jnp.float32
bf16 = jnp.bfloat16
NT = (((1,), (1,)), ((), ()))
NN = (((1,), (0,)), ((), ()))
VMEM_LIMIT = 30 * 1024 * 1024
MIB = dict(shard=60, piece=60, project=60, attend=52, assemble=16, mix=16, back_out=20, attend_back=20, back_in=20, chunk=16, fold=16, pair_sum=16, owner_sum=16, finish=16, token_grad=16)
TN = (((0,), (0,)), ((), ()))
SHARD = IN_COLS + OUT_ROWS + 128
SCALE = 0.3
COST = dict(shard=2, piece=1, project=13, attend=11, assemble=3, mix=6, back_out=9, attend_back=13, back_in=14, fold=2, token_grad=3, chunk=4, pair_sum=3, owner_sum=2, finish=3)


def dot(a, b, dims=NN):
    return lax.dot_general(a, b, dims, preferred_element_type=f32)


def call(kernel, name, grid, in_specs, out_specs, out_shape, scratch=(), prefetch=0, alias=None):
    return pl.pallas_call(
        kernel,
        name=name,
        grid_spec=pltpu.PrefetchScalarGridSpec(
            num_scalar_prefetch=prefetch,
            grid=grid,
            in_specs=in_specs,
            out_specs=out_specs,
            scratch_shapes=scratch,
        ),
        out_shape=out_shape,
        input_output_aliases=alias or {},
        compiler_params=pltpu.CompilerParams(
            dimension_semantics=("arbitrary",) * len(grid), vmem_limit_bytes=int(MIB.get(name, 52) * 1024 * 1024)
        ),
        cost_estimate=pl.CostEstimate(flops=int(COST.get(name, 1) * 1e9 * SCALE), bytes_accessed=int(COST.get(name, 1) * 1000000 * SCALE), transcendentals=0),
    )


ALL = ("z", "yl", "c", "yh", "x")


def shift(x, axis, by):
    count = lax.axis_size(axis)
    return lax.ppermute(x, axis, [(i, (i + by) % count) for i in range(count)])


def after(x, *others):
    return lax.optimization_barrier((x,) + others)[0]


def add(a, b):
    return (a.astype(f32) + b.astype(f32)).astype(bf16)


def block_of():
    at = jnp.arange(8, dtype=jnp.int32)
    same = (at // 4) == lax.axis_index("yh")
    step = (at % 4 - lax.axis_index("x")) % 4
    kind = jnp.where(step == 0, 3, jnp.where(step == 1, 1, jnp.where(step == 2, 0, 2)))
    return (jnp.where(same, 4, 0) + kind).astype(jnp.int32)


def out_pairs(back):
    pairs = []
    for j in range(8):
        for b in range(2):
            for k in range(8):
                pairs.append(((2 * j + b) * 8 + k, (8 * b + k) * 8 + j))
    return [(t, s) for s, t in pairs] if back else pairs


def turn(v, cosine, sine_a, sine_b):
    return v * cosine + pltpu.roll(v, PAIR - HALF, 1) * sine_a + pltpu.roll(v, HALF, 1) * sine_b


def norm(x):
    center = x - jnp.mean(x, axis=1, keepdims=True)
    inverse = lax.rsqrt(jnp.mean(center * center, axis=1, keepdims=True) + norm_epsilon)
    return center * inverse, inverse


def piece_kernel(place_ref, out_ref, down_ref, piece_ref):
    piece_ref[:, 0:128] = out_ref[...]
    for m in range(4):
        piece_ref[:, 128 + 128 * m : 256 + 128 * m] = down_ref[64 * m : 64 * m + 64, :]


def spread(row, size, offset):
    n = row.shape[1]
    v = lax.broadcasted_iota(jnp.int32, (n, size), 0)
    t = lax.broadcasted_iota(jnp.int32, (n, size), 1)
    return dot(row, jnp.where(offset(t) == v, 1.0, 0.0).astype(bf16))


def shard_kernel(place_ref, q_ref, k_ref, v_ref, up_ref, gain_ref, lbias_ref, bqkv_ref, bout_ref, bup_ref, bdown_ref, shard_ref):
    j, i = place_ref[0], place_ref[1]
    shard_ref[:, 0:128] = q_ref[...]
    shard_ref[:, 128:256] = k_ref[...]
    shard_ref[:, 256:384] = v_ref[...]
    shard_ref[:, QKV:IN_COLS] = up_ref[...]
    rows = []
    for ref in (gain_ref, lbias_ref, bout_ref, bdown_ref):
        rows.append(spread(ref[...], D, lambda t: t - 64 * i))
    rows.append(spread(bqkv_ref[...], QKV, lambda t: (t // 128) * D + 128 * j + t % 128 - 192 * i))
    rows.append(spread(bup_ref[...], FFD, lambda t: t + FFD * j - 256 * i))
    row = jnp.concatenate(rows, axis=1)
    count = row.shape[1] // 128
    table = jnp.concatenate([row[:, 128 * r : 128 * r + 128] for r in range(count)] + [jnp.zeros((64 - count, 128), f32)], axis=0)
    shard_ref[:, IN_COLS:] = table.astype(bf16)


def assemble_kernel(g0, g1, g2, g3, g4, out_ref, turned_ref):
    for i in range(16):
        b, k = i // 8, i % 8
        rows = pl.ds(64 * i, 64)
        at = pl.ds(128 * k, 128)
        for m, g_ref in enumerate((g0, g1, g2, g3, g4)):
            row = 64 * b if m == 0 else PAIR + 256 * b + 64 * (m - 1)
            out_ref[pl.ds(row, 64), at] = g_ref[rows, :]
    turned_ref[...] = out_ref[...].T


def token_blocks(refs):
    own, other, left, right, left3, right3, far0, far1 = refs
    return [
        ((far0, 0), (far1, 0)),
        ((right3, 0), (right3, 1)),
        ((left3, 0), (left3, 1)),
        ((other, 0), (other, 1)),
        ((left3, 2), (right3, 2)),
        ((right, 0), (right, 1)),
        ((left, 0), (left, 1)),
        ((own, 0), (own, 1)),
    ]


def grad_blocks(refs):
    own, other, left, right, far_own, far_other = refs
    return [
        ((far_other, 0), (far_other, 1)),
        ((right, 2), (right, 3)),
        ((left, 2), (left, 3)),
        ((other, 0), (other, 1)),
        ((far_own, 0), (far_own, 1)),
        ((right, 0), (right, 1)),
        ((left, 0), (left, 1)),
        ((own, 0), (own, 1)),
    ]


def load_pair(back_ref, blocks, hold_ref):
    for half in range(2):
        want = back_ref[2 * pl.program_id(0) + half]
        for block, pair in enumerate(blocks):

            @pl.when(want == block)
            def _(pair=pair):
                for s, (ref, row) in enumerate(pair):
                    hold_ref[256 * s + 128 * half : 256 * s + 128 * half + 128, :] = ref[row]


def project_kernel(back_ref, *refs):
    token_refs, refs = refs[:8], refs[8:]
    w_ref, vec_ref, cos_ref, sa_ref, sb_ref = refs[:5]
    hid_ref, qkv_ref, act_ref, dgelu_ref, small_ref, hold_ref = refs[5:]

    @pl.when(pl.program_id(0) == 0)
    def _():
        total = vec_ref[0:64, :].astype(f32)
        for i in range(1, 16):
            total = total + vec_ref[64 * i : 64 * i + 64, :].astype(f32)
        small_ref[...] = jnp.concatenate([total[r : r + 1, :] for r in range(39)], axis=1)

    load_pair(back_ref, token_blocks(token_refs), hold_ref)
    gain, lbias = small_ref[:, 0:D], small_ref[:, D : 2 * D]
    bias = small_ref[:, 4 * D :]
    cosine, sa, sb = cos_ref[...], sa_ref[...], sb_ref[...]
    for s in range(2):
        normed, _ = norm(hold_ref[256 * s : 256 * s + 256, :].astype(f32))
        hidden = (normed * gain + lbias).astype(bf16)
        proj = dot(hidden, w_ref[...]) + bias
        hid_ref[s] = hidden
        qkv_ref[s, :, 0:PAIR] = turn(proj[:, 0:PAIR], cosine, sa, sb).astype(bf16)
        qkv_ref[s, :, PAIR : 2 * PAIR] = turn(proj[:, PAIR : 2 * PAIR], cosine, sa, sb).astype(bf16)
        qkv_ref[s, :, 2 * PAIR : QKV] = proj[:, 2 * PAIR : QKV].astype(bf16)
        up = proj[:, QKV:]
        cdf = 0.5 * (1.0 + lax.erf(up * 0.7071067811865476))
        density = jnp.exp(-0.5 * up * up) * 0.3989422804014327
        act_ref[s] = (up * cdf).astype(bf16)
        dgelu_ref[s] = (cdf + up * density).astype(bf16)


def head_lanes(h):
    lane = lax.broadcasted_iota(jnp.int32, (1, PAIR), 1)
    return (lane < HEAD_DIM) if h == 0 else (lane >= HEAD_DIM)


def allowed_mask(seg_row_ref, seg_col_ref, b, keys):
    key_pos = lax.broadcasted_iota(jnp.int32, (keys, QB), 0)
    query_pos = lax.broadcasted_iota(jnp.int32, (keys, QB), 1) + b * QB
    same = seg_col_ref[0, 0:keys, :] == seg_row_ref[0, :, b * QB : (b + 1) * QB]
    return (key_pos <= query_pos) & same


def attend_kernel(qkv_ref, seg_row_ref, seg_col_ref, att_ref, lse_ref):
    value_t = qkv_ref[:, 2 * PAIR : QKV].astype(f32).T.astype(bf16)
    for b in range(SEQ // QB):
        keys = (b + 1) * QB
        rows = slice(b * QB, (b + 1) * QB)
        allowed = allowed_mask(seg_row_ref, seg_col_ref, b, keys)
        query = qkv_ref[rows, 0:PAIR]
        mixed = []
        for h in range(2):
            q = jnp.where(head_lanes(h), query * 0.125, jnp.zeros_like(query))
            s = jnp.where(allowed, dot(qkv_ref[0:keys, PAIR : 2 * PAIR], q, NT), masked_score)
            top = jnp.max(s, axis=0, keepdims=True)
            e = jnp.exp(s - top)
            total = jnp.sum(e, axis=0, keepdims=True)
            p = (e * (1.0 / total)).astype(bf16)
            lse_ref[0, h : h + 1, rows] = top + jnp.log(total)
            mixed.append(dot(value_t[h * HEAD_DIM : (h + 1) * HEAD_DIM, 0:keys], p))
        att_ref[rows, :] = jnp.concatenate(mixed, axis=0).T.astype(bf16)


def attend_back_kernel(
    qkv_ref, da_ref, lse_ref, seg_row_ref, seg_col_ref, cos_ref, sa_ref, sb_ref, out_ref, sum_ref, dk_ref, dv_ref
):
    key_t = qkv_ref[:, PAIR : 2 * PAIR].astype(f32).T.astype(bf16)
    dk_ref[...] = jnp.zeros_like(dk_ref)
    dv_ref[...] = jnp.zeros_like(dv_ref)
    sums = jnp.zeros((1, PAIR), f32)
    for b in range(SEQ // QB):
        keys = (b + 1) * QB
        rows = slice(b * QB, (b + 1) * QB)
        allowed = allowed_mask(seg_row_ref, seg_col_ref, b, keys)
        query = qkv_ref[rows, 0:PAIR]
        grad = da_ref[rows, :]
        dq = []
        for h in range(2):
            q = jnp.where(head_lanes(h), query * 0.125, jnp.zeros_like(query))
            g = jnp.where(head_lanes(h), grad, jnp.zeros_like(grad))
            s = jnp.where(allowed, dot(qkv_ref[0:keys, PAIR : 2 * PAIR], q, NT), masked_score)
            soft = jnp.exp(s - lse_ref[0, h : h + 1, rows])
            dp = dot(qkv_ref[0:keys, 2 * PAIR : QKV], g, NT)
            t = soft * dp
            inner = jnp.sum(t, axis=0, keepdims=True)
            ds = (t - soft * inner).astype(bf16)
            dv_ref[0:keys, :] += dot(soft.astype(bf16), g)
            dk_ref[0:keys, :] += dot(ds, q)
            dq.append(dot(key_t[h * HEAD_DIM : (h + 1) * HEAD_DIM, 0:keys], ds))
        dq = jnp.concatenate(dq, axis=0).T * 0.125
        dq = turn(dq, cos_ref[rows, :], -sa_ref[rows, :], -sb_ref[rows, :]).astype(bf16)
        out_ref[rows, 0:PAIR] = dq
        sums += jnp.sum(dq.astype(f32), axis=0, keepdims=True)
    dk = turn(dk_ref[...], cos_ref[...], -sa_ref[...], -sb_ref[...]).astype(bf16)
    dv = dv_ref[...].astype(bf16)
    out_ref[:, PAIR : 2 * PAIR] = dk
    out_ref[:, 2 * PAIR : QKV] = dv
    sum_ref[0, :, 0:PAIR] = sums
    sum_ref[0, :, PAIR : 2 * PAIR] = jnp.sum(dk.astype(f32), axis=0, keepdims=True)
    sum_ref[0, :, 2 * PAIR : QKV] = jnp.sum(dv.astype(f32), axis=0, keepdims=True)


def mix_kernel(att_ref, act_ref, w_ref, out_ref):
    left = jnp.concatenate([att_ref[...], act_ref[...]], axis=1)
    part = dot(left, w_ref[...]).astype(bf16)
    out_ref[:, 0] = part.reshape(4, 128, D)


def back_out_kernel(back_ref, *refs):
    grad_refs, refs = refs[:6], refs[6:]
    w_ref, dgelu_ref, da_ref, dup_ref, g_ref, sum_ref, hold_ref = refs

    @pl.when(pl.program_id(0) == 0)
    def _():
        sum_ref[...] = jnp.zeros_like(sum_ref)

    load_pair(back_ref, grad_blocks(grad_refs), hold_ref)
    g = hold_ref[...]
    r = dot(g, w_ref[...])
    for s in range(2):
        part = slice(256 * s, 256 * s + 256)
        g_ref[s] = g[part]
        da_ref[s] = r[part, 0:PAIR].astype(bf16)
        dup = (r[part, PAIR:] * dgelu_ref[s].astype(f32)).astype(bf16)
        dup_ref[s] = dup
        sum_ref[...] += jnp.sum(dup.astype(f32), axis=0, keepdims=True)


def back_in_kernel(back_ref, *refs):
    token_refs, refs = refs[:8], refs[8:]
    dqkv_ref, dup_ref, w_ref = refs[:3]
    to_right, to_left, *outs = refs[3:11]
    sum_ref, hold_ref = refs[11:]

    @pl.when(pl.program_id(0) == 0)
    def _():
        sum_ref[...] = jnp.zeros_like(sum_ref)

    load_pair(back_ref, token_blocks(token_refs), hold_ref)
    left = [jnp.concatenate([dqkv_ref[s], dup_ref[s]], axis=1) for s in range(2)]
    grad = dot(jnp.concatenate(left, axis=0), w_ref[...], NT)
    low = grad.astype(bf16)
    for half in range(2):
        at = back_ref[2 * pl.program_id(0) + half]
        parts = [low[256 * s + 128 * half : 256 * s + 128 * half + 128] for s in range(2)]
        for block in range(8):

            @pl.when(at == block)
            def _(block=block, parts=parts):
                group, kind = block // 4, block % 4
                if kind == 0:
                    to_right[group] = parts[0]
                    to_left[group] = parts[1]
                else:
                    ref = outs[3 * group + kind - 1]
                    for s in range(2):
                        ref[s] = parts[s]

    normed, _ = norm(hold_ref[...].astype(f32))
    sum_ref[0:1, :] += jnp.sum(grad * normed, axis=0, keepdims=True)
    sum_ref[1:2, :] += jnp.sum(grad, axis=0, keepdims=True)


def fold_kernel(a_ref, b_ref, r0, l0, r1, l1, r0o, l0o, r1o, l1o):
    for g, (r, l, ro, lo) in enumerate(((r0, l0, r0o, l0o), (r1, l1, r1o, l1o))):
        ro[0] = add(r[0], a_ref[g])
        lo[0] = add(l[0], b_ref[g])


def token_grad_kernel(x_ref, g_ref, c_ref, a_ref, b_ref, e_ref, gain_ref, out_ref):
    for s in range(2):
        grad = c_ref[s].astype(f32) + a_ref[s].astype(f32) + b_ref[s].astype(f32) + e_ref[s].astype(f32)
        normed, inverse = norm(x_ref[s].astype(f32))
        n = grad * gain_ref[...]
        inner = n - jnp.mean(n, axis=1, keepdims=True) - normed * jnp.mean(n * normed, axis=1, keepdims=True)
        out_ref[s] = (g_ref[s].astype(f32) + inverse * inner).astype(bf16)


def chunk_kernel(place_ref, out_ref, down_ref, up_ref, qkv_ref, vec_ref, mine_ref, other_ref):
    for c in range(2):

        @pl.when(place_ref[2] == c)
        def _(c=c):
            for i in range(16):
                ref, at = (mine_ref if i % 2 == c else other_ref), i // 2
                b, cols = i // 8, slice(128 * (i % 8), 128 * (i % 8) + 128)
                ref[at, :, 0:128] = out_ref[64 * b : 64 * b + 64, cols]
                for m in range(4):
                    row = 256 * b + 64 * m
                    ref[at, :, 128 + 128 * m : 256 + 128 * m] = down_ref[row : row + 64, cols]
                ref[at, :, OUT_ROWS : OUT_ROWS + FFD] = up_ref[64 * i : 64 * i + 64, :]
                ref[at, :, OUT_ROWS + FFD : SHARD - 128] = qkv_ref[64 * i : 64 * i + 64, :]
                ref[at, :, SHARD - 128 :] = vec_ref[...]


def pair_sum_kernel(mine_ref, got_ref, out_ref):
    out_ref[...] = add(mine_ref[...], got_ref[...])


def owner_sum_kernel(got_ref, out_ref, rest_ref):
    total = got_ref[0].astype(f32)
    for k in range(1, 8):
        total = total + got_ref[k].astype(f32)
    out_ref[...] = total[:, 0:OUT_ROWS].astype(bf16)
    rest_ref[...] = total[:, OUT_ROWS:].astype(bf16)


def finish_kernel(place_ref, got_ref, qkv_ref, up_ref, out_ref, down_ref, gain_ref, lbias_ref, bqkv_ref, bout_ref, bup_ref, vec_ref, bq_ref, bu_ref):
    i = place_ref[1]
    total = jnp.zeros((64, 128), f32)
    for k in range(8):
        at = slice(128 * k, 128 * k + 128)
        out_ref[:, at] = got_ref[k, :, 0:128].astype(f32)
        for m in range(4):
            down_ref[64 * m : 64 * m + 64, at] = got_ref[k, :, 128 + 128 * m : 256 + 128 * m].astype(f32)
        up_ref[:, FFD * k : FFD * k + FFD] = got_ref[k, :, OUT_ROWS : OUT_ROWS + FFD].astype(f32)
        for t in range(3):
            start = OUT_ROWS + FFD + 128 * t
            qkv_ref[:, D * t + 128 * k : D * t + 128 * k + 128] = got_ref[k, :, start : start + 128].astype(f32)
        last = got_ref[k, :, SHARD - 128 :].astype(f32)
        for t in range(3):
            bq_ref[8 * t + k : 8 * t + k + 1, :] = last[24 + t : 25 + t, :]
        bu_ref[4 * k : 4 * k + 4, :] = last[27:31, :]
        total = total + last
    vec_ref[...] = total
    odd = i % 2 == 1

    def lanes(row):
        return jnp.where(odd, pltpu.roll(row, 64, 1), row)

    for n, ref in enumerate((gain_ref, lbias_ref, bout_ref)):
        ref[...] = lanes(vec_ref[pl.ds(8 * n + i // 2, 1), :])[:, 0:64]
    start = (3 * i) // 2
    first, second = bq_ref[pl.ds(start, 1), :], bq_ref[pl.ds(start + 1, 1), :]
    lane = lax.broadcasted_iota(jnp.int32, (1, 128), 1)
    turned0, turned1 = pltpu.roll(first, 64, 1), pltpu.roll(second, 64, 1)
    bqkv_ref[:, 0:128] = jnp.where(odd, jnp.where(lane < 64, turned0, turned1), first)
    bqkv_ref[:, 128:192] = jnp.where(odd, turned1, second)[:, 0:64]
    bup_ref[:, 0:128] = bu_ref[pl.ds(2 * i, 1), :]
    bup_ref[:, 128:256] = bu_ref[pl.ds(2 * i + 1, 1), :]


def shape(dims, dtype):
    return jax.ShapeDtypeStruct(dims, dtype)


def rotary_tables():
    frequency = np.float32(10000.0) ** (np.float32(-2.0) * np.arange(HALF, dtype=np.float32) / np.float32(ROTARY))
    angles = np.arange(SEQ, dtype=np.float32)[:, None] * frequency.astype(np.float32)[None, :]
    cosine, sine = np.cos(angles.astype(np.float64)), np.sin(angles.astype(np.float64))
    one = np.ones((SEQ, HEAD_DIM - ROTARY))
    zero = np.zeros((SEQ, HEAD_DIM - ROTARY))
    none = np.zeros((SEQ, HALF))
    cos = np.concatenate([cosine, cosine, one] * 2, axis=1)
    sine_a = np.concatenate([-sine, none, zero] * 2, axis=1)
    sine_b = np.concatenate([none, sine, zero] * 2, axis=1)
    return [jnp.asarray(t.astype(np.float32)) for t in (cos, sine_a, sine_b)]


def whole(dims):
    return pl.BlockSpec(dims, lambda i, *_: (0,) * len(dims), pipeline_mode=pl.Buffered(1))


def fixed(dims):
    return pl.BlockSpec(dims, lambda i, *_: (0,) * len(dims))


def body(tokens, segments, ln_gain, ln_bias, w_qkv, b_qkv, w_out, b_out, w_up, b_up, w_down, b_down, out_grad):
    j = lax.axis_index("yh") * 4 + lax.axis_index("x")
    i = lax.axis_index("z") * 4 + lax.axis_index("yl") * 2 + lax.axis_index("c")
    place = [j, i, lax.axis_index("c"), lax.axis_index("z"), lax.axis_index("yl")]
    place = jnp.stack(place).astype(jnp.int32)
    back = block_of()
    tokens_n = 2 * SEQ

    rows = lambda n, size=512: pl.BlockSpec((size, n), lambda i, *_: (i, 0))
    at_j = lambda dims, base=0: pl.BlockSpec(dims, lambda i, place: (0, base + place[0]))
    pairs = lambda n: pl.BlockSpec((2, 256, n), lambda i, *_: (0, i, 0))
    by_seq = lambda n: pl.BlockSpec((n, 1, 128, D), lambda i: (0, i, 0, 0))
    own_seq = pl.BlockSpec((1, 128, D), lambda i: (i, 0, 0))
    own_block = shape((2, 128, D), bf16)
    flat = lambda a: a.reshape(tokens_n, -1)
    line = lambda a: a.reshape(1, -1)

    shard = call(
        shard_kernel,
        "shard",
        (1,),
        [at_j((64, 128)), at_j((64, 128), 8), at_j((64, 128), 16), at_j((64, FFD))]
        + [whole((1, n)) for n in (64, 64, 192, 64, 256, 64)],
        fixed((64, IN_COLS + 128)),
        shape((64, IN_COLS + 128), bf16),
        prefetch=1,
    )(place, w_qkv, w_qkv, w_qkv, w_up, *[line(a) for a in (ln_gain, ln_bias, b_qkv, b_out, b_up, b_down)])
    w_in = lax.all_gather(shard, ("z", "yl", "c"), axis=0, tiled=True)

    other = shift(tokens, "yh", 1)
    left = shift(tokens, "x", 1)
    right = shift(tokens, "x", -1)
    g_other = shift(after(out_grad, left, right, other), "yh", 1)
    left3 = shift(jnp.concatenate([other, left[0:1]]), "x", 1)
    right3 = shift(jnp.concatenate([other, right[1:2]]), "x", -1)
    piece = call(
        piece_kernel,
        "piece",
        (1,),
        [at_j((64, 128)), at_j((256, 128))],
        fixed((64, OUT_ROWS)),
        shape((64, OUT_ROWS), bf16),
        prefetch=1,
    )(place, w_out, w_down)
    piece = lax.ppermute(after(piece, left3, right3), ALL, out_pairs(False))
    far0 = shift(after(left3, g_other)[0:1], "x", 1)
    far1 = shift(after(right3, g_other)[1:2], "x", -1)
    token_refs = (tokens, other, left, right, left3, right3, far0, far1)
    token_specs = [whole(a.shape) for a in token_refs]
    pieces = lax.all_gather(after(piece, far0, far1), ("z", "yl", "c"), axis=0, tiled=True)

    g_both = after(jnp.concatenate([out_grad, g_other]), far0, far1)
    g_left = shift(g_both, "x", 1)
    g_right = shift(g_both, "x", -1)

    cos, sine_a, sine_b = rotary_tables()
    seg_row = segments[:, None, :]
    seg_col = segments[:, :, None]
    table = whole((SEQ, PAIR))

    hidden, qkv, activated, dgelu, small = call(
        project_kernel,
        "project",
        (4,),
        token_specs
        + [whole((D, IN_COLS)), pl.BlockSpec((D, 128), lambda i, *_: (0, 7))]
        + [pl.BlockSpec((256, PAIR), lambda i, *_: (i, 0))] * 3,
        [pairs(n) for n in (D, QKV, FFD, FFD)] + [fixed((1, 39 * 128))],
        [pltpu.HBM((2, SEQ, n), bf16) for n in (D, QKV, FFD, FFD)] + [shape((1, 39 * 128), f32)],
        scratch=[pltpu.VMEM((512, D), bf16)],
        prefetch=1,
    )(back, *token_refs, w_in, w_in, cos, sine_a, sine_b)

    seg_row_spec = pl.BlockSpec((1, 1, SEQ), lambda i: (i, 0, 0))
    seg_col_spec = pl.BlockSpec((1, SEQ, 1), lambda i: (i, 0, 0))
    lse_spec = pl.BlockSpec((1, 2, SEQ), lambda i: (i, 0, 0))
    attended, lse = call(
        attend_kernel,
        "attend",
        (2,),
        [rows(QKV, SEQ), seg_row_spec, seg_col_spec],
        [rows(PAIR, SEQ), lse_spec],
        [shape((tokens_n, PAIR), bf16), shape((2, 2, SEQ), f32)],
    )(flat(qkv), seg_row, seg_col)

    far_own, far_other = after(g_left, attended)[0:2], after(g_right, attended)[2:4]
    far_own, far_other = shift(far_own, "x", 1), shift(far_other, "x", -1)
    grad_refs = (out_grad, g_other, g_left, g_right, far_own, far_other)

    w_mix, w_mix_turned = call(
        assemble_kernel,
        "assemble",
        (1,),
        [pl.BlockSpec((D, 128), functools.partial(lambda m, i: (0, m), m)) for m in range(5)],
        [fixed((OUT_ROWS, D)), fixed((D, OUT_ROWS))],
        [shape((OUT_ROWS, D), bf16), shape((D, OUT_ROWS), bf16)],
    )(*[pieces] * 5)
    parts = call(
        mix_kernel,
        "mix",
        (4,),
        [rows(PAIR), rows(FFD), whole((OUT_ROWS, D))],
        pl.BlockSpec((4, 1, 128, D), lambda i: (i % 2, i // 2, 0, 0)),
        pltpu.HBM((8, 2, 128, D), bf16),
    )(attended, flat(activated), w_mix)
    summed = lax.psum_scatter(parts, ("yh", "x"), scatter_dimension=0, tiled=True)[0]
    mixed = tokens.astype(f32) + summed.astype(f32) + (small[0, 2 * D : 3 * D] + small[0, 3 * D : 4 * D])
    mixed = mixed.astype(bf16)
    grad_attended, grad_up, g_rows, up_sums = call(
        back_out_kernel,
        "back_out",
        (4,),
        [whole(a.shape) for a in grad_refs] + [whole((D, OUT_ROWS)), pairs(FFD)],
        [pairs(PAIR), pairs(FFD), pairs(D), fixed((1, FFD))],
        [shape((2, SEQ, n), bf16) for n in (PAIR, FFD)] + [pltpu.HBM((2, SEQ, D), bf16)] + [shape((1, FFD), f32)],
        scratch=[pltpu.VMEM((512, D), bf16)],
        prefetch=1,
    )(after(back, parts), *grad_refs, w_mix_turned, dgelu)

    grad_qkv, qkv_sums = call(
        attend_back_kernel,
        "attend_back",
        (2,),
        [rows(QKV, SEQ), rows(PAIR, SEQ), lse_spec, seg_row_spec, seg_col_spec, table, table, table],
        [rows(QKV, SEQ), pl.BlockSpec((1, 1, QKV), lambda i: (i, 0, 0))],
        [shape((tokens_n, QKV), bf16), shape((2, 1, QKV), f32)],
        scratch=[pltpu.VMEM((SEQ, PAIR), f32), pltpu.VMEM((SEQ, PAIR), f32)],
    )(flat(qkv), flat(grad_attended), lse, seg_row, seg_col, cos, sine_a, sine_b)

    block = shape((2, 128, D), bf16)
    *sent, ln_sums = call(
        back_in_kernel,
        "back_in",
        (4,),
        token_specs + [pairs(QKV), pairs(FFD), whole((D, IN_COLS))],
        [fixed((2, 128, D))] * 8 + [fixed((2, D))],
        [block] * 8 + [shape((2, D), f32)],
        scratch=[pltpu.VMEM((512, D), bf16)],
        prefetch=1,
    )(back, *token_refs, grad_qkv.reshape(2, SEQ, QKV), grad_up, w_in)

    to_right, to_left, right0, left0, own0, right1, left1, own1 = sent
    a = shift(to_right, "x", 1)
    b = shift(to_left, "x", -1)
    first = pl.BlockSpec((1, 128, D), lambda i: (0, 0, 0))
    second = pl.BlockSpec((1, 128, D), lambda i: (1, 0, 0))
    right0, left0, right1, left1 = call(
        fold_kernel,
        "fold",
        (1,),
        [whole((2, 128, D))] * 2 + [first, second, first, second],
        [first, second, first, second],
        [block] * 4,
        alias={2: 0, 3: 1, 4: 2, 5: 3},
    )(a, b, right0, left0, right1, left1)
    from_left0 = shift(right0, "x", 1)
    from_right0 = shift(left0, "x", -1)
    from_left1 = shift(right1, "x", 1)
    from_right1 = shift(left1, "x", -1)
    total = own0.astype(f32) + from_left0.astype(f32) + from_right0.astype(f32)
    from_other = shift(total.astype(bf16), "yh", 1)
    grad_tokens = call(
        token_grad_kernel,
        "token_grad",
        (1,),
        [whole((2, 128, D))] * 6 + [pl.BlockSpec((1, D), lambda i: (0, 0))],
        fixed((2, 128, D)),
        block,
    )(tokens, out_grad, own1, from_left1, from_right1, from_other, small)

    g_rows = after(flat(g_rows), to_right)
    hidden = after(flat(hidden), to_right)
    grad_out = dot(attended, g_rows, TN).astype(bf16)
    grad_down = dot(flat(activated), g_rows, TN).astype(bf16)
    grad_w_up = dot(hidden, flat(grad_up), TN).astype(bf16)
    grad_w_qkv = dot(hidden, grad_qkv, TN).astype(bf16)
    g_sum = jnp.sum(out_grad.astype(f32), axis=(0, 1))
    vec = [ln_sums.reshape(16, 128), g_sum.reshape(8, 128), jnp.sum(qkv_sums, axis=0).reshape(3, 128), up_sums.reshape(4, 128)]
    vec = jnp.pad(jnp.concatenate(vec).astype(bf16), ((0, 33), (0, 0)))
    halves = shape((8, 64, SHARD), bf16)
    own_half, other_half = call(
        chunk_kernel,
        "chunk",
        (1,),
        [whole((PAIR, D)), whole((FFD, D)), whole((D, FFD)), whole((D, QKV)), whole((64, 128))],
        [fixed(halves.shape)] * 2,
        [halves] * 2,
        prefetch=1,
    )(place, after(grad_out, a, b), grad_down, grad_w_up, grad_w_qkv, vec)
    got = shift(other_half, "c", 1)
    quarter = pl.BlockSpec((2, 64, SHARD), lambda i: (i, 0, 0))
    chip_half = call(pair_sum_kernel, "pair_sum", (4,), [quarter] * 2, quarter, halves)(own_half, got)
    got = lax.all_to_all(after(chip_half, right0, left0), ("z", "yl"), 0, 0, tiled=True)
    out_owned, rest_owned = call(
        owner_sum_kernel,
        "owner_sum",
        (1,),
        [whole(halves.shape)],
        [fixed((64, OUT_ROWS)), fixed((64, SHARD - OUT_ROWS))],
        [shape((64, OUT_ROWS), bf16), shape((64, SHARD - OUT_ROWS), bf16)],
    )(got)
    out_owned = lax.ppermute(out_owned, ALL, out_pairs(True))

    def spread_ctx(a):
        return lax.all_to_all(jnp.broadcast_to(a[None], (8,) + a.shape), ("yh", "x"), 0, 0, tiled=True)

    both = spread_ctx(after(jnp.concatenate([out_owned, rest_owned], axis=1), grad_tokens))
    sizes = [(64, 3 * D), (64, 4 * D), (64, D), (256, D), (1, 64), (1, 64), (1, 192), (1, 64), (1, 256)]
    done = call(
        finish_kernel,
        "finish",
        (1,),
        [fixed((8, 64, SHARD))],
        [fixed(dims) for dims in sizes],
        [shape(dims, f32) for dims in sizes],
        scratch=[pltpu.VMEM((64, 128), f32), pltpu.VMEM((32, 128), f32), pltpu.VMEM((32, 128), f32)],
        prefetch=1,
    )(place, both)
    grad_w_qkv, grad_w_up, grad_w_out, grad_w_down = done[:4]
    grad_gain, grad_lbias, grad_bqkv, grad_bout, grad_bup = [a.reshape(-1) for a in done[4:]]
    return (
        mixed,
        grad_tokens,
        grad_gain,
        grad_lbias,
        grad_w_qkv,
        grad_bqkv,
        grad_w_out,
        grad_bout,
        grad_w_up,
        grad_bup,
        grad_w_down,
        grad_bout,
    )


def solution(mesh):
    fine = Mesh(mesh.devices.reshape(4, 2, 2, 2, 4), ALL)
    dp = ("z", "yl", "c")
    ctx = ("yh", "x")
    in_specs = (
        P(dp, ctx, None),
        P(dp, None),
        P(dp),
        P(dp),
        P(dp, None),
        P(dp),
        P(dp, None),
        P(dp),
        P(dp, None),
        P(dp),
        P(dp, None),
        P(dp),
        P(dp, ctx, None),
    )
    out_specs = (
        P(dp, ctx, None),
        P(dp, ctx, None),
        P(dp),
        P(dp),
        P(dp, None),
        P(dp),
        P(dp, None),
        P(dp),
        P(dp, None),
        P(dp),
        P(dp, None),
        P(dp),
    )
    return jax.shard_map(body, mesh=fine, in_specs=in_specs, out_specs=out_specs, check_vma=False)
```

```python
import functools

import jax
import jax.numpy as jnp
import numpy as np
from jax import lax
from jax.experimental import pallas as pl
from jax.experimental.pallas import tpu as pltpu
from jax.sharding import Mesh
from jax.sharding import PartitionSpec as P

HEAD_DIM = 64
ROTARY = 32
HALF = ROTARY // 2
SEQ = 1024
D = 1024
PAIR = 128
FFD = 512
QKV = 3 * PAIR
IN_COLS = QKV + FFD
OUT_ROWS = PAIR + FFD
QB = 256

norm_epsilon = 1e-05
masked_score = -1e30
f32 = jnp.float32
bf16 = jnp.bfloat16
NT = (((1,), (1,)), ((), ()))
NN = (((1,), (0,)), ((), ()))
VMEM_LIMIT = 30 * 1024 * 1024
MIB = dict(shard=60, piece=60, project=60, attend=52, assemble=16, mix=16, back_out=60, attend_back=20, back_in=20, chunk=16, fold=16, pair_sum=16, owner_sum=16, finish=16, token_grad=16)
TN = (((0,), (0,)), ((), ()))
SHARD = IN_COLS + OUT_ROWS + 128
SCALE = 0.3
COST = dict(shard=2, piece=1, project=13, attend=11, assemble=3, mix=6, back_out=9, attend_back=13, back_in=14, fold=2, token_grad=3, chunk=4, pair_sum=3, owner_sum=2, finish=3)


def dot(a, b, dims=NN):
    return lax.dot_general(a, b, dims, preferred_element_type=f32)


def call(kernel, name, grid, in_specs, out_specs, out_shape, scratch=(), prefetch=0, alias=None):
    return pl.pallas_call(
        kernel,
        name=name,
        grid_spec=pltpu.PrefetchScalarGridSpec(
            num_scalar_prefetch=prefetch,
            grid=grid,
            in_specs=in_specs,
            out_specs=out_specs,
            scratch_shapes=scratch,
        ),
        out_shape=out_shape,
        input_output_aliases=alias or {},
        compiler_params=pltpu.CompilerParams(
            dimension_semantics=("arbitrary",) * len(grid), vmem_limit_bytes=int(MIB.get(name, 52) * 1024 * 1024)
        ),
        cost_estimate=pl.CostEstimate(flops=int(COST.get(name, 1) * 1e9 * SCALE), bytes_accessed=int(COST.get(name, 1) * 1000000 * SCALE), transcendentals=0),
    )


ALL = ("z", "yl", "c", "yh", "x")


def shift(x, axis, by):
    count = lax.axis_size(axis)
    return lax.ppermute(x, axis, [(i, (i + by) % count) for i in range(count)])


def after(x, *others):
    return lax.optimization_barrier((x,) + others)[0]


def add(a, b):
    return (a.astype(f32) + b.astype(f32)).astype(bf16)


def block_of():
    at = jnp.arange(8, dtype=jnp.int32)
    same = (at // 4) == lax.axis_index("yh")
    step = (at % 4 - lax.axis_index("x")) % 4
    kind = jnp.where(step == 0, 3, jnp.where(step == 1, 1, jnp.where(step == 2, 0, 2)))
    return (jnp.where(same, 4, 0) + kind).astype(jnp.int32)


def out_pairs(back):
    pairs = []
    for j in range(8):
        for b in range(2):
            for k in range(8):
                pairs.append(((2 * j + b) * 8 + k, (8 * b + k) * 8 + j))
    return [(t, s) for s, t in pairs] if back else pairs


def turn(v, cosine, sine_a, sine_b):
    return v * cosine + pltpu.roll(v, PAIR - HALF, 1) * sine_a + pltpu.roll(v, HALF, 1) * sine_b


def norm(x):
    center = x - jnp.mean(x, axis=1, keepdims=True)
    inverse = lax.rsqrt(jnp.mean(center * center, axis=1, keepdims=True) + norm_epsilon)
    return center * inverse, inverse


def piece_kernel(place_ref, out_ref, down_ref, piece_ref):
    piece_ref[:, 0:128] = out_ref[...]
    for m in range(4):
        piece_ref[:, 128 + 128 * m : 256 + 128 * m] = down_ref[64 * m : 64 * m + 64, :]


def spread(row, size, offset):
    n = row.shape[0]
    row = row.reshape(1, n)
    v = lax.broadcasted_iota(jnp.int32, (n, size), 0)
    t = lax.broadcasted_iota(jnp.int32, (n, size), 1)
    return dot(row, jnp.where(offset(t) == v, 1.0, 0.0).astype(bf16))


def shard_kernel(place_ref, q_ref, k_ref, v_ref, up_ref, gain_ref, lbias_ref, bqkv_ref, bout_ref, bup_ref, bdown_ref, shard_ref):
    j, i = place_ref[0], place_ref[1]
    shard_ref[:, 0:128] = q_ref[...]
    shard_ref[:, 128:256] = k_ref[...]
    shard_ref[:, 256:384] = v_ref[...]
    shard_ref[:, QKV:IN_COLS] = up_ref[...]
    rows = []
    for ref in (gain_ref, lbias_ref, bout_ref, bdown_ref):
        rows.append(spread(ref[...], D, lambda t: t - 64 * i))
    rows.append(spread(bqkv_ref[...], QKV, lambda t: (t // 128) * D + 128 * j + t % 128 - 192 * i))
    rows.append(spread(bup_ref[...], FFD, lambda t: t + FFD * j - 256 * i))
    row = jnp.concatenate(rows, axis=1)
    count = row.shape[1] // 128
    table = jnp.concatenate([row[:, 128 * r : 128 * r + 128] for r in range(count)] + [jnp.zeros((64 - count, 128), f32)], axis=0)
    shard_ref[:, IN_COLS:] = table.astype(bf16)


def assemble_kernel(g0, g1, g2, g3, g4, out_ref, turned_ref):
    for i in range(16):
        b, k = i // 8, i % 8
        rows = pl.ds(64 * i, 64)
        at = pl.ds(128 * k, 128)
        for m, g_ref in enumerate((g0, g1, g2, g3, g4)):
            row = FFD + 64 * b if m == 0 else 256 * b + 64 * (m - 1)
            out_ref[pl.ds(row, 64), at] = g_ref[rows, :]
    turned_ref[...] = out_ref[...].T


def token_blocks(refs):
    own, other, left, right, left3, right3, far0, far1 = refs
    return [
        ((far0, 0), (far1, 0)),
        ((right3, 0), (right3, 1)),
        ((left3, 0), (left3, 1)),
        ((other, 0), (other, 1)),
        ((left3, 2), (right3, 2)),
        ((right, 0), (right, 1)),
        ((left, 0), (left, 1)),
        ((own, 0), (own, 1)),
    ]


def grad_blocks(refs):
    own, other, left, right, far_own, far_other = refs
    return [
        ((far_other, 0), (far_other, 1)),
        ((right, 2), (right, 3)),
        ((left, 2), (left, 3)),
        ((other, 0), (other, 1)),
        ((far_own, 0), (far_own, 1)),
        ((right, 0), (right, 1)),
        ((left, 0), (left, 1)),
        ((own, 0), (own, 1)),
    ]


def load_pair(back_ref, blocks, hold_ref):
    for half in range(2):
        want = back_ref[2 * pl.program_id(0) + half]
        for block, pair in enumerate(blocks):

            @pl.when(want == block)
            def _(pair=pair):
                for s, (ref, row) in enumerate(pair):
                    hold_ref[256 * s + 128 * half : 256 * s + 128 * half + 128, :] = ref[row]


def project_kernel(back_ref, *refs):
    token_refs, refs = refs[:8], refs[8:]
    w_ref, vec_ref, cos_ref, sa_ref, sb_ref = refs[:5]
    hid_ref, qkv_ref, act_ref, dgelu_ref, small_ref, hold_ref = refs[5:]

    @pl.when(pl.program_id(0) == 0)
    def _():
        total = vec_ref[0:64, :].astype(f32)
        for i in range(1, 16):
            total = total + vec_ref[64 * i : 64 * i + 64, :].astype(f32)
        small_ref[...] = jnp.concatenate([total[r : r + 1, :] for r in range(39)], axis=1)

    load_pair(back_ref, token_blocks(token_refs), hold_ref)
    gain, lbias = small_ref[:, 0:D], small_ref[:, D : 2 * D]
    bias = small_ref[:, 4 * D :]
    cosine, sa, sb = cos_ref[...], sa_ref[...], sb_ref[...]
    for s in range(2):
        normed, _ = norm(hold_ref[256 * s : 256 * s + 256, :].astype(f32))
        hidden = (normed * gain + lbias).astype(bf16)
        proj = dot(hidden, w_ref[...]) + bias
        hid_ref[s] = hidden
        qkv_ref[s, :, 0:PAIR] = turn(proj[:, 0:PAIR], cosine, sa, sb).astype(bf16)
        qkv_ref[s, :, PAIR : 2 * PAIR] = turn(proj[:, PAIR : 2 * PAIR], cosine, sa, sb).astype(bf16)
        qkv_ref[s, :, 2 * PAIR : QKV] = proj[:, 2 * PAIR : QKV].astype(bf16)
        up = proj[:, QKV:]
        cdf = 0.5 * (1.0 + lax.erf(up * 0.7071067811865476))
        density = jnp.exp(-0.5 * up * up) * 0.3989422804014327
        act_ref[s] = (up * cdf).astype(bf16)
        dgelu_ref[s] = (cdf + up * density).astype(bf16)


def head_lanes(h):
    lane = lax.broadcasted_iota(jnp.int32, (1, PAIR), 1)
    return (lane < HEAD_DIM) if h == 0 else (lane >= HEAD_DIM)


def allowed_mask(seg_row_ref, seg_col_ref, b, keys):
    key_pos = lax.broadcasted_iota(jnp.int32, (keys, QB), 0)
    query_pos = lax.broadcasted_iota(jnp.int32, (keys, QB), 1) + b * QB
    same = seg_col_ref[0, 0:keys, :] == seg_row_ref[0, :, b * QB : (b + 1) * QB]
    return (key_pos <= query_pos) & same


def attend_kernel(qkv_ref, seg_row_ref, seg_col_ref, both_ref, att_ref, lse_ref):
    value_t = qkv_ref[:, 2 * PAIR : QKV].astype(f32).T.astype(bf16)
    for b in range(SEQ // QB):
        keys = (b + 1) * QB
        rows = slice(b * QB, (b + 1) * QB)
        allowed = allowed_mask(seg_row_ref, seg_col_ref, b, keys)
        query = qkv_ref[rows, 0:PAIR]
        mixed = []
        for h in range(2):
            q = jnp.where(head_lanes(h), query * 0.125, jnp.zeros_like(query))
            s = jnp.where(allowed, dot(qkv_ref[0:keys, PAIR : 2 * PAIR], q, NT), masked_score)
            top = jnp.max(s, axis=0, keepdims=True)
            e = jnp.exp(s - top)
            total = jnp.sum(e, axis=0, keepdims=True)
            p = (e * (1.0 / total)).astype(bf16)
            lse_ref[0, h : h + 1, rows] = top + jnp.log(total)
            mixed.append(dot(value_t[h * HEAD_DIM : (h + 1) * HEAD_DIM, 0:keys], p))
        att_ref[rows, :] = jnp.concatenate(mixed, axis=0).T.astype(bf16)


def attend_back_kernel(
    qkv_ref, da_ref, lse_ref, seg_row_ref, seg_col_ref, cos_ref, sa_ref, sb_ref, out_ref, sum_ref, dk_ref, dv_ref
):
    key_t = qkv_ref[:, PAIR : 2 * PAIR].astype(f32).T.astype(bf16)
    dk_ref[...] = jnp.zeros_like(dk_ref)
    dv_ref[...] = jnp.zeros_like(dv_ref)
    sums = jnp.zeros((1, PAIR), f32)
    for b in range(SEQ // QB):
        keys = (b + 1) * QB
        rows = slice(b * QB, (b + 1) * QB)
        allowed = allowed_mask(seg_row_ref, seg_col_ref, b, keys)
        query = qkv_ref[rows, 0:PAIR]
        grad = da_ref[rows, :]
        dq = []
        for h in range(2):
            q = jnp.where(head_lanes(h), query * 0.125, jnp.zeros_like(query))
            g = jnp.where(head_lanes(h), grad, jnp.zeros_like(grad))
            s = jnp.where(allowed, dot(qkv_ref[0:keys, PAIR : 2 * PAIR], q, NT), masked_score)
            soft = jnp.exp(s - lse_ref[0, h : h + 1, rows])
            dp = dot(qkv_ref[0:keys, 2 * PAIR : QKV], g, NT)
            t = soft * dp
            inner = jnp.sum(t, axis=0, keepdims=True)
            ds = (t - soft * inner).astype(bf16)
            dv_ref[0:keys, :] += dot(soft.astype(bf16), g)
            dk_ref[0:keys, :] += dot(ds, q)
            dq.append(dot(key_t[h * HEAD_DIM : (h + 1) * HEAD_DIM, 0:keys], ds))
        dq = jnp.concatenate(dq, axis=0).T * 0.125
        dq = turn(dq, cos_ref[rows, :], -sa_ref[rows, :], -sb_ref[rows, :]).astype(bf16)
        out_ref[rows, 0:PAIR] = dq
        sums += jnp.sum(dq.astype(f32), axis=0, keepdims=True)
    dk = turn(dk_ref[...], cos_ref[...], -sa_ref[...], -sb_ref[...]).astype(bf16)
    dv = dv_ref[...].astype(bf16)
    out_ref[:, PAIR : 2 * PAIR] = dk
    out_ref[:, 2 * PAIR : QKV] = dv
    sum_ref[0, :, 0:PAIR] = sums
    sum_ref[0, :, PAIR : 2 * PAIR] = jnp.sum(dk.astype(f32), axis=0, keepdims=True)
    sum_ref[0, :, 2 * PAIR : QKV] = jnp.sum(dv.astype(f32), axis=0, keepdims=True)


def mix_kernel(left_ref, w_ref, out_ref):
    part = dot(left_ref[...], w_ref[...]).astype(bf16)
    out_ref[:, 0] = part.reshape(4, 128, D)


def back_out_kernel(back_ref, *refs):
    grad_refs, refs = refs[:6], refs[6:]
    w_ref, dgelu_ref, da_ref, dup_ref, g_ref, sum_ref, hold_ref = refs

    @pl.when(pl.program_id(0) == 0)
    def _():
        sum_ref[...] = jnp.zeros_like(sum_ref)

    load_pair(back_ref, grad_blocks(grad_refs), hold_ref)
    g = hold_ref[...]
    r = dot(g, w_ref[...])
    for s in range(2):
        part = slice(256 * s, 256 * s + 256)
        g_ref[s] = g[part]
        da_ref[s] = r[part, FFD:].astype(bf16)
        dup = (r[part, 0:FFD] * dgelu_ref[s].astype(f32)).astype(bf16)
        dup_ref[s] = dup
        sum_ref[...] += jnp.sum(dup.astype(f32), axis=0, keepdims=True)


def back_in_kernel(back_ref, *refs):
    token_refs, refs = refs[:8], refs[8:]
    dqkv_ref, dup_ref, w_ref = refs[:3]
    to_right, to_left, *outs = refs[3:11]
    sum_ref, hold_ref = refs[11:]

    @pl.when(pl.program_id(0) == 0)
    def _():
        sum_ref[...] = jnp.zeros_like(sum_ref)

    load_pair(back_ref, token_blocks(token_refs), hold_ref)
    left = [jnp.concatenate([dqkv_ref[s], dup_ref[s]], axis=1) for s in range(2)]
    grad = dot(jnp.concatenate(left, axis=0), w_ref[...], NT)
    low = grad.astype(bf16)
    for half in range(2):
        at = back_ref[2 * pl.program_id(0) + half]
        parts = [low[256 * s + 128 * half : 256 * s + 128 * half + 128] for s in range(2)]
        for block in range(8):

            @pl.when(at == block)
            def _(block=block, parts=parts):
                group, kind = block // 4, block % 4
                if kind == 0:
                    to_right[group] = parts[0]
                    to_left[group] = parts[1]
                else:
                    ref = outs[3 * group + kind - 1]
                    for s in range(2):
                        ref[s] = parts[s]

    normed, _ = norm(hold_ref[...].astype(f32))
    sum_ref[0:1, :] += jnp.sum(grad * normed, axis=0, keepdims=True)
    sum_ref[1:2, :] += jnp.sum(grad, axis=0, keepdims=True)


def fold_kernel(a_ref, b_ref, r0, l0, r1, l1, r0o, l0o, r1o, l1o):
    for g, (r, l, ro, lo) in enumerate(((r0, l0, r0o, l0o), (r1, l1, r1o, l1o))):
        ro[0] = add(r[0], a_ref[g])
        lo[0] = add(l[0], b_ref[g])


def token_grad_kernel(x_ref, g_ref, c_ref, a_ref, b_ref, e_ref, gain_ref, out_ref):
    for s in range(2):
        grad = c_ref[s].astype(f32) + a_ref[s].astype(f32) + b_ref[s].astype(f32) + e_ref[s].astype(f32)
        normed, inverse = norm(x_ref[s].astype(f32))
        n = grad * gain_ref[...]
        inner = n - jnp.mean(n, axis=1, keepdims=True) - normed * jnp.mean(n * normed, axis=1, keepdims=True)
        out_ref[s] = (g_ref[s].astype(f32) + inverse * inner).astype(bf16)


def chunk_kernel(place_ref, mix_ref, up_ref, qkv_ref, vec_ref, mine_ref, other_ref):
    for c in range(2):

        @pl.when(place_ref[2] == c)
        def _(c=c):
            for i in range(16):
                ref, at = (mine_ref if i % 2 == c else other_ref), i // 2
                b, cols = i // 8, slice(128 * (i % 8), 128 * (i % 8) + 128)
                ref[at, :, 0:128] = mix_ref[FFD + 64 * b : FFD + 64 * b + 64, cols]
                for m in range(4):
                    row = 256 * b + 64 * m
                    ref[at, :, 128 + 128 * m : 256 + 128 * m] = mix_ref[row : row + 64, cols]
                ref[at, :, OUT_ROWS : OUT_ROWS + FFD] = up_ref[64 * i : 64 * i + 64, :]
                ref[at, :, OUT_ROWS + FFD : SHARD - 128] = qkv_ref[64 * i : 64 * i + 64, :]
                ref[at, :, SHARD - 128 :] = vec_ref[...]


def pair_sum_kernel(mine_ref, got_ref, out_ref):
    out_ref[...] = add(mine_ref[...], got_ref[...])


def owner_sum_kernel(got_ref, out_ref, rest_ref):
    total = got_ref[0].astype(f32)
    for k in range(1, 8):
        total = total + got_ref[k].astype(f32)
    out_ref[...] = total[:, 0:OUT_ROWS].astype(bf16)
    rest_ref[...] = total[:, OUT_ROWS:].astype(bf16)


def finish_kernel(place_ref, got_ref, qkv_ref, up_ref, out_ref, down_ref, gain_ref, lbias_ref, bqkv_ref, bout_ref, bdown_ref, bup_ref, vec_ref, bq_ref, bu_ref):
    i = place_ref[1]
    total = jnp.zeros((64, 128), f32)
    for k in range(8):
        at = slice(128 * k, 128 * k + 128)
        out_ref[:, at] = got_ref[k, :, 0:128].astype(f32)
        for m in range(4):
            down_ref[64 * m : 64 * m + 64, at] = got_ref[k, :, 128 + 128 * m : 256 + 128 * m].astype(f32)
        up_ref[:, FFD * k : FFD * k + FFD] = got_ref[k, :, OUT_ROWS : OUT_ROWS + FFD].astype(f32)
        for t in range(3):
            start = OUT_ROWS + FFD + 128 * t
            qkv_ref[:, D * t + 128 * k : D * t + 128 * k + 128] = got_ref[k, :, start : start + 128].astype(f32)
        last = got_ref[k, :, SHARD - 128 :].astype(f32)
        for t in range(3):
            bq_ref[8 * t + k : 8 * t + k + 1, :] = last[24 + t : 25 + t, :]
        bu_ref[4 * k : 4 * k + 4, :] = last[27:31, :]
        total = total + last
    vec_ref[...] = total
    odd = i % 2 == 1

    def lanes(row):
        return jnp.where(odd, pltpu.roll(row, 64, 1), row)

    for n, refs in enumerate(((gain_ref,), (lbias_ref,), (bout_ref, bdown_ref))):
        for ref in refs:
            ref[...] = lanes(vec_ref[pl.ds(8 * n + i // 2, 1), :])[:, 0:64]
    start = (3 * i) // 2
    first, second = bq_ref[pl.ds(start, 1), :], bq_ref[pl.ds(start + 1, 1), :]
    lane = lax.broadcasted_iota(jnp.int32, (1, 128), 1)
    turned0, turned1 = pltpu.roll(first, 64, 1), pltpu.roll(second, 64, 1)
    bqkv_ref[:, 0:128] = jnp.where(odd, jnp.where(lane < 64, turned0, turned1), first)
    bqkv_ref[:, 128:192] = jnp.where(odd, turned1, second)[:, 0:64]
    bup_ref[:, 0:128] = bu_ref[pl.ds(2 * i, 1), :]
    bup_ref[:, 128:256] = bu_ref[pl.ds(2 * i + 1, 1), :]


def shape(dims, dtype):
    return jax.ShapeDtypeStruct(dims, dtype)


def rotary_tables():
    frequency = np.float32(10000.0) ** (np.float32(-2.0) * np.arange(HALF, dtype=np.float32) / np.float32(ROTARY))
    angles = np.arange(SEQ, dtype=np.float32)[:, None] * frequency.astype(np.float32)[None, :]
    cosine, sine = np.cos(angles.astype(np.float64)), np.sin(angles.astype(np.float64))
    one = np.ones((SEQ, HEAD_DIM - ROTARY))
    zero = np.zeros((SEQ, HEAD_DIM - ROTARY))
    none = np.zeros((SEQ, HALF))
    cos = np.concatenate([cosine, cosine, one] * 2, axis=1)
    sine_a = np.concatenate([-sine, none, zero] * 2, axis=1)
    sine_b = np.concatenate([none, sine, zero] * 2, axis=1)
    return [jnp.asarray(t.astype(np.float32)) for t in (cos, sine_a, sine_b)]


def whole(dims):
    return pl.BlockSpec(dims, lambda i, *_: (0,) * len(dims), pipeline_mode=pl.Buffered(1))


def fixed(dims):
    return pl.BlockSpec(dims, lambda i, *_: (0,) * len(dims))


def body(tokens, segments, ln_gain, ln_bias, w_qkv, b_qkv, w_out, b_out, w_up, b_up, w_down, b_down, out_grad):
    j = lax.axis_index("yh") * 4 + lax.axis_index("x")
    i = lax.axis_index("z") * 4 + lax.axis_index("yl") * 2 + lax.axis_index("c")
    place = [j, i, lax.axis_index("c"), lax.axis_index("z"), lax.axis_index("yl")]
    place = jnp.stack(place).astype(jnp.int32)
    back = block_of()
    tokens_n = 2 * SEQ

    rows = lambda n, size=512: pl.BlockSpec((size, n), lambda i, *_: (i, 0))
    at_j = lambda dims, base=0: pl.BlockSpec(dims, lambda i, place: (0, base + place[0]))
    pairs = lambda n: pl.BlockSpec((2, 256, n), lambda i, *_: (0, i, 0))
    by_seq = lambda n: pl.BlockSpec((n, 1, 128, D), lambda i: (0, i, 0, 0))
    own_seq = pl.BlockSpec((1, 128, D), lambda i: (i, 0, 0))
    own_block = shape((2, 128, D), bf16)
    flat = lambda a: a.reshape(tokens_n, -1)
    line = lambda a: a

    shard = call(
        shard_kernel,
        "shard",
        (1,),
        [at_j((64, 128)), at_j((64, 128), 8), at_j((64, 128), 16), at_j((64, FFD))]
        + [whole((n,)) for n in (64, 64, 192, 64, 256, 64)],
        fixed((64, IN_COLS + 128)),
        shape((64, IN_COLS + 128), bf16),
        prefetch=1,
    )(place, w_qkv, w_qkv, w_qkv, w_up, *[line(a) for a in (ln_gain, ln_bias, b_qkv, b_out, b_up, b_down)])
    w_in = lax.all_gather(shard, ("z", "yl", "c"), axis=0, tiled=True)

    other = shift(tokens, "yh", 1)
    left = shift(tokens, "x", 1)
    right = shift(tokens, "x", -1)
    g_other = shift(after(out_grad, left, right, other), "yh", 1)
    left3 = shift(jnp.concatenate([other, left[0:1]]), "x", 1)
    right3 = shift(jnp.concatenate([other, right[1:2]]), "x", -1)
    piece = call(
        piece_kernel,
        "piece",
        (1,),
        [at_j((64, 128)), at_j((256, 128))],
        fixed((64, OUT_ROWS)),
        shape((64, OUT_ROWS), bf16),
        prefetch=1,
    )(place, w_out, w_down)
    piece = lax.ppermute(after(piece, left3, right3), ALL, out_pairs(False))
    far0 = shift(after(left3, g_other)[0:1], "x", 1)
    far1 = shift(after(right3, g_other)[1:2], "x", -1)
    token_refs = (tokens, other, left, right, left3, right3, far0, far1)
    token_specs = [whole(a.shape) for a in token_refs]
    pieces = lax.all_gather(after(piece, far0, far1), ("z", "yl", "c"), axis=0, tiled=True)

    g_both = after(jnp.concatenate([out_grad, g_other]), far0, far1)
    g_left = shift(g_both, "x", 1)
    g_right = shift(g_both, "x", -1)

    cos, sine_a, sine_b = rotary_tables()
    seg_row = segments[:, None, :]
    seg_col = segments[:, :, None]
    table = whole((SEQ, PAIR))

    hidden, qkv, activated, dgelu, small = call(
        project_kernel,
        "project",
        (4,),
        token_specs
        + [whole((D, IN_COLS)), pl.BlockSpec((D, 128), lambda i, *_: (0, 7))]
        + [pl.BlockSpec((256, PAIR), lambda i, *_: (i, 0))] * 3,
        [pairs(n) for n in (D, QKV, FFD, FFD)] + [fixed((1, 39 * 128))],
        [pltpu.HBM((2, SEQ, n), bf16) for n in (D, QKV, OUT_ROWS, FFD)] + [shape((1, 39 * 128), f32)],
        scratch=[pltpu.VMEM((512, D), bf16)],
        prefetch=1,
    )(back, *token_refs, w_in, w_in, cos, sine_a, sine_b)

    seg_row_spec = pl.BlockSpec((1, 1, SEQ), lambda i: (i, 0, 0))
    seg_col_spec = pl.BlockSpec((1, SEQ, 1), lambda i: (i, 0, 0))
    lse_spec = pl.BlockSpec((1, 2, SEQ), lambda i: (i, 0, 0))
    act_att, lse = call(
        attend_kernel,
        "attend",
        (2,),
        [rows(QKV, SEQ), seg_row_spec, seg_col_spec, pl.BlockSpec(memory_space=pl.ANY)],
        [pl.BlockSpec((SEQ, PAIR), lambda i: (i, FFD // PAIR)), lse_spec],
        [pltpu.HBM((tokens_n, OUT_ROWS), bf16), shape((2, 2, SEQ), f32)],
        alias={3: 0},
    )(flat(qkv), seg_row, seg_col, flat(activated))

    far_own, far_other = after(g_left, act_att)[0:2], after(g_right, act_att)[2:4]
    far_own, far_other = shift(far_own, "x", 1), shift(far_other, "x", -1)
    grad_refs = (out_grad, g_other, g_left, g_right, far_own, far_other)

    w_mix, w_mix_turned = call(
        assemble_kernel,
        "assemble",
        (1,),
        [pl.BlockSpec((D, 128), functools.partial(lambda m, i: (0, m), m)) for m in range(5)],
        [fixed((OUT_ROWS, D)), fixed((D, OUT_ROWS))],
        [shape((OUT_ROWS, D), bf16), shape((D, OUT_ROWS), bf16)],
    )(*[pieces] * 5)
    parts = call(
        mix_kernel,
        "mix",
        (4,),
        [rows(OUT_ROWS), whole((OUT_ROWS, D))],
        pl.BlockSpec((4, 1, 128, D), lambda i: (i % 2, i // 2, 0, 0)),
        pltpu.HBM((8, 2, 128, D), bf16),
    )(act_att, w_mix)
    summed = lax.psum_scatter(parts, ("yh", "x"), scatter_dimension=0, tiled=True)[0]
    mixed = tokens.astype(f32) + summed.astype(f32) + (small[0, 2 * D : 3 * D] + small[0, 3 * D : 4 * D])
    mixed = mixed.astype(bf16)
    grad_attended, grad_up, g_rows, up_sums = call(
        back_out_kernel,
        "back_out",
        (4,),
        [whole(a.shape) for a in grad_refs] + [whole((D, OUT_ROWS)), pairs(FFD)],
        [pairs(PAIR), pairs(FFD), pairs(D), fixed((1, FFD))],
        [shape((2, SEQ, n), bf16) for n in (PAIR, FFD)] + [pltpu.HBM((2, SEQ, D), bf16)] + [shape((1, FFD), f32)],
        scratch=[pltpu.VMEM((512, D), bf16)],
        prefetch=1,
    )(after(back, parts), *grad_refs, w_mix_turned, dgelu)

    grad_qkv, qkv_sums = call(
        attend_back_kernel,
        "attend_back",
        (2,),
        [rows(QKV, SEQ), rows(PAIR, SEQ), lse_spec, seg_row_spec, seg_col_spec, table, table, table],
        [rows(QKV, SEQ), pl.BlockSpec((1, 1, QKV), lambda i: (i, 0, 0))],
        [shape((tokens_n, QKV), bf16), shape((2, 1, QKV), f32)],
        scratch=[pltpu.VMEM((SEQ, PAIR), f32), pltpu.VMEM((SEQ, PAIR), f32)],
    )(flat(qkv), flat(grad_attended), lse, seg_row, seg_col, cos, sine_a, sine_b)

    block = shape((2, 128, D), bf16)
    *sent, ln_sums = call(
        back_in_kernel,
        "back_in",
        (4,),
        token_specs + [pairs(QKV), pairs(FFD), whole((D, IN_COLS))],
        [fixed((2, 128, D))] * 8 + [fixed((2, D))],
        [pltpu.HBM((2, 128, D), bf16)] * 8 + [shape((2, D), f32)],
        scratch=[pltpu.VMEM((512, D), bf16)],
        prefetch=1,
    )(back, *token_refs, grad_qkv.reshape(2, SEQ, QKV), grad_up, w_in)

    to_right, to_left, right0, left0, own0, right1, left1, own1 = sent
    a = shift(to_right, "x", 1)
    b = shift(to_left, "x", -1)
    first = pl.BlockSpec((1, 128, D), lambda i: (0, 0, 0))
    second = pl.BlockSpec((1, 128, D), lambda i: (1, 0, 0))
    right0, left0, right1, left1 = call(
        fold_kernel,
        "fold",
        (1,),
        [whole((2, 128, D))] * 2 + [first, second, first, second],
        [first, second, first, second],
        [block] * 4,
        alias={2: 0, 3: 1, 4: 2, 5: 3},
    )(a, b, right0, left0, right1, left1)
    from_left0 = shift(right0, "x", 1)
    from_right0 = shift(left0, "x", -1)
    from_left1 = shift(right1, "x", 1)
    from_right1 = shift(left1, "x", -1)
    total = own0.astype(f32) + from_left0.astype(f32) + from_right0.astype(f32)
    from_other = shift(total.astype(bf16), "yh", 1)
    grad_tokens = call(
        token_grad_kernel,
        "token_grad",
        (1,),
        [whole((2, 128, D))] * 6 + [pl.BlockSpec((1, D), lambda i: (0, 0))],
        fixed((2, 128, D)),
        block,
    )(tokens, out_grad, own1, from_left1, from_right1, from_other, small)

    g_rows = after(flat(g_rows), to_right)
    hidden = after(flat(hidden), to_right)
    grad_mix = dot(act_att, g_rows, TN).astype(bf16)
    grad_w_up = dot(hidden, flat(grad_up), TN).astype(bf16)
    grad_w_qkv = dot(hidden, grad_qkv, TN).astype(bf16)
    g_sum = jnp.sum(out_grad.astype(f32), axis=(0, 1))
    vec = [ln_sums.reshape(16, 128), g_sum.reshape(8, 128), jnp.sum(qkv_sums, axis=0).reshape(3, 128), up_sums.reshape(4, 128)]
    vec = jnp.pad(jnp.concatenate(vec).astype(bf16), ((0, 33), (0, 0)))
    halves = shape((8, 64, SHARD), bf16)
    own_half, other_half = call(
        chunk_kernel,
        "chunk",
        (1,),
        [whole((OUT_ROWS, D)), whole((D, FFD)), whole((D, QKV)), whole((64, 128))],
        [fixed(halves.shape)] * 2,
        [halves] * 2,
        prefetch=1,
    )(place, after(grad_mix, a, b), grad_w_up, grad_w_qkv, vec)
    got = shift(other_half, "c", 1)
    quarter = pl.BlockSpec((2, 64, SHARD), lambda i: (i, 0, 0))
    chip_half = call(pair_sum_kernel, "pair_sum", (4,), [quarter] * 2, quarter, halves)(own_half, got)
    got = lax.all_to_all(after(chip_half, right0, left0), ("z", "yl"), 0, 0, tiled=True)
    out_owned, rest_owned = call(
        owner_sum_kernel,
        "owner_sum",
        (1,),
        [whole(halves.shape)],
        [fixed((64, OUT_ROWS)), fixed((64, SHARD - OUT_ROWS))],
        [shape((64, OUT_ROWS), bf16), shape((64, SHARD - OUT_ROWS), bf16)],
    )(got)
    out_owned = lax.ppermute(out_owned, ALL, out_pairs(True))

    def spread_ctx(a):
        return lax.all_to_all(jnp.broadcast_to(a[None], (8,) + a.shape), ("yh", "x"), 0, 0, tiled=True)

    both = spread_ctx(after(jnp.concatenate([out_owned, rest_owned], axis=1), from_left1, from_right1, from_other))
    sizes = [(64, 3 * D), (64, 4 * D), (64, D), (256, D), (1, 64), (1, 64), (1, 192), (1, 64), (1, 64), (1, 256)]
    done = call(
        finish_kernel,
        "finish",
        (1,),
        [fixed((8, 64, SHARD))],
        [fixed(dims) for dims in sizes],
        [shape(dims, f32) for dims in sizes],
        scratch=[pltpu.VMEM((64, 128), f32), pltpu.VMEM((32, 128), f32), pltpu.VMEM((32, 128), f32)],
        prefetch=1,
    )(place, after(both, mixed))
    grad_w_qkv, grad_w_up, grad_w_out, grad_w_down = done[:4]
    grad_gain, grad_lbias, grad_bqkv, grad_bout, grad_bdown, grad_bup = [a.reshape(-1) for a in done[4:]]
    return (
        mixed,
        grad_tokens,
        grad_gain,
        grad_lbias,
        grad_w_qkv,
        grad_bqkv,
        grad_w_out,
        grad_bout,
        grad_w_up,
        grad_bup,
        grad_w_down,
        grad_bdown,
    )


def solution(mesh):
    fine = Mesh(mesh.devices.reshape(4, 2, 2, 2, 4), ALL)
    dp = ("z", "yl", "c")
    ctx = ("yh", "x")
    in_specs = (
        P(dp, ctx, None),
        P(dp, None),
        P(dp),
        P(dp),
        P(dp, None),
        P(dp),
        P(dp, None),
        P(dp),
        P(dp, None),
        P(dp),
        P(dp, None),
        P(dp),
        P(dp, ctx, None),
    )
    out_specs = (
        P(dp, ctx, None),
        P(dp, ctx, None),
        P(dp),
        P(dp),
        P(dp, None),
        P(dp),
        P(dp, None),
        P(dp),
        P(dp, None),
        P(dp),
        P(dp, None),
        P(dp),
    )
    return jax.shard_map(body, mesh=fine, in_specs=in_specs, out_specs=out_specs, check_vma=False)
```

```python
import functools

import jax
import jax.numpy as jnp
import numpy as np
from jax import lax
from jax.experimental import pallas as pl
from jax.experimental.pallas import tpu as pltpu
from jax.sharding import Mesh
from jax.sharding import PartitionSpec as P

HEAD_DIM = 64
ROTARY = 32
HALF = ROTARY // 2
SEQ = 1024
D = 1024
PAIR = 128
FFD = 512
QKV = 3 * PAIR
IN_COLS = QKV + FFD
OUT_ROWS = PAIR + FFD
QB = 256

norm_epsilon = 1e-05
masked_score = -1e30
f32 = jnp.float32
bf16 = jnp.bfloat16
NT = (((1,), (1,)), ((), ()))
NN = (((1,), (0,)), ((), ()))
VMEM_LIMIT = 30 * 1024 * 1024
MIB = dict(shard=60, piece=60, project=60, attend=52, assemble=16, mix=16, back_out=60, attend_back=20, back_in=20, chunk=16, fold=16, pair_sum=16, owner_sum=16, finish=16, token_grad=16)
TN = (((0,), (0,)), ((), ()))
SHARD = IN_COLS + OUT_ROWS + 128
SCALE = 0.3
COST = dict(shard=2, piece=1, project=13, attend=11, assemble=3, mix=6, back_out=9, attend_back=13, back_in=14, fold=2, token_grad=3, chunk=4, pair_sum=3, owner_sum=2, finish=3)


def dot(a, b, dims=NN):
    return lax.dot_general(a, b, dims, preferred_element_type=f32)


def call(kernel, name, grid, in_specs, out_specs, out_shape, scratch=(), prefetch=0, alias=None):
    return pl.pallas_call(
        kernel,
        name=name,
        grid_spec=pltpu.PrefetchScalarGridSpec(
            num_scalar_prefetch=prefetch,
            grid=grid,
            in_specs=in_specs,
            out_specs=out_specs,
            scratch_shapes=scratch,
        ),
        out_shape=out_shape,
        input_output_aliases=alias or {},
        compiler_params=pltpu.CompilerParams(
            dimension_semantics=("arbitrary",) * len(grid), vmem_limit_bytes=int(MIB.get(name, 52) * 1024 * 1024)
        ),
        cost_estimate=pl.CostEstimate(flops=int(COST.get(name, 1) * 1e9 * SCALE), bytes_accessed=int(COST.get(name, 1) * 1000000 * SCALE), transcendentals=0),
    )


ALL = ("z", "yl", "c", "yh", "x")


def shift(x, axis, by):
    count = lax.axis_size(axis)
    return lax.ppermute(x, axis, [(i, (i + by) % count) for i in range(count)])


def after(x, *others):
    return lax.optimization_barrier((x,) + others)[0]


def add(a, b):
    return (a.astype(f32) + b.astype(f32)).astype(bf16)


def block_of():
    at = jnp.arange(8, dtype=jnp.int32)
    same = (at // 4) == lax.axis_index("yh")
    step = (at % 4 - lax.axis_index("x")) % 4
    kind = jnp.where(step == 0, 3, jnp.where(step == 1, 1, jnp.where(step == 2, 0, 2)))
    return (jnp.where(same, 4, 0) + kind).astype(jnp.int32)


def out_pairs(back):
    pairs = []
    for j in range(8):
        for b in range(2):
            for k in range(8):
                pairs.append(((2 * j + b) * 8 + k, (8 * b + k) * 8 + j))
    return [(t, s) for s, t in pairs] if back else pairs


def turn(v, cosine, sine):
    lane = lax.broadcasted_iota(jnp.int32, (1, PAIR), 1) % HEAD_DIM
    crossed = jnp.where(lane < HALF, -pltpu.roll(v, PAIR - HALF, 1), pltpu.roll(v, HALF, 1))
    return v * cosine + crossed * sine


def norm(x):
    center = x - jnp.mean(x, axis=1, keepdims=True)
    inverse = lax.rsqrt(jnp.mean(center * center, axis=1, keepdims=True) + norm_epsilon)
    return center * inverse, inverse


def piece_kernel(place_ref, out_ref, down_ref, piece_ref):
    piece_ref[:, 0:128] = out_ref[...]
    for m in range(4):
        piece_ref[:, 128 + 128 * m : 256 + 128 * m] = down_ref[64 * m : 64 * m + 64, :]


def spread(row, size, offset):
    n = row.shape[0]
    row = row.reshape(1, n)
    v = lax.broadcasted_iota(jnp.int32, (n, size), 0)
    t = lax.broadcasted_iota(jnp.int32, (n, size), 1)
    return dot(row, jnp.where(offset(t) == v, 1.0, 0.0).astype(bf16))


def shard_kernel(place_ref, q_ref, k_ref, v_ref, up_ref, piece_ref, gain_ref, lbias_ref, bqkv_ref, bout_ref, bup_ref, bdown_ref, shard_ref):
    j, i = place_ref[0], place_ref[1]
    shard_ref[:, 0:128] = q_ref[...]
    shard_ref[:, 128:256] = k_ref[...]
    shard_ref[:, 256:384] = v_ref[...]
    shard_ref[:, QKV:IN_COLS] = up_ref[...]
    shard_ref[:, IN_COLS : IN_COLS + OUT_ROWS] = piece_ref[...]
    rows = []
    for ref in (gain_ref, lbias_ref, bout_ref, bdown_ref):
        rows.append(spread(ref[...], D, lambda t: t - 64 * i))
    rows.append(spread(bqkv_ref[...], QKV, lambda t: (t // 128) * D + 128 * j + t % 128 - 192 * i))
    rows.append(spread(bup_ref[...], FFD, lambda t: t + FFD * j - 256 * i))
    row = jnp.concatenate(rows, axis=1)
    count = row.shape[1] // 128
    table = jnp.concatenate([row[:, 128 * r : 128 * r + 128] for r in range(count)] + [jnp.zeros((64 - count, 128), f32)], axis=0)
    shard_ref[:, IN_COLS + OUT_ROWS :] = table.astype(bf16)


def assemble_kernel(g0, g1, g2, g3, g4, out_ref, turned_ref):
    for i in range(16):
        b, k = i // 8, i % 8
        rows = pl.ds(64 * i, 64)
        at = pl.ds(128 * k, 128)
        for m, g_ref in enumerate((g0, g1, g2, g3, g4)):
            row = FFD + 64 * b if m == 0 else 256 * b + 64 * (m - 1)
            out_ref[pl.ds(row, 64), at] = g_ref[rows, :]
    turned_ref[...] = out_ref[...].T


def token_blocks(refs):
    own, other, left, right, left3, right3, far0, far1 = refs
    return [
        ((far0, 0), (far1, 0)),
        ((right3, 0), (right3, 1)),
        ((left3, 0), (left3, 1)),
        ((other, 0), (other, 1)),
        ((left3, 2), (right3, 2)),
        ((right, 0), (right, 1)),
        ((left, 0), (left, 1)),
        ((own, 0), (own, 1)),
    ]


def grad_blocks(refs):
    own, other, left, right, far_own, far_other = refs
    return [
        ((far_other, 0), (far_other, 1)),
        ((right, 2), (right, 3)),
        ((left, 2), (left, 3)),
        ((other, 0), (other, 1)),
        ((far_own, 0), (far_own, 1)),
        ((right, 0), (right, 1)),
        ((left, 0), (left, 1)),
        ((own, 0), (own, 1)),
    ]


def load_pair(back_ref, blocks, hold_ref):
    for half in range(2):
        want = back_ref[2 * pl.program_id(0) + half]
        for block, pair in enumerate(blocks):

            @pl.when(want == block)
            def _(pair=pair):
                for s, (ref, row) in enumerate(pair):
                    hold_ref[256 * s + 128 * half : 256 * s + 128 * half + 128, :] = ref[row]


def project_kernel(back_ref, *refs):
    token_refs, refs = refs[:8], refs[8:]
    w_ref, vec_ref, cos_ref, sin_ref = refs[:4]
    hid_ref, qkv_ref, act_ref, dgelu_ref, small_ref, hold_ref = refs[4:]

    @pl.when(pl.program_id(0) == 0)
    def _():
        total = vec_ref[0:64, :].astype(f32)
        for i in range(1, 16):
            total = total + vec_ref[64 * i : 64 * i + 64, :].astype(f32)
        small_ref[...] = jnp.concatenate([total[r : r + 1, :] for r in range(39)], axis=1)

    load_pair(back_ref, token_blocks(token_refs), hold_ref)
    gain, lbias = small_ref[:, 0:D], small_ref[:, D : 2 * D]
    bias = small_ref[:, 4 * D :]
    cosine, sine = cos_ref[...], sin_ref[...]
    for s in range(2):
        normed, _ = norm(hold_ref[256 * s : 256 * s + 256, :].astype(f32))
        hidden = (normed * gain + lbias).astype(bf16)
        proj = dot(hidden, w_ref[...]) + bias
        hid_ref[s] = hidden
        qkv_ref[s, :, 0:PAIR] = turn(proj[:, 0:PAIR], cosine, sine).astype(bf16)
        qkv_ref[s, :, PAIR : 2 * PAIR] = turn(proj[:, PAIR : 2 * PAIR], cosine, sine).astype(bf16)
        qkv_ref[s, :, 2 * PAIR : QKV] = proj[:, 2 * PAIR : QKV].astype(bf16)
        up = proj[:, QKV:]
        cdf = 0.5 * (1.0 + lax.erf(up * 0.7071067811865476))
        density = jnp.exp(-0.5 * up * up) * 0.3989422804014327
        act_ref[s] = (up * cdf).astype(bf16)
        dgelu_ref[s] = (cdf + up * density).astype(bf16)


def head_lanes(h):
    lane = lax.broadcasted_iota(jnp.int32, (1, PAIR), 1)
    return (lane < HEAD_DIM) if h == 0 else (lane >= HEAD_DIM)


def allowed_mask(seg_row_ref, seg_col_ref, b, keys):
    key_pos = lax.broadcasted_iota(jnp.int32, (keys, QB), 0)
    query_pos = lax.broadcasted_iota(jnp.int32, (keys, QB), 1) + b * QB
    same = seg_col_ref[0, 0:keys, :] == seg_row_ref[0, :, b * QB : (b + 1) * QB]
    return (key_pos <= query_pos) & same


def attend_kernel(qkv_ref, seg_row_ref, seg_col_ref, both_ref, att_ref, lse_ref):
    value_t = qkv_ref[:, 2 * PAIR : QKV].astype(f32).T.astype(bf16)
    for b in range(SEQ // QB):
        keys = (b + 1) * QB
        rows = slice(b * QB, (b + 1) * QB)
        allowed = allowed_mask(seg_row_ref, seg_col_ref, b, keys)
        query = qkv_ref[rows, 0:PAIR]
        mixed = []
        for h in range(2):
            q = jnp.where(head_lanes(h), query * 0.125, jnp.zeros_like(query))
            s = jnp.where(allowed, dot(qkv_ref[0:keys, PAIR : 2 * PAIR], q, NT), masked_score)
            top = jnp.max(s, axis=0, keepdims=True)
            e = jnp.exp(s - top)
            total = jnp.sum(e, axis=0, keepdims=True)
            p = (e * (1.0 / total)).astype(bf16)
            lse_ref[0, h : h + 1, rows] = top + jnp.log(total)
            mixed.append(dot(value_t[h * HEAD_DIM : (h + 1) * HEAD_DIM, 0:keys], p))
        att_ref[rows, :] = jnp.concatenate(mixed, axis=0).T.astype(bf16)


def attend_back_kernel(
    qkv_ref, da_ref, lse_ref, seg_row_ref, seg_col_ref, cos_ref, sin_ref, out_ref, sum_ref, dk_ref, dv_ref
):
    key_t = qkv_ref[:, PAIR : 2 * PAIR].astype(f32).T.astype(bf16)
    dk_ref[...] = jnp.zeros_like(dk_ref)
    dv_ref[...] = jnp.zeros_like(dv_ref)
    sums = jnp.zeros((1, PAIR), f32)
    for b in range(SEQ // QB):
        keys = (b + 1) * QB
        rows = slice(b * QB, (b + 1) * QB)
        allowed = allowed_mask(seg_row_ref, seg_col_ref, b, keys)
        query = qkv_ref[rows, 0:PAIR]
        grad = da_ref[rows, :]
        dq = []
        for h in range(2):
            q = jnp.where(head_lanes(h), query * 0.125, jnp.zeros_like(query))
            g = jnp.where(head_lanes(h), grad, jnp.zeros_like(grad))
            s = jnp.where(allowed, dot(qkv_ref[0:keys, PAIR : 2 * PAIR], q, NT), masked_score)
            soft = jnp.exp(s - lse_ref[0, h : h + 1, rows])
            dp = dot(qkv_ref[0:keys, 2 * PAIR : QKV], g, NT)
            t = soft * dp
            inner = jnp.sum(t, axis=0, keepdims=True)
            ds = (t - soft * inner).astype(bf16)
            dv_ref[0:keys, :] += dot(soft.astype(bf16), g)
            dk_ref[0:keys, :] += dot(ds, q)
            dq.append(dot(key_t[h * HEAD_DIM : (h + 1) * HEAD_DIM, 0:keys], ds))
        dq = jnp.concatenate(dq, axis=0).T * 0.125
        dq = turn(dq, cos_ref[rows, :], -sin_ref[rows, :]).astype(bf16)
        out_ref[rows, 0:PAIR] = dq
        sums += jnp.sum(dq.astype(f32), axis=0, keepdims=True)
    dk = turn(dk_ref[...], cos_ref[...], -sin_ref[...]).astype(bf16)
    dv = dv_ref[...].astype(bf16)
    out_ref[:, PAIR : 2 * PAIR] = dk
    out_ref[:, 2 * PAIR : QKV] = dv
    sum_ref[0, :, 0:PAIR] = sums
    sum_ref[0, :, PAIR : 2 * PAIR] = jnp.sum(dk.astype(f32), axis=0, keepdims=True)
    sum_ref[0, :, 2 * PAIR : QKV] = jnp.sum(dv.astype(f32), axis=0, keepdims=True)


def mix_kernel(left_ref, w_ref, out_ref):
    part = dot(left_ref[...], w_ref[...]).astype(bf16)
    out_ref[:, 0] = part.reshape(4, 128, D)


def back_out_kernel(back_ref, *refs):
    grad_refs, refs = refs[:6], refs[6:]
    w_ref, dgelu_ref, da_ref, dup_ref, g_ref, sum_ref, hold_ref = refs

    @pl.when(pl.program_id(0) == 0)
    def _():
        sum_ref[...] = jnp.zeros_like(sum_ref)

    load_pair(back_ref, grad_blocks(grad_refs), hold_ref)
    g = hold_ref[...]
    r = dot(g, w_ref[...])
    for s in range(2):
        part = slice(256 * s, 256 * s + 256)
        g_ref[s] = g[part]
        da_ref[s] = r[part, FFD:].astype(bf16)
        dup = (r[part, 0:FFD] * dgelu_ref[s].astype(f32)).astype(bf16)
        dup_ref[s] = dup
        sum_ref[...] += jnp.sum(dup.astype(f32), axis=0, keepdims=True)


def back_in_kernel(back_ref, *refs):
    token_refs, refs = refs[:8], refs[8:]
    dqkv_ref, dup_ref, w_ref = refs[:3]
    to_right, to_left, *outs = refs[3:11]
    sum_ref, hold_ref = refs[11:]

    @pl.when(pl.program_id(0) == 0)
    def _():
        sum_ref[...] = jnp.zeros_like(sum_ref)

    load_pair(back_ref, token_blocks(token_refs), hold_ref)
    left = [jnp.concatenate([dqkv_ref[s], dup_ref[s]], axis=1) for s in range(2)]
    grad = dot(jnp.concatenate(left, axis=0), w_ref[...], NT)
    low = grad.astype(bf16)
    for half in range(2):
        at = back_ref[2 * pl.program_id(0) + half]
        parts = [low[256 * s + 128 * half : 256 * s + 128 * half + 128] for s in range(2)]
        for block in range(8):

            @pl.when(at == block)
            def _(block=block, parts=parts):
                group, kind = block // 4, block % 4
                if kind == 0:
                    to_right[group] = parts[0]
                    to_left[group] = parts[1]
                else:
                    ref = outs[3 * group + kind - 1]
                    for s in range(2):
                        ref[s] = parts[s]

    normed, _ = norm(hold_ref[...].astype(f32))
    sum_ref[0:1, :] += jnp.sum(grad * normed, axis=0, keepdims=True)
    sum_ref[1:2, :] += jnp.sum(grad, axis=0, keepdims=True)


def fold_kernel(a_ref, b_ref, r0, l0, r1, l1, r0o, l0o, r1o, l1o):
    for g, (r, l, ro, lo) in enumerate(((r0, l0, r0o, l0o), (r1, l1, r1o, l1o))):
        ro[0] = add(r[0], a_ref[g])
        lo[0] = add(l[0], b_ref[g])


def token_grad_kernel(x_ref, g_ref, c_ref, a_ref, b_ref, e_ref, gain_ref, out_ref):
    for s in range(2):
        grad = c_ref[s].astype(f32) + a_ref[s].astype(f32) + b_ref[s].astype(f32) + e_ref[s].astype(f32)
        normed, inverse = norm(x_ref[s].astype(f32))
        n = grad * gain_ref[...]
        inner = n - jnp.mean(n, axis=1, keepdims=True) - normed * jnp.mean(n * normed, axis=1, keepdims=True)
        out_ref[s] = (g_ref[s].astype(f32) + inverse * inner).astype(bf16)


def chunk_kernel(place_ref, mix_ref, up_ref, qkv_ref, vec_ref, mine_ref, other_ref):
    for c in range(2):

        @pl.when(place_ref[2] == c)
        def _(c=c):
            for i in range(16):
                ref, at = (mine_ref if i % 2 == c else other_ref), i // 2
                b, cols = i // 8, slice(128 * (i % 8), 128 * (i % 8) + 128)
                ref[at, :, 0:128] = mix_ref[FFD + 64 * b : FFD + 64 * b + 64, cols]
                for m in range(4):
                    row = 256 * b + 64 * m
                    ref[at, :, 128 + 128 * m : 256 + 128 * m] = mix_ref[row : row + 64, cols]
                ref[at, :, OUT_ROWS : OUT_ROWS + FFD] = up_ref[64 * i : 64 * i + 64, :]
                ref[at, :, OUT_ROWS + FFD : SHARD - 128] = qkv_ref[64 * i : 64 * i + 64, :]
                ref[at, :, SHARD - 128 :] = vec_ref[...]


def pair_sum_kernel(mine_ref, got_ref, out_ref):
    out_ref[...] = add(mine_ref[...], got_ref[...])


def owner_sum_kernel(got_ref, out_ref, rest_ref):
    total = got_ref[0].astype(f32)
    for k in range(1, 8):
        total = total + got_ref[k].astype(f32)
    out_ref[...] = total[:, 0:OUT_ROWS].astype(bf16)
    rest_ref[...] = total[:, OUT_ROWS:].astype(bf16)


def finish_kernel(place_ref, got_ref, qkv_ref, up_ref, out_ref, down_ref, gain_ref, lbias_ref, bqkv_ref, bout_ref, bdown_ref, bup_ref, vec_ref, bq_ref, bu_ref):
    i = place_ref[1]
    total = jnp.zeros((64, 128), f32)
    for k in range(8):
        at = slice(128 * k, 128 * k + 128)
        out_ref[:, at] = got_ref[k, :, 0:128].astype(f32)
        for m in range(4):
            down_ref[64 * m : 64 * m + 64, at] = got_ref[k, :, 128 + 128 * m : 256 + 128 * m].astype(f32)
        up_ref[:, FFD * k : FFD * k + FFD] = got_ref[k, :, OUT_ROWS : OUT_ROWS + FFD].astype(f32)
        for t in range(3):
            start = OUT_ROWS + FFD + 128 * t
            qkv_ref[:, D * t + 128 * k : D * t + 128 * k + 128] = got_ref[k, :, start : start + 128].astype(f32)
        last = got_ref[k, :, SHARD - 128 :].astype(f32)
        for t in range(3):
            bq_ref[8 * t + k : 8 * t + k + 1, :] = last[24 + t : 25 + t, :]
        bu_ref[4 * k : 4 * k + 4, :] = last[27:31, :]
        total = total + last
    vec_ref[...] = total
    odd = i % 2 == 1

    def lanes(row):
        return jnp.where(odd, pltpu.roll(row, 64, 1), row)

    for n, refs in enumerate(((gain_ref,), (lbias_ref,), (bout_ref, bdown_ref))):
        for ref in refs:
            ref[...] = lanes(vec_ref[pl.ds(8 * n + i // 2, 1), :])[:, 0:64]
    start = (3 * i) // 2
    first, second = bq_ref[pl.ds(start, 1), :], bq_ref[pl.ds(start + 1, 1), :]
    lane = lax.broadcasted_iota(jnp.int32, (1, 128), 1)
    turned0, turned1 = pltpu.roll(first, 64, 1), pltpu.roll(second, 64, 1)
    bqkv_ref[:, 0:128] = jnp.where(odd, jnp.where(lane < 64, turned0, turned1), first)
    bqkv_ref[:, 128:192] = jnp.where(odd, turned1, second)[:, 0:64]
    bup_ref[:, 0:128] = bu_ref[pl.ds(2 * i, 1), :]
    bup_ref[:, 128:256] = bu_ref[pl.ds(2 * i + 1, 1), :]


def shape(dims, dtype):
    return jax.ShapeDtypeStruct(dims, dtype)


def rotary_tables():
    frequency = np.float32(10000.0) ** (np.float32(-2.0) * np.arange(HALF, dtype=np.float32) / np.float32(ROTARY))
    angles = np.arange(SEQ, dtype=np.float32)[:, None] * frequency.astype(np.float32)[None, :]
    cosine, sine = np.cos(angles.astype(np.float64)), np.sin(angles.astype(np.float64))
    one = np.ones((SEQ, HEAD_DIM - ROTARY))
    zero = np.zeros((SEQ, HEAD_DIM - ROTARY))
    cos = np.concatenate([cosine, cosine, one] * 2, axis=1)
    sin = np.concatenate([sine, sine, zero] * 2, axis=1)
    return [jnp.asarray(t.astype(np.float32)) for t in (cos, sin)]


def whole(dims):
    return pl.BlockSpec(dims, lambda i, *_: (0,) * len(dims), pipeline_mode=pl.Buffered(1))


def fixed(dims):
    return pl.BlockSpec(dims, lambda i, *_: (0,) * len(dims))


def body(tokens, segments, ln_gain, ln_bias, w_qkv, b_qkv, w_out, b_out, w_up, b_up, w_down, b_down, out_grad):
    j = lax.axis_index("yh") * 4 + lax.axis_index("x")
    i = lax.axis_index("z") * 4 + lax.axis_index("yl") * 2 + lax.axis_index("c")
    place = [j, i, lax.axis_index("c"), lax.axis_index("z"), lax.axis_index("yl")]
    place = jnp.stack(place).astype(jnp.int32)
    back = block_of()
    tokens_n = 2 * SEQ

    rows = lambda n, size=512: pl.BlockSpec((size, n), lambda i, *_: (i, 0))
    at_j = lambda dims, base=0: pl.BlockSpec(dims, lambda i, place: (0, base + place[0]))
    pairs = lambda n: pl.BlockSpec((2, 256, n), lambda i, *_: (0, i, 0))
    by_seq = lambda n: pl.BlockSpec((n, 1, 128, D), lambda i: (0, i, 0, 0))
    own_seq = pl.BlockSpec((1, 128, D), lambda i: (i, 0, 0))
    own_block = shape((2, 128, D), bf16)
    flat = lambda a: a.reshape(tokens_n, -1)
    line = lambda a: a

    other = shift(tokens, "yh", 1)
    left = shift(tokens, "x", 1)
    right = shift(tokens, "x", -1)
    piece = call(
        piece_kernel,
        "piece",
        (1,),
        [at_j((64, 128)), at_j((256, 128))],
        fixed((64, OUT_ROWS)),
        shape((64, OUT_ROWS), bf16),
        prefetch=1,
    )(place, w_out, w_down)
    piece = lax.ppermute(piece, ALL, out_pairs(False))
    shard = call(
        shard_kernel,
        "shard",
        (1,),
        [at_j((64, 128)), at_j((64, 128), 8), at_j((64, 128), 16), at_j((64, FFD)), whole((64, OUT_ROWS))]
        + [whole((n,)) for n in (64, 64, 192, 64, 256, 64)],
        fixed((64, SHARD)),
        shape((64, SHARD), bf16),
        prefetch=1,
    )(place, w_qkv, w_qkv, w_qkv, w_up, after(piece, left, right, other), *[line(a) for a in (ln_gain, ln_bias, b_qkv, b_out, b_up, b_down)])
    w_all = lax.all_gather(shard, ("z", "yl", "c"), axis=0, tiled=True)

    g_other = shift(after(out_grad, left, right, other), "yh", 1)
    left3 = shift(jnp.concatenate([other, left[0:1]]), "x", 1)
    right3 = shift(jnp.concatenate([other, right[1:2]]), "x", -1)
    far0 = shift(after(left3, g_other)[0:1], "x", 1)
    far1 = shift(after(right3, g_other)[1:2], "x", -1)
    token_refs = (tokens, other, left, right, left3, right3, far0, far1)
    token_specs = [whole(a.shape) for a in token_refs]


    g_both = after(jnp.concatenate([out_grad, g_other]), far0, far1)
    g_left = shift(g_both, "x", 1)
    g_right = shift(g_both, "x", -1)

    cos, sin = rotary_tables()
    seg_row = segments[:, None, :]
    seg_col = segments[:, :, None]
    table = whole((SEQ, PAIR))

    hidden, qkv, activated, dgelu, small = call(
        project_kernel,
        "project",
        (4,),
        token_specs
        + [whole((D, IN_COLS)), pl.BlockSpec((D, 128), lambda i, *_: (0, 12))]
        + [pl.BlockSpec((256, PAIR), lambda i, *_: (i, 0))] * 2,
        [pairs(n) for n in (D, QKV, FFD, FFD)] + [fixed((1, 39 * 128))],
        [pltpu.HBM((2, SEQ, n), bf16) for n in (D, QKV, OUT_ROWS, FFD)] + [shape((1, 39 * 128), f32)],
        scratch=[pltpu.VMEM((512, D), bf16)],
        prefetch=1,
    )(back, *token_refs, w_all, w_all, cos, sin)

    seg_row_spec = pl.BlockSpec((1, 1, SEQ), lambda i: (i, 0, 0))
    seg_col_spec = pl.BlockSpec((1, SEQ, 1), lambda i: (i, 0, 0))
    lse_spec = pl.BlockSpec((1, 2, SEQ), lambda i: (i, 0, 0))
    act_att, lse = call(
        attend_kernel,
        "attend",
        (2,),
        [rows(QKV, SEQ), seg_row_spec, seg_col_spec, pl.BlockSpec(memory_space=pl.ANY)],
        [pl.BlockSpec((SEQ, PAIR), lambda i: (i, FFD // PAIR)), lse_spec],
        [pltpu.HBM((tokens_n, OUT_ROWS), bf16), shape((2, 2, SEQ), f32)],
        alias={3: 0},
    )(flat(qkv), seg_row, seg_col, flat(activated))

    far_own, far_other = after(g_left, act_att)[0:2], after(g_right, act_att)[2:4]
    far_own, far_other = shift(far_own, "x", 1), shift(far_other, "x", -1)
    grad_refs = (out_grad, g_other, g_left, g_right, far_own, far_other)

    w_mix, w_mix_turned = call(
        assemble_kernel,
        "assemble",
        (1,),
        [pl.BlockSpec((D, 128), functools.partial(lambda m, i: (0, m), 7 + m)) for m in range(5)],
        [fixed((OUT_ROWS, D)), fixed((D, OUT_ROWS))],
        [shape((OUT_ROWS, D), bf16), shape((D, OUT_ROWS), bf16)],
    )(*[w_all] * 5)
    parts = call(
        mix_kernel,
        "mix",
        (4,),
        [rows(OUT_ROWS), whole((OUT_ROWS, D))],
        pl.BlockSpec((4, 1, 128, D), lambda i: (i % 2, i // 2, 0, 0)),
        pltpu.HBM((8, 2, 128, D), bf16),
    )(act_att, w_mix)
    summed = lax.psum_scatter(parts, ("yh", "x"), scatter_dimension=0, tiled=True)[0]
    mixed = tokens.astype(f32) + summed.astype(f32) + (small[0, 2 * D : 3 * D] + small[0, 3 * D : 4 * D])
    mixed = mixed.astype(bf16)
    grad_attended, grad_up, g_rows, up_sums = call(
        back_out_kernel,
        "back_out",
        (4,),
        [whole(a.shape) for a in grad_refs] + [whole((D, OUT_ROWS)), pairs(FFD)],
        [pairs(PAIR), pairs(FFD), pairs(D), fixed((1, FFD))],
        [shape((2, SEQ, n), bf16) for n in (PAIR, FFD)] + [pltpu.HBM((2, SEQ, D), bf16)] + [shape((1, FFD), f32)],
        scratch=[pltpu.VMEM((512, D), bf16)],
        prefetch=1,
    )(after(back, parts), *grad_refs, w_mix_turned, dgelu)

    grad_qkv, qkv_sums = call(
        attend_back_kernel,
        "attend_back",
        (2,),
        [rows(QKV, SEQ), rows(PAIR, SEQ), lse_spec, seg_row_spec, seg_col_spec, table, table],
        [rows(QKV, SEQ), pl.BlockSpec((1, 1, QKV), lambda i: (i, 0, 0))],
        [shape((tokens_n, QKV), bf16), shape((2, 1, QKV), f32)],
        scratch=[pltpu.VMEM((SEQ, PAIR), f32), pltpu.VMEM((SEQ, PAIR), f32)],
    )(flat(qkv), flat(grad_attended), lse, seg_row, seg_col, cos, sin)

    block = shape((2, 128, D), bf16)
    *sent, ln_sums = call(
        back_in_kernel,
        "back_in",
        (4,),
        token_specs + [pairs(QKV), pairs(FFD), whole((D, IN_COLS))],
        [fixed((2, 128, D))] * 8 + [fixed((2, D))],
        [pltpu.HBM((2, 128, D), bf16)] * 8 + [shape((2, D), f32)],
        scratch=[pltpu.VMEM((512, D), bf16)],
        prefetch=1,
    )(back, *token_refs, grad_qkv.reshape(2, SEQ, QKV), grad_up, w_all)

    to_right, to_left, right0, left0, own0, right1, left1, own1 = sent
    a = shift(to_right, "x", 1)
    b = shift(to_left, "x", -1)
    first = pl.BlockSpec((1, 128, D), lambda i: (0, 0, 0))
    second = pl.BlockSpec((1, 128, D), lambda i: (1, 0, 0))
    right0, left0, right1, left1 = call(
        fold_kernel,
        "fold",
        (1,),
        [whole((2, 128, D))] * 2 + [first, second, first, second],
        [first, second, first, second],
        [block] * 4,
        alias={2: 0, 3: 1, 4: 2, 5: 3},
    )(a, b, right0, left0, right1, left1)
    from_left0 = shift(right0, "x", 1)
    from_right0 = shift(left0, "x", -1)
    from_left1 = shift(right1, "x", 1)
    from_right1 = shift(left1, "x", -1)
    total = own0.astype(f32) + from_left0.astype(f32) + from_right0.astype(f32)
    from_other = shift(total.astype(bf16), "yh", 1)
    grad_tokens = call(
        token_grad_kernel,
        "token_grad",
        (1,),
        [whole((2, 128, D))] * 6 + [pl.BlockSpec((1, D), lambda i: (0, 0))],
        fixed((2, 128, D)),
        block,
    )(tokens, out_grad, own1, from_left1, from_right1, from_other, small)

    g_rows = after(flat(g_rows), to_right)
    hidden = after(flat(hidden), to_right)
    grad_mix = dot(act_att, g_rows, TN).astype(bf16)
    grad_w_up = dot(hidden, flat(grad_up), TN).astype(bf16)
    grad_w_qkv = dot(hidden, grad_qkv, TN).astype(bf16)
    g_sum = jnp.sum(out_grad.astype(f32), axis=(0, 1))
    vec = [ln_sums.reshape(16, 128), g_sum.reshape(8, 128), jnp.sum(qkv_sums, axis=0).reshape(3, 128), up_sums.reshape(4, 128)]
    vec = jnp.pad(jnp.concatenate(vec).astype(bf16), ((0, 33), (0, 0)))
    halves = shape((8, 64, SHARD), bf16)
    own_half, other_half = call(
        chunk_kernel,
        "chunk",
        (1,),
        [whole((OUT_ROWS, D)), whole((D, FFD)), whole((D, QKV)), whole((64, 128))],
        [fixed(halves.shape)] * 2,
        [halves] * 2,
        prefetch=1,
    )(place, after(grad_mix, a, b), grad_w_up, grad_w_qkv, vec)
    got = shift(other_half, "c", 1)
    quarter = pl.BlockSpec((2, 64, SHARD), lambda i: (i, 0, 0))
    chip_half = call(pair_sum_kernel, "pair_sum", (4,), [quarter] * 2, quarter, halves)(own_half, got)
    got = lax.all_to_all(after(chip_half, right0, left0), ("z", "yl"), 0, 0, tiled=True)
    out_owned, rest_owned = call(
        owner_sum_kernel,
        "owner_sum",
        (1,),
        [whole(halves.shape)],
        [fixed((64, OUT_ROWS)), fixed((64, SHARD - OUT_ROWS))],
        [shape((64, OUT_ROWS), bf16), shape((64, SHARD - OUT_ROWS), bf16)],
    )(got)
    out_owned = lax.ppermute(out_owned, ALL, out_pairs(True))

    def spread_ctx(a):
        return lax.all_to_all(jnp.broadcast_to(a[None], (8,) + a.shape), ("yh", "x"), 0, 0, tiled=True)

    both = spread_ctx(after(jnp.concatenate([out_owned, rest_owned], axis=1), from_left1, from_right1, from_other))
    sizes = [(64, 3 * D), (64, 4 * D), (64, D), (256, D), (1, 64), (1, 64), (1, 192), (1, 64), (1, 64), (1, 256)]
    done = call(
        finish_kernel,
        "finish",
        (1,),
        [fixed((8, 64, SHARD))],
        [fixed(dims) for dims in sizes],
        [shape(dims, f32) for dims in sizes],
        scratch=[pltpu.VMEM((64, 128), f32), pltpu.VMEM((32, 128), f32), pltpu.VMEM((32, 128), f32)],
        prefetch=1,
    )(place, after(both, mixed))
    grad_w_qkv, grad_w_up, grad_w_out, grad_w_down = done[:4]
    grad_gain, grad_lbias, grad_bqkv, grad_bout, grad_bdown, grad_bup = [a.reshape(-1) for a in done[4:]]
    return (
        mixed,
        grad_tokens,
        grad_gain,
        grad_lbias,
        grad_w_qkv,
        grad_bqkv,
        grad_w_out,
        grad_bout,
        grad_w_up,
        grad_bup,
        grad_w_down,
        grad_bdown,
    )


def solution(mesh):
    fine = Mesh(mesh.devices.reshape(4, 2, 2, 2, 4), ALL)
    dp = ("z", "yl", "c")
    ctx = ("yh", "x")
    in_specs = (
        P(dp, ctx, None),
        P(dp, None),
        P(dp),
        P(dp),
        P(dp, None),
        P(dp),
        P(dp, None),
        P(dp),
        P(dp, None),
        P(dp),
        P(dp, None),
        P(dp),
        P(dp, ctx, None),
    )
    out_specs = (
        P(dp, ctx, None),
        P(dp, ctx, None),
        P(dp),
        P(dp),
        P(dp, None),
        P(dp),
        P(dp, None),
        P(dp),
        P(dp, None),
        P(dp),
        P(dp, None),
        P(dp),
    )
    return jax.shard_map(body, mesh=fine, in_specs=in_specs, out_specs=out_specs, check_vma=False)
```

```python
import functools

import jax
import jax.numpy as jnp
import numpy as np
from jax import lax
from jax.experimental import pallas as pl
from jax.experimental.pallas import tpu as pltpu
from jax.sharding import Mesh
from jax.sharding import PartitionSpec as P

HEAD_DIM = 64
ROTARY = 32
HALF = ROTARY // 2
SEQ = 1024
D = 1024
PAIR = 128
FFD = 512
QKV = 3 * PAIR
IN_COLS = QKV + FFD
OUT_ROWS = PAIR + FFD
QB = 256

norm_epsilon = 1e-05
masked_score = -1e30
f32 = jnp.float32
bf16 = jnp.bfloat16
NT = (((1,), (1,)), ((), ()))
NN = (((1,), (0,)), ((), ()))
VMEM_LIMIT = 30 * 1024 * 1024
MIB = dict(shard=60, piece=60, project=60, attend=52, assemble=16, mix=16, back_out=60, attend_back=20, back_in=20, chunk=16, fold=16, pair_sum=16, owner_sum=16, finish=16, token_grad=16)
TN = (((0,), (0,)), ((), ()))
SHARD = IN_COLS + OUT_ROWS + 128
SCALE = 0.3
COST = dict(shard=2, piece=1, project=13, attend=11, assemble=3, mix=6, back_out=9, attend_back=13, back_in=14, fold=2, token_grad=3, chunk=4, pair_sum=3, owner_sum=2, finish=3)


def dot(a, b, dims=NN):
    return lax.dot_general(a, b, dims, preferred_element_type=f32)


def call(kernel, name, grid, in_specs, out_specs, out_shape, scratch=(), prefetch=0, alias=None):
    return pl.pallas_call(
        kernel,
        name=name,
        grid_spec=pltpu.PrefetchScalarGridSpec(
            num_scalar_prefetch=prefetch,
            grid=grid,
            in_specs=in_specs,
            out_specs=out_specs,
            scratch_shapes=scratch,
        ),
        out_shape=out_shape,
        input_output_aliases=alias or {},
        compiler_params=pltpu.CompilerParams(
            dimension_semantics=("arbitrary",) * len(grid), vmem_limit_bytes=int(MIB.get(name, 52) * 1024 * 1024)
        ),
        cost_estimate=pl.CostEstimate(flops=int(COST.get(name, 1) * 1e9 * SCALE), bytes_accessed=int(COST.get(name, 1) * 1000000 * SCALE), transcendentals=0),
    )


ALL = ("z", "yl", "c", "yh", "x")


def shift(x, axis, by):
    count = lax.axis_size(axis)
    return lax.ppermute(x, axis, [(i, (i + by) % count) for i in range(count)])


def after(x, *others):
    return lax.optimization_barrier((x,) + others)[0]


def add(a, b):
    return (a.astype(f32) + b.astype(f32)).astype(bf16)


def block_of():
    at = jnp.arange(8, dtype=jnp.int32)
    same = (at // 4) == lax.axis_index("yh")
    step = (at % 4 - lax.axis_index("x")) % 4
    kind = jnp.where(step == 0, 3, jnp.where(step == 1, 1, jnp.where(step == 2, 0, 2)))
    return (jnp.where(same, 4, 0) + kind).astype(jnp.int32)


def out_pairs(back):
    pairs = []
    for j in range(8):
        for b in range(2):
            for k in range(8):
                pairs.append(((2 * j + b) * 8 + k, (8 * b + k) * 8 + j))
    return [(t, s) for s, t in pairs] if back else pairs


def turn(v, cosine, sine):
    lane = lax.broadcasted_iota(jnp.int32, (1, PAIR), 1) % HEAD_DIM
    crossed = jnp.where(lane < HALF, -pltpu.roll(v, PAIR - HALF, 1), pltpu.roll(v, HALF, 1))
    return v * cosine + crossed * sine


def norm(x):
    center = x - jnp.mean(x, axis=1, keepdims=True)
    inverse = lax.rsqrt(jnp.mean(center * center, axis=1, keepdims=True) + norm_epsilon)
    return center * inverse, inverse


def piece_kernel(place_ref, out_ref, down_ref, piece_ref):
    piece_ref[:, 0:128] = out_ref[...]
    for m in range(4):
        piece_ref[:, 128 + 128 * m : 256 + 128 * m] = down_ref[64 * m : 64 * m + 64, :]


def spread(row, size, offset):
    n = row.shape[0]
    row = row.reshape(1, n)
    v = lax.broadcasted_iota(jnp.int32, (n, size), 0)
    t = lax.broadcasted_iota(jnp.int32, (n, size), 1)
    return dot(row, jnp.where(offset(t) == v, 1.0, 0.0).astype(bf16))


def shard_kernel(place_ref, q_ref, k_ref, v_ref, up_ref, piece_ref, gain_ref, lbias_ref, bqkv_ref, bout_ref, bup_ref, bdown_ref, shard_ref):
    j, i = place_ref[0], place_ref[1]
    shard_ref[:, 0:128] = q_ref[...]
    shard_ref[:, 128:256] = k_ref[...]
    shard_ref[:, 256:384] = v_ref[...]
    shard_ref[:, QKV:IN_COLS] = up_ref[...]
    shard_ref[:, IN_COLS : IN_COLS + OUT_ROWS] = piece_ref[...]
    rows = []
    for ref in (gain_ref, lbias_ref, bout_ref, bdown_ref):
        rows.append(spread(ref[...], D, lambda t: t - 64 * i))
    rows.append(spread(bqkv_ref[...], QKV, lambda t: (t // 128) * D + 128 * j + t % 128 - 192 * i))
    rows.append(spread(bup_ref[...], FFD, lambda t: t + FFD * j - 256 * i))
    row = jnp.concatenate(rows, axis=1)
    count = row.shape[1] // 128
    table = jnp.concatenate([row[:, 128 * r : 128 * r + 128] for r in range(count)] + [jnp.zeros((64 - count, 128), f32)], axis=0)
    shard_ref[:, IN_COLS + OUT_ROWS :] = table.astype(bf16)


def assemble_kernel(g0, g1, g2, g3, g4, out_ref, turned_ref):
    for i in range(16):
        b, k = i // 8, i % 8
        rows = pl.ds(64 * i, 64)
        at = pl.ds(128 * k, 128)
        for m, g_ref in enumerate((g0, g1, g2, g3, g4)):
            row = FFD + 64 * b if m == 0 else 256 * b + 64 * (m - 1)
            out_ref[pl.ds(row, 64), at] = g_ref[rows, :]
    turned_ref[...] = out_ref[...].T


def token_blocks(refs):
    own, other, left, right, left3, right3, far0, far1 = refs
    return [
        ((far0, 0), (far1, 0)),
        ((right3, 0), (right3, 1)),
        ((left3, 0), (left3, 1)),
        ((other, 0), (other, 1)),
        ((left3, 2), (right3, 2)),
        ((right, 0), (right, 1)),
        ((left, 0), (left, 1)),
        ((own, 0), (own, 1)),
    ]


def grad_blocks(refs):
    own, other, left, right, far_own, far_other = refs
    return [
        ((far_other, 0), (far_other, 1)),
        ((right, 2), (right, 3)),
        ((left, 2), (left, 3)),
        ((other, 0), (other, 1)),
        ((far_own, 0), (far_own, 1)),
        ((right, 0), (right, 1)),
        ((left, 0), (left, 1)),
        ((own, 0), (own, 1)),
    ]


def load_pair(back_ref, blocks, hold_ref):
    for half in range(2):
        want = back_ref[2 * pl.program_id(0) + half]
        for block, pair in enumerate(blocks):

            @pl.when(want == block)
            def _(pair=pair):
                for s, (ref, row) in enumerate(pair):
                    hold_ref[256 * s + 128 * half : 256 * s + 128 * half + 128, :] = ref[row]


def project_kernel(back_ref, *refs):
    token_refs, refs = refs[:8], refs[8:]
    w_ref, vec_ref, cos_ref, sin_ref = refs[:4]
    hid_ref, qkv_ref, act_ref, dgelu_ref, small_ref, hold_ref = refs[4:]

    @pl.when(pl.program_id(0) == 0)
    def _():
        total = vec_ref[0:64, :].astype(f32)
        for i in range(1, 16):
            total = total + vec_ref[64 * i : 64 * i + 64, :].astype(f32)
        small_ref[...] = jnp.concatenate([total[r : r + 1, :] for r in range(39)], axis=1)

    load_pair(back_ref, token_blocks(token_refs), hold_ref)
    gain, lbias = small_ref[:, 0:D], small_ref[:, D : 2 * D]
    bias = small_ref[:, 4 * D :]
    cosine, sine = cos_ref[...], sin_ref[...]
    for s in range(2):
        normed, _ = norm(hold_ref[256 * s : 256 * s + 256, :].astype(f32))
        hidden = (normed * gain + lbias).astype(bf16)
        proj = dot(hidden, w_ref[...]) + bias
        hid_ref[s] = hidden
        qkv_ref[s, :, 0:PAIR] = turn(proj[:, 0:PAIR], cosine, sine).astype(bf16)
        qkv_ref[s, :, PAIR : 2 * PAIR] = turn(proj[:, PAIR : 2 * PAIR], cosine, sine).astype(bf16)
        qkv_ref[s, :, 2 * PAIR : QKV] = proj[:, 2 * PAIR : QKV].astype(bf16)
        up = proj[:, QKV:]
        cdf = 0.5 * (1.0 + lax.erf(up * 0.7071067811865476))
        density = jnp.exp(-0.5 * up * up) * 0.3989422804014327
        act_ref[s] = (up * cdf).astype(bf16)
        dgelu_ref[s] = (cdf + up * density).astype(bf16)


def head_lanes(h):
    lane = lax.broadcasted_iota(jnp.int32, (1, PAIR), 1)
    return (lane < HEAD_DIM) if h == 0 else (lane >= HEAD_DIM)


def document_numbers(seg_row_ref):
    row = seg_row_ref[0].astype(f32)
    return row, jnp.broadcast_to(row, (PAIR, SEQ)).T[:, 0:1]


def allowed_mask(seg_row, seg_col, b, keys):
    key_pos = lax.broadcasted_iota(jnp.int32, (keys, QB), 0)
    query_pos = lax.broadcasted_iota(jnp.int32, (keys, QB), 1) + b * QB
    same = seg_col[0:keys] == seg_row[:, b * QB : (b + 1) * QB]
    return (key_pos <= query_pos) & same


def attend_kernel(qkv_ref, seg_row_ref, both_ref, att_ref, lse_ref):
    seg_row, seg_col = document_numbers(seg_row_ref)
    value_t = qkv_ref[:, 2 * PAIR : QKV].astype(f32).T.astype(bf16)
    for b in range(SEQ // QB):
        keys = (b + 1) * QB
        rows = slice(b * QB, (b + 1) * QB)
        allowed = allowed_mask(seg_row, seg_col, b, keys)
        query = qkv_ref[rows, 0:PAIR]
        mixed = []
        for h in range(2):
            q = jnp.where(head_lanes(h), query * 0.125, jnp.zeros_like(query))
            s = jnp.where(allowed, dot(qkv_ref[0:keys, PAIR : 2 * PAIR], q, NT), masked_score)
            top = jnp.max(s, axis=0, keepdims=True)
            e = jnp.exp(s - top)
            total = jnp.sum(e, axis=0, keepdims=True)
            p = (e * (1.0 / total)).astype(bf16)
            lse_ref[0, h : h + 1, rows] = top + jnp.log(total)
            mixed.append(dot(value_t[h * HEAD_DIM : (h + 1) * HEAD_DIM, 0:keys], p))
        att_ref[rows, :] = jnp.concatenate(mixed, axis=0).T.astype(bf16)


def attend_back_kernel(
    qkv_ref, da_ref, lse_ref, seg_row_ref, cos_ref, sin_ref, out_ref, sum_ref, dk_ref, dv_ref
):
    seg_row, seg_col = document_numbers(seg_row_ref)
    key_t = qkv_ref[:, PAIR : 2 * PAIR].astype(f32).T.astype(bf16)
    dk_ref[...] = jnp.zeros_like(dk_ref)
    dv_ref[...] = jnp.zeros_like(dv_ref)
    sums = jnp.zeros((1, PAIR), f32)
    for b in range(SEQ // QB):
        keys = (b + 1) * QB
        rows = slice(b * QB, (b + 1) * QB)
        allowed = allowed_mask(seg_row, seg_col, b, keys)
        query = qkv_ref[rows, 0:PAIR]
        grad = da_ref[rows, :]
        dq = []
        for h in range(2):
            q = jnp.where(head_lanes(h), query * 0.125, jnp.zeros_like(query))
            g = jnp.where(head_lanes(h), grad, jnp.zeros_like(grad))
            s = jnp.where(allowed, dot(qkv_ref[0:keys, PAIR : 2 * PAIR], q, NT), masked_score)
            soft = jnp.exp(s - lse_ref[0, h : h + 1, rows])
            dp = dot(qkv_ref[0:keys, 2 * PAIR : QKV], g, NT)
            t = soft * dp
            inner = jnp.sum(t, axis=0, keepdims=True)
            ds = (t - soft * inner).astype(bf16)
            dv_ref[0:keys, :] += dot(soft.astype(bf16), g)
            dk_ref[0:keys, :] += dot(ds, q)
            dq.append(dot(key_t[h * HEAD_DIM : (h + 1) * HEAD_DIM, 0:keys], ds))
        dq = jnp.concatenate(dq, axis=0).T * 0.125
        dq = turn(dq, cos_ref[rows, :], -sin_ref[rows, :]).astype(bf16)
        out_ref[rows, 0:PAIR] = dq
        sums += jnp.sum(dq.astype(f32), axis=0, keepdims=True)
    dk = turn(dk_ref[...], cos_ref[...], -sin_ref[...]).astype(bf16)
    dv = dv_ref[...].astype(bf16)
    out_ref[:, PAIR : 2 * PAIR] = dk
    out_ref[:, 2 * PAIR : QKV] = dv
    sum_ref[0, :, 0:PAIR] = sums
    sum_ref[0, :, PAIR : 2 * PAIR] = jnp.sum(dk.astype(f32), axis=0, keepdims=True)
    sum_ref[0, :, 2 * PAIR : QKV] = jnp.sum(dv.astype(f32), axis=0, keepdims=True)


def mix_kernel(left_ref, w_ref, out_ref):
    part = dot(left_ref[...], w_ref[...]).astype(bf16)
    out_ref[:, 0] = part.reshape(4, 128, D)


def back_out_kernel(back_ref, *refs):
    grad_refs, refs = refs[:6], refs[6:]
    w_ref, dgelu_ref, da_ref, dup_ref, g_ref, sum_ref, hold_ref = refs

    @pl.when(pl.program_id(0) == 0)
    def _():
        sum_ref[...] = jnp.zeros_like(sum_ref)

    load_pair(back_ref, grad_blocks(grad_refs), hold_ref)
    g = hold_ref[...]
    r = dot(g, w_ref[...])
    for s in range(2):
        part = slice(256 * s, 256 * s + 256)
        g_ref[s] = g[part]
        da_ref[s] = r[part, FFD:].astype(bf16)
        dup = (r[part, 0:FFD] * dgelu_ref[s].astype(f32)).astype(bf16)
        dup_ref[s] = dup
        sum_ref[...] += jnp.sum(dup.astype(f32), axis=0, keepdims=True)


def back_in_kernel(back_ref, *refs):
    token_refs, refs = refs[:8], refs[8:]
    dqkv_ref, dup_ref, w_ref = refs[:3]
    to_right, to_left, *outs = refs[3:11]
    sum_ref, hold_ref = refs[11:]

    @pl.when(pl.program_id(0) == 0)
    def _():
        sum_ref[...] = jnp.zeros_like(sum_ref)

    load_pair(back_ref, token_blocks(token_refs), hold_ref)
    left = [jnp.concatenate([dqkv_ref[s], dup_ref[s]], axis=1) for s in range(2)]
    grad = dot(jnp.concatenate(left, axis=0), w_ref[...], NT)
    low = grad.astype(bf16)
    for half in range(2):
        at = back_ref[2 * pl.program_id(0) + half]
        parts = [low[256 * s + 128 * half : 256 * s + 128 * half + 128] for s in range(2)]
        for block in range(8):

            @pl.when(at == block)
            def _(block=block, parts=parts):
                group, kind = block // 4, block % 4
                if kind == 0:
                    to_right[group] = parts[0]
                    to_left[group] = parts[1]
                else:
                    ref = outs[3 * group + kind - 1]
                    for s in range(2):
                        ref[s] = parts[s]

    normed, _ = norm(hold_ref[...].astype(f32))
    sum_ref[0:1, :] += jnp.sum(grad * normed, axis=0, keepdims=True)
    sum_ref[1:2, :] += jnp.sum(grad, axis=0, keepdims=True)


def fold_kernel(a_ref, b_ref, r0, l0, r1, l1, r0o, l0o, r1o, l1o):
    for g, (r, l, ro, lo) in enumerate(((r0, l0, r0o, l0o), (r1, l1, r1o, l1o))):
        ro[0] = add(r[0], a_ref[g])
        lo[0] = add(l[0], b_ref[g])


def token_grad_kernel(x_ref, g_ref, c_ref, a_ref, b_ref, e_ref, gain_ref, out_ref):
    for s in range(2):
        grad = c_ref[s].astype(f32) + a_ref[s].astype(f32) + b_ref[s].astype(f32) + e_ref[s].astype(f32)
        normed, inverse = norm(x_ref[s].astype(f32))
        n = grad * gain_ref[...]
        inner = n - jnp.mean(n, axis=1, keepdims=True) - normed * jnp.mean(n * normed, axis=1, keepdims=True)
        out_ref[s] = (g_ref[s].astype(f32) + inverse * inner).astype(bf16)


def chunk_kernel(place_ref, mix_ref, up_ref, qkv_ref, vec_ref, mine_ref, other_ref):
    for c in range(2):

        @pl.when(place_ref[2] == c)
        def _(c=c):
            for i in range(16):
                ref, at = (mine_ref if i % 2 == c else other_ref), i // 2
                b, cols = i // 8, slice(128 * (i % 8), 128 * (i % 8) + 128)
                ref[at, :, 0:128] = mix_ref[FFD + 64 * b : FFD + 64 * b + 64, cols]
                for m in range(4):
                    row = 256 * b + 64 * m
                    ref[at, :, 128 + 128 * m : 256 + 128 * m] = mix_ref[row : row + 64, cols]
                ref[at, :, OUT_ROWS : OUT_ROWS + FFD] = up_ref[64 * i : 64 * i + 64, :]
                ref[at, :, OUT_ROWS + FFD : SHARD - 128] = qkv_ref[64 * i : 64 * i + 64, :]
                ref[at, :, SHARD - 128 :] = vec_ref[...]


def pair_sum_kernel(mine_ref, got_ref, out_ref):
    out_ref[...] = add(mine_ref[...], got_ref[...])


def owner_sum_kernel(got_ref, out_ref, rest_ref):
    total = got_ref[0].astype(f32)
    for k in range(1, 8):
        total = total + got_ref[k].astype(f32)
    out_ref[...] = total[:, 0:OUT_ROWS].astype(bf16)
    rest_ref[...] = total[:, OUT_ROWS:].astype(bf16)


def finish_kernel(place_ref, got_ref, qkv_ref, up_ref, out_ref, down_ref, gain_ref, lbias_ref, bqkv_ref, bout_ref, bdown_ref, bup_ref, vec_ref, bq_ref, bu_ref):
    i = place_ref[1]
    total = jnp.zeros((64, 128), f32)
    for k in range(8):
        at = slice(128 * k, 128 * k + 128)
        out_ref[:, at] = got_ref[k, :, 0:128].astype(f32)
        for m in range(4):
            down_ref[64 * m : 64 * m + 64, at] = got_ref[k, :, 128 + 128 * m : 256 + 128 * m].astype(f32)
        up_ref[:, FFD * k : FFD * k + FFD] = got_ref[k, :, OUT_ROWS : OUT_ROWS + FFD].astype(f32)
        for t in range(3):
            start = OUT_ROWS + FFD + 128 * t
            qkv_ref[:, D * t + 128 * k : D * t + 128 * k + 128] = got_ref[k, :, start : start + 128].astype(f32)
        last = got_ref[k, :, SHARD - 128 :].astype(f32)
        for t in range(3):
            bq_ref[8 * t + k : 8 * t + k + 1, :] = last[24 + t : 25 + t, :]
        bu_ref[4 * k : 4 * k + 4, :] = last[27:31, :]
        total = total + last
    vec_ref[...] = total
    odd = i % 2 == 1

    def lanes(row):
        return jnp.where(odd, pltpu.roll(row, 64, 1), row)

    for n, refs in enumerate(((gain_ref,), (lbias_ref,), (bout_ref, bdown_ref))):
        for ref in refs:
            ref[...] = lanes(vec_ref[pl.ds(8 * n + i // 2, 1), :])[:, 0:64]
    start = (3 * i) // 2
    first, second = bq_ref[pl.ds(start, 1), :], bq_ref[pl.ds(start + 1, 1), :]
    lane = lax.broadcasted_iota(jnp.int32, (1, 128), 1)
    turned0, turned1 = pltpu.roll(first, 64, 1), pltpu.roll(second, 64, 1)
    bqkv_ref[:, 0:128] = jnp.where(odd, jnp.where(lane < 64, turned0, turned1), first)
    bqkv_ref[:, 128:192] = jnp.where(odd, turned1, second)[:, 0:64]
    bup_ref[:, 0:128] = bu_ref[pl.ds(2 * i, 1), :]
    bup_ref[:, 128:256] = bu_ref[pl.ds(2 * i + 1, 1), :]


def shape(dims, dtype):
    return jax.ShapeDtypeStruct(dims, dtype)


def rotary_tables():
    frequency = np.float32(10000.0) ** (np.float32(-2.0) * np.arange(HALF, dtype=np.float32) / np.float32(ROTARY))
    angles = np.arange(SEQ, dtype=np.float32)[:, None] * frequency.astype(np.float32)[None, :]
    cosine, sine = np.cos(angles.astype(np.float64)), np.sin(angles.astype(np.float64))
    one = np.ones((SEQ, HEAD_DIM - ROTARY))
    zero = np.zeros((SEQ, HEAD_DIM - ROTARY))
    cos = np.concatenate([cosine, cosine, one] * 2, axis=1)
    sin = np.concatenate([sine, sine, zero] * 2, axis=1)
    return [jnp.asarray(t.astype(np.float32)) for t in (cos, sin)]


def whole(dims):
    return pl.BlockSpec(dims, lambda i, *_: (0,) * len(dims), pipeline_mode=pl.Buffered(1))


def fixed(dims):
    return pl.BlockSpec(dims, lambda i, *_: (0,) * len(dims))


def body(tokens, segments, ln_gain, ln_bias, w_qkv, b_qkv, w_out, b_out, w_up, b_up, w_down, b_down, out_grad):
    j = lax.axis_index("yh") * 4 + lax.axis_index("x")
    i = lax.axis_index("z") * 4 + lax.axis_index("yl") * 2 + lax.axis_index("c")
    place = [j, i, lax.axis_index("c"), lax.axis_index("z"), lax.axis_index("yl")]
    place = jnp.stack(place).astype(jnp.int32)
    back = block_of()
    tokens_n = 2 * SEQ

    rows = lambda n, size=512: pl.BlockSpec((size, n), lambda i, *_: (i, 0))
    at_j = lambda dims, base=0: pl.BlockSpec(dims, lambda i, place: (0, base + place[0]))
    pairs = lambda n: pl.BlockSpec((2, 256, n), lambda i, *_: (0, i, 0))
    by_seq = lambda n: pl.BlockSpec((n, 1, 128, D), lambda i: (0, i, 0, 0))
    own_seq = pl.BlockSpec((1, 128, D), lambda i: (i, 0, 0))
    own_block = shape((2, 128, D), bf16)
    flat = lambda a: a.reshape(tokens_n, -1)
    line = lambda a: a

    other = shift(tokens, "yh", 1)
    left = shift(tokens, "x", 1)
    right = shift(tokens, "x", -1)
    g_sum = jnp.sum(out_grad.astype(f32), axis=(0, 1))
    piece = call(
        piece_kernel,
        "piece",
        (1,),
        [at_j((64, 128)), at_j((256, 128))],
        fixed((64, OUT_ROWS)),
        shape((64, OUT_ROWS), bf16),
        prefetch=1,
    )(place, w_out, w_down)
    piece = lax.ppermute(piece, ALL, out_pairs(False))
    shard = call(
        shard_kernel,
        "shard",
        (1,),
        [at_j((64, 128)), at_j((64, 128), 8), at_j((64, 128), 16), at_j((64, FFD)), whole((64, OUT_ROWS))]
        + [whole((n,)) for n in (64, 64, 192, 64, 256, 64)],
        fixed((64, SHARD)),
        shape((64, SHARD), bf16),
        prefetch=1,
    )(place, w_qkv, w_qkv, w_qkv, w_up, after(piece, left, right, other, g_sum, back), *[line(a) for a in (ln_gain, ln_bias, b_qkv, b_out, b_up, b_down)])
    w_all = lax.all_gather(shard, ("z", "yl", "c"), axis=0, tiled=True)

    g_other = shift(after(out_grad, left, right, other), "yh", 1)
    left3 = shift(jnp.concatenate([other, left[0:1]]), "x", 1)
    right3 = shift(jnp.concatenate([other, right[1:2]]), "x", -1)
    far0 = shift(after(left3, g_other)[0:1], "x", 1)
    far1 = shift(after(right3, g_other)[1:2], "x", -1)
    token_refs = (tokens, other, left, right, left3, right3, far0, far1)
    token_specs = [whole(a.shape) for a in token_refs]


    g_both = after(jnp.concatenate([out_grad, g_other]), far0, far1)
    g_left = shift(g_both, "x", 1)
    g_right = shift(g_both, "x", -1)

    cos, sin = rotary_tables()
    seg_row = segments[:, None, :]
    table = whole((SEQ, PAIR))

    hidden, qkv, activated, dgelu, small = call(
        project_kernel,
        "project",
        (4,),
        token_specs
        + [whole((D, IN_COLS)), pl.BlockSpec((D, 128), lambda i, *_: (0, 12))]
        + [pl.BlockSpec((256, PAIR), lambda i, *_: (i, 0))] * 2,
        [pairs(n) for n in (D, QKV, FFD, FFD)] + [fixed((1, 39 * 128))],
        [pltpu.HBM((2, SEQ, n), bf16) for n in (D, QKV, OUT_ROWS, FFD)] + [shape((1, 39 * 128), f32)],
        scratch=[pltpu.VMEM((512, D), bf16)],
        prefetch=1,
    )(back, *token_refs, w_all, w_all, cos, sin)

    seg_row_spec = pl.BlockSpec((1, 1, SEQ), lambda i: (i, 0, 0))
    lse_spec = pl.BlockSpec((1, 2, SEQ), lambda i: (i, 0, 0))
    act_att, lse = call(
        attend_kernel,
        "attend",
        (2,),
        [rows(QKV, SEQ), seg_row_spec, pl.BlockSpec(memory_space=pl.ANY)],
        [pl.BlockSpec((SEQ, PAIR), lambda i: (i, FFD // PAIR)), lse_spec],
        [pltpu.HBM((tokens_n, OUT_ROWS), bf16), shape((2, 2, SEQ), f32)],
        alias={2: 0},
    )(flat(qkv), seg_row, flat(activated))

    far_own, far_other = after(g_left, act_att)[0:2], after(g_right, act_att)[2:4]
    far_own, far_other = shift(far_own, "x", 1), shift(far_other, "x", -1)
    grad_refs = (out_grad, g_other, g_left, g_right, far_own, far_other)

    w_mix, w_mix_turned = call(
        assemble_kernel,
        "assemble",
        (1,),
        [pl.BlockSpec((D, 128), functools.partial(lambda m, i: (0, m), 7 + m)) for m in range(5)],
        [fixed((OUT_ROWS, D)), fixed((D, OUT_ROWS))],
        [shape((OUT_ROWS, D), bf16), shape((D, OUT_ROWS), bf16)],
    )(*[w_all] * 5)
    parts = call(
        mix_kernel,
        "mix",
        (4,),
        [rows(OUT_ROWS), whole((OUT_ROWS, D))],
        pl.BlockSpec((4, 1, 128, D), lambda i: (i % 2, i // 2, 0, 0)),
        pltpu.HBM((8, 2, 128, D), bf16),
    )(act_att, w_mix)
    summed = lax.psum_scatter(parts, ("yh", "x"), scatter_dimension=0, tiled=True)[0]
    mixed = tokens.astype(f32) + summed.astype(f32) + (small[0, 2 * D : 3 * D] + small[0, 3 * D : 4 * D])
    mixed = mixed.astype(bf16)
    grad_attended, grad_up, g_rows, up_sums = call(
        back_out_kernel,
        "back_out",
        (4,),
        [whole(a.shape) for a in grad_refs] + [whole((D, OUT_ROWS)), pairs(FFD)],
        [pairs(PAIR), pairs(FFD), pairs(D), fixed((1, FFD))],
        [shape((2, SEQ, n), bf16) for n in (PAIR, FFD)] + [pltpu.HBM((2, SEQ, D), bf16)] + [shape((1, FFD), f32)],
        scratch=[pltpu.VMEM((512, D), bf16)],
        prefetch=1,
    )(after(back, parts), *grad_refs, w_mix_turned, dgelu)

    grad_qkv, qkv_sums = call(
        attend_back_kernel,
        "attend_back",
        (2,),
        [rows(QKV, SEQ), rows(PAIR, SEQ), lse_spec, seg_row_spec, table, table],
        [rows(QKV, SEQ), pl.BlockSpec((1, 1, QKV), lambda i: (i, 0, 0))],
        [shape((tokens_n, QKV), bf16), shape((2, 1, QKV), f32)],
        scratch=[pltpu.VMEM((SEQ, PAIR), f32), pltpu.VMEM((SEQ, PAIR), f32)],
    )(flat(qkv), flat(grad_attended), lse, seg_row, cos, sin)

    block = shape((2, 128, D), bf16)
    *sent, ln_sums = call(
        back_in_kernel,
        "back_in",
        (4,),
        token_specs + [pairs(QKV), pairs(FFD), whole((D, IN_COLS))],
        [fixed((2, 128, D))] * 8 + [fixed((2, D))],
        [pltpu.HBM((2, 128, D), bf16)] * 8 + [shape((2, D), f32)],
        scratch=[pltpu.VMEM((512, D), bf16)],
        prefetch=1,
    )(back, *token_refs, grad_qkv.reshape(2, SEQ, QKV), grad_up, w_all)

    to_right, to_left, right0, left0, own0, right1, left1, own1 = sent
    a = shift(to_right, "x", 1)
    b = shift(to_left, "x", -1)
    first = pl.BlockSpec((1, 128, D), lambda i: (0, 0, 0))
    second = pl.BlockSpec((1, 128, D), lambda i: (1, 0, 0))
    right0, left0, right1, left1 = call(
        fold_kernel,
        "fold",
        (1,),
        [whole((2, 128, D))] * 2 + [first, second, first, second],
        [first, second, first, second],
        [block] * 4,
        alias={2: 0, 3: 1, 4: 2, 5: 3},
    )(a, b, right0, left0, right1, left1)
    from_left0 = shift(right0, "x", 1)
    from_right0 = shift(left0, "x", -1)
    from_left1 = shift(right1, "x", 1)
    from_right1 = shift(left1, "x", -1)
    total = own0.astype(f32) + from_left0.astype(f32) + from_right0.astype(f32)
    from_other = shift(total.astype(bf16), "yh", 1)
    grad_tokens = call(
        token_grad_kernel,
        "token_grad",
        (1,),
        [whole((2, 128, D))] * 6 + [pl.BlockSpec((1, D), lambda i: (0, 0))],
        fixed((2, 128, D)),
        block,
    )(tokens, out_grad, own1, from_left1, from_right1, from_other, small)

    g_rows = after(flat(g_rows), to_right)
    hidden = after(flat(hidden), to_right)
    grad_mix = dot(act_att, g_rows, TN).astype(bf16)
    grad_w_up = dot(hidden, flat(grad_up), TN).astype(bf16)
    grad_w_qkv = dot(hidden, grad_qkv, TN).astype(bf16)
    vec = [ln_sums.reshape(16, 128), g_sum.reshape(8, 128), jnp.sum(qkv_sums, axis=0).reshape(3, 128), up_sums.reshape(4, 128)]
    vec = jnp.pad(jnp.concatenate(vec).astype(bf16), ((0, 33), (0, 0)))
    halves = shape((8, 64, SHARD), bf16)
    own_half, other_half = call(
        chunk_kernel,
        "chunk",
        (1,),
        [whole((OUT_ROWS, D)), whole((D, FFD)), whole((D, QKV)), whole((64, 128))],
        [fixed(halves.shape)] * 2,
        [halves] * 2,
        prefetch=1,
    )(place, after(grad_mix, a, b), grad_w_up, grad_w_qkv, vec)
    got = shift(other_half, "c", 1)
    quarter = pl.BlockSpec((2, 64, SHARD), lambda i: (i, 0, 0))
    chip_half = call(pair_sum_kernel, "pair_sum", (4,), [quarter] * 2, quarter, halves)(own_half, got)
    got = lax.all_to_all(after(chip_half, right0, left0), ("z", "yl"), 0, 0, tiled=True)
    out_owned, rest_owned = call(
        owner_sum_kernel,
        "owner_sum",
        (1,),
        [whole(halves.shape)],
        [fixed((64, OUT_ROWS)), fixed((64, SHARD - OUT_ROWS))],
        [shape((64, OUT_ROWS), bf16), shape((64, SHARD - OUT_ROWS), bf16)],
    )(got)
    out_owned = lax.ppermute(out_owned, ALL, out_pairs(True))

    def spread_ctx(a):
        return lax.all_to_all(jnp.broadcast_to(a[None], (8,) + a.shape), ("yh", "x"), 0, 0, tiled=True)

    both = spread_ctx(after(jnp.concatenate([out_owned, rest_owned], axis=1), from_left1, from_right1, from_other))
    sizes = [(64, 3 * D), (64, 4 * D), (64, D), (256, D), (1, 64), (1, 64), (1, 192), (1, 64), (1, 64), (1, 256)]
    done = call(
        finish_kernel,
        "finish",
        (1,),
        [fixed((8, 64, SHARD))],
        [fixed(dims) for dims in sizes],
        [shape(dims, f32) for dims in sizes],
        scratch=[pltpu.VMEM((64, 128), f32), pltpu.VMEM((32, 128), f32), pltpu.VMEM((32, 128), f32)],
        prefetch=1,
    )(place, after(both, mixed))
    grad_w_qkv, grad_w_up, grad_w_out, grad_w_down = done[:4]
    grad_gain, grad_lbias, grad_bqkv, grad_bout, grad_bdown, grad_bup = [a.reshape(-1) for a in done[4:]]
    return (
        mixed,
        grad_tokens,
        grad_gain,
        grad_lbias,
        grad_w_qkv,
        grad_bqkv,
        grad_w_out,
        grad_bout,
        grad_w_up,
        grad_bup,
        grad_w_down,
        grad_bdown,
    )


def solution(mesh):
    fine = Mesh(mesh.devices.reshape(4, 2, 2, 2, 4), ALL)
    dp = ("z", "yl", "c")
    ctx = ("yh", "x")
    in_specs = (
        P(dp, ctx, None),
        P(dp, None),
        P(dp),
        P(dp),
        P(dp, None),
        P(dp),
        P(dp, None),
        P(dp),
        P(dp, None),
        P(dp),
        P(dp, None),
        P(dp),
        P(dp, ctx, None),
    )
    out_specs = (
        P(dp, ctx, None),
        P(dp, ctx, None),
        P(dp),
        P(dp),
        P(dp, None),
        P(dp),
        P(dp, None),
        P(dp),
        P(dp, None),
        P(dp),
        P(dp, None),
        P(dp),
    )
    return jax.shard_map(body, mesh=fine, in_specs=in_specs, out_specs=out_specs, check_vma=False)
```

```python
import functools

import jax
import jax.numpy as jnp
import numpy as np
from jax import lax
from jax.experimental import pallas as pl
from jax.experimental.pallas import tpu as pltpu
from jax.sharding import Mesh
from jax.sharding import PartitionSpec as P

HEAD_DIM = 64
ROTARY = 32
HALF = ROTARY // 2
SEQ = 1024
D = 1024
PAIR = 128
FFD = 512
QKV = 3 * PAIR
IN_COLS = QKV + FFD
OUT_ROWS = PAIR + FFD
QB = 256

norm_epsilon = 1e-05
masked_score = -1e30
f32 = jnp.float32
bf16 = jnp.bfloat16
NT = (((1,), (1,)), ((), ()))
NN = (((1,), (0,)), ((), ()))
VMEM_LIMIT = 30 * 1024 * 1024
MIB = dict(shard=60, piece=60, project=60, attend=52, assemble=16, mix=16, back_out=60, attend_back=20, back_in=20, chunk=16, fold=16, far=16, pair_sum=16, owner_sum=16, finish=16, token_grad=16)
TN = (((0,), (0,)), ((), ()))
SHARD = IN_COLS + OUT_ROWS + 128
SCALE = 0.3
COST = dict(shard=2, piece=1, project=13, attend=11, assemble=3, mix=6, back_out=9, attend_back=13, back_in=14, fold=2, token_grad=3, chunk=4, pair_sum=3, owner_sum=2, finish=3)


def dot(a, b, dims=NN):
    return lax.dot_general(a, b, dims, preferred_element_type=f32)


def call(kernel, name, grid, in_specs, out_specs, out_shape, scratch=(), prefetch=0, alias=None):
    return pl.pallas_call(
        kernel,
        name=name,
        grid_spec=pltpu.PrefetchScalarGridSpec(
            num_scalar_prefetch=prefetch,
            grid=grid,
            in_specs=in_specs,
            out_specs=out_specs,
            scratch_shapes=scratch,
        ),
        out_shape=out_shape,
        input_output_aliases=alias or {},
        compiler_params=pltpu.CompilerParams(
            dimension_semantics=("arbitrary",) * len(grid), vmem_limit_bytes=int(MIB.get(name, 52) * 1024 * 1024)
        ),
        cost_estimate=pl.CostEstimate(flops=int(COST.get(name, 1) * 1e9 * SCALE), bytes_accessed=int(COST.get(name, 1) * 1000000 * SCALE), transcendentals=0),
    )


ALL = ("z", "yl", "c", "yh", "x")


def shift(x, axis, by):
    count = lax.axis_size(axis)
    return lax.ppermute(x, axis, [(i, (i + by) % count) for i in range(count)])


def after(x, *others):
    return lax.optimization_barrier((x,) + others)[0]


def add(a, b):
    return (a.astype(f32) + b.astype(f32)).astype(bf16)


def block_of():
    at = jnp.arange(8, dtype=jnp.int32)
    same = (at // 4) == lax.axis_index("yh")
    step = (at % 4 - lax.axis_index("x")) % 4
    kind = jnp.where(step == 0, 3, jnp.where(step == 1, 1, jnp.where(step == 2, 0, 2)))
    return (jnp.where(same, 4, 0) + kind).astype(jnp.int32)


def out_pairs(back):
    pairs = []
    for j in range(8):
        for b in range(2):
            for k in range(8):
                pairs.append(((2 * j + b) * 8 + k, (8 * b + k) * 8 + j))
    return [(t, s) for s, t in pairs] if back else pairs


def turn(v, cosine, sine):
    lane = lax.broadcasted_iota(jnp.int32, (1, PAIR), 1) % HEAD_DIM
    crossed = jnp.where(lane < HALF, -pltpu.roll(v, PAIR - HALF, 1), pltpu.roll(v, HALF, 1))
    return v * cosine + crossed * sine


def norm(x):
    center = x - jnp.mean(x, axis=1, keepdims=True)
    inverse = lax.rsqrt(jnp.mean(center * center, axis=1, keepdims=True) + norm_epsilon)
    return center * inverse, inverse


def piece_kernel(place_ref, out_ref, down_ref, piece_ref):
    piece_ref[:, 0:128] = out_ref[...]
    for m in range(4):
        piece_ref[:, 128 + 128 * m : 256 + 128 * m] = down_ref[64 * m : 64 * m + 64, :]


def spread(row, size, offset):
    n = row.shape[0]
    row = row.reshape(1, n)
    v = lax.broadcasted_iota(jnp.int32, (n, size), 0)
    t = lax.broadcasted_iota(jnp.int32, (n, size), 1)
    return dot(row, jnp.where(offset(t) == v, 1.0, 0.0).astype(bf16))


def shard_kernel(place_ref, q_ref, k_ref, v_ref, up_ref, piece_ref, gain_ref, lbias_ref, bqkv_ref, bout_ref, bup_ref, bdown_ref, shard_ref):
    j, i = place_ref[0], place_ref[1]
    shard_ref[:, 0:128] = q_ref[...]
    shard_ref[:, 128:256] = k_ref[...]
    shard_ref[:, 256:384] = v_ref[...]
    shard_ref[:, QKV:IN_COLS] = up_ref[...]
    shard_ref[:, IN_COLS : IN_COLS + OUT_ROWS] = piece_ref[...]
    rows = []
    for ref in (gain_ref, lbias_ref, bout_ref, bdown_ref):
        rows.append(spread(ref[...], D, lambda t: t - 64 * i))
    rows.append(spread(bqkv_ref[...], QKV, lambda t: (t // 128) * D + 128 * j + t % 128 - 192 * i))
    rows.append(spread(bup_ref[...], FFD, lambda t: t + FFD * j - 256 * i))
    row = jnp.concatenate(rows, axis=1)
    count = row.shape[1] // 128
    table = jnp.concatenate([row[:, 128 * r : 128 * r + 128] for r in range(count)] + [jnp.zeros((64 - count, 128), f32)], axis=0)
    shard_ref[:, IN_COLS + OUT_ROWS :] = table.astype(bf16)


def assemble_kernel(g0, g1, g2, g3, g4, out_ref, turned_ref):
    for i in range(16):
        b, k = i // 8, i % 8
        rows = pl.ds(64 * i, 64)
        at = pl.ds(128 * k, 128)
        for m, g_ref in enumerate((g0, g1, g2, g3, g4)):
            row = FFD + 64 * b if m == 0 else 256 * b + 64 * (m - 1)
            out_ref[pl.ds(row, 64), at] = g_ref[rows, :]
    turned_ref[...] = out_ref[...].T


def token_blocks(refs):
    own, other, left, right, left3, right3, far0, far1 = refs
    return [
        ((far0, 0), (far1, 0)),
        ((right3, 0), (right3, 1)),
        ((left3, 0), (left3, 1)),
        ((other, 0), (other, 1)),
        ((left3, 2), (right3, 2)),
        ((right, 0), (right, 1)),
        ((left, 0), (left, 1)),
        ((own, 0), (own, 1)),
    ]


def grad_blocks(refs):
    own, other, left, right, far_own, far_other = refs
    return [
        ((far_other, 0), (far_other, 1)),
        ((right, 2), (right, 3)),
        ((left, 2), (left, 3)),
        ((other, 0), (other, 1)),
        ((far_own, 0), (far_own, 1)),
        ((right, 0), (right, 1)),
        ((left, 0), (left, 1)),
        ((own, 0), (own, 1)),
    ]


def load_pair(back_ref, blocks, hold_ref):
    for half in range(2):
        want = back_ref[2 * pl.program_id(0) + half]
        for block, pair in enumerate(blocks):

            @pl.when(want == block)
            def _(pair=pair):
                for s, (ref, row) in enumerate(pair):
                    hold_ref[256 * s + 128 * half : 256 * s + 128 * half + 128, :] = ref[row]


def project_kernel(back_ref, *refs):
    token_refs, refs = refs[:8], refs[8:]
    w_ref, vec_ref, cos_ref, sin_ref = refs[:4]
    hid_ref, qkv_ref, act_ref, dgelu_ref, small_ref, hold_ref = refs[4:]

    @pl.when(pl.program_id(0) == 0)
    def _():
        total = vec_ref[0:64, :].astype(f32)
        for i in range(1, 16):
            total = total + vec_ref[64 * i : 64 * i + 64, :].astype(f32)
        small_ref[...] = jnp.concatenate([total[r : r + 1, :] for r in range(39)], axis=1)

    load_pair(back_ref, token_blocks(token_refs), hold_ref)
    gain, lbias = small_ref[:, 0:D], small_ref[:, D : 2 * D]
    bias = small_ref[:, 4 * D :]
    cosine, sine = cos_ref[...], sin_ref[...]
    for s in range(2):
        normed, _ = norm(hold_ref[256 * s : 256 * s + 256, :].astype(f32))
        hidden = (normed * gain + lbias).astype(bf16)
        proj = dot(hidden, w_ref[...]) + bias
        hid_ref[s] = hidden
        qkv_ref[s, :, 0:PAIR] = turn(proj[:, 0:PAIR], cosine, sine).astype(bf16)
        qkv_ref[s, :, PAIR : 2 * PAIR] = turn(proj[:, PAIR : 2 * PAIR], cosine, sine).astype(bf16)
        qkv_ref[s, :, 2 * PAIR : QKV] = proj[:, 2 * PAIR : QKV].astype(bf16)
        up = proj[:, QKV:]
        cdf = 0.5 * (1.0 + lax.erf(up * 0.7071067811865476))
        density = jnp.exp(-0.5 * up * up) * 0.3989422804014327
        act_ref[s] = (up * cdf).astype(bf16)
        dgelu_ref[s] = (cdf + up * density).astype(bf16)


def head_lanes(h):
    lane = lax.broadcasted_iota(jnp.int32, (1, PAIR), 1)
    return (lane < HEAD_DIM) if h == 0 else (lane >= HEAD_DIM)


def document_numbers(seg_row_ref):
    row = seg_row_ref[0].astype(f32)
    return row, jnp.broadcast_to(row, (PAIR, SEQ)).T[:, 0:1]


def allowed_mask(seg_row, seg_col, b, keys):
    key_pos = lax.broadcasted_iota(jnp.int32, (keys, QB), 0)
    query_pos = lax.broadcasted_iota(jnp.int32, (keys, QB), 1) + b * QB
    same = seg_col[0:keys] == seg_row[:, b * QB : (b + 1) * QB]
    return (key_pos <= query_pos) & same


def attend_kernel(qkv_ref, seg_row_ref, both_ref, att_ref, lse_ref):
    seg_row, seg_col = document_numbers(seg_row_ref)
    value_t = qkv_ref[:, 2 * PAIR : QKV].astype(f32).T.astype(bf16)
    for b in range(SEQ // QB):
        keys = (b + 1) * QB
        rows = slice(b * QB, (b + 1) * QB)
        allowed = allowed_mask(seg_row, seg_col, b, keys)
        query = qkv_ref[rows, 0:PAIR]
        mixed = []
        for h in range(2):
            q = jnp.where(head_lanes(h), query * 0.125, jnp.zeros_like(query))
            s = jnp.where(allowed, dot(qkv_ref[0:keys, PAIR : 2 * PAIR], q, NT), masked_score)
            top = jnp.max(s, axis=0, keepdims=True)
            e = jnp.exp(s - top)
            total = jnp.sum(e, axis=0, keepdims=True)
            p = (e * (1.0 / total)).astype(bf16)
            lse_ref[0, h : h + 1, rows] = top + jnp.log(total)
            mixed.append(dot(value_t[h * HEAD_DIM : (h + 1) * HEAD_DIM, 0:keys], p))
        att_ref[rows, :] = jnp.concatenate(mixed, axis=0).T.astype(bf16)


def attend_back_kernel(
    qkv_ref, da_ref, lse_ref, seg_row_ref, cos_ref, sin_ref, out_ref, sum_ref, dk_ref, dv_ref
):
    seg_row, seg_col = document_numbers(seg_row_ref)
    key_t = qkv_ref[:, PAIR : 2 * PAIR].astype(f32).T.astype(bf16)
    dk_ref[...] = jnp.zeros_like(dk_ref)
    dv_ref[...] = jnp.zeros_like(dv_ref)
    sums = jnp.zeros((1, PAIR), f32)
    for b in range(SEQ // QB):
        keys = (b + 1) * QB
        rows = slice(b * QB, (b + 1) * QB)
        allowed = allowed_mask(seg_row, seg_col, b, keys)
        query = qkv_ref[rows, 0:PAIR]
        grad = da_ref[rows, :]
        dq = []
        for h in range(2):
            q = jnp.where(head_lanes(h), query * 0.125, jnp.zeros_like(query))
            g = jnp.where(head_lanes(h), grad, jnp.zeros_like(grad))
            s = jnp.where(allowed, dot(qkv_ref[0:keys, PAIR : 2 * PAIR], q, NT), masked_score)
            soft = jnp.exp(s - lse_ref[0, h : h + 1, rows])
            dp = dot(qkv_ref[0:keys, 2 * PAIR : QKV], g, NT)
            t = soft * dp
            inner = jnp.sum(t, axis=0, keepdims=True)
            ds = (t - soft * inner).astype(bf16)
            dv_ref[0:keys, :] += dot(soft.astype(bf16), g)
            dk_ref[0:keys, :] += dot(ds, q)
            dq.append(dot(key_t[h * HEAD_DIM : (h + 1) * HEAD_DIM, 0:keys], ds))
        dq = jnp.concatenate(dq, axis=0).T * 0.125
        dq = turn(dq, cos_ref[rows, :], -sin_ref[rows, :]).astype(bf16)
        out_ref[rows, 0:PAIR] = dq
        sums += jnp.sum(dq.astype(f32), axis=0, keepdims=True)
    dk = turn(dk_ref[...], cos_ref[...], -sin_ref[...]).astype(bf16)
    dv = dv_ref[...].astype(bf16)
    out_ref[:, PAIR : 2 * PAIR] = dk
    out_ref[:, 2 * PAIR : QKV] = dv
    sum_ref[0, :, 0:PAIR] = sums
    sum_ref[0, :, PAIR : 2 * PAIR] = jnp.sum(dk.astype(f32), axis=0, keepdims=True)
    sum_ref[0, :, 2 * PAIR : QKV] = jnp.sum(dv.astype(f32), axis=0, keepdims=True)


def mix_kernel(left_ref, w_ref, out_ref):
    part = dot(left_ref[...], w_ref[...]).astype(bf16)
    out_ref[:, 0] = part.reshape(4, 128, D)


def far_kernel(left_ref, right_ref, own_ref, other_ref):
    own_ref[...] = left_ref[...]
    other_ref[...] = right_ref[...]


def back_out_kernel(back_ref, *refs):
    grad_refs, refs = refs[:6], refs[6:]
    w_ref, dgelu_ref, da_ref, dup_ref, g_ref, sum_ref, hold_ref = refs

    @pl.when(pl.program_id(0) == 0)
    def _():
        sum_ref[...] = jnp.zeros_like(sum_ref)

    load_pair(back_ref, grad_blocks(grad_refs), hold_ref)
    g = hold_ref[...]
    r = dot(g, w_ref[...])
    for s in range(2):
        part = slice(256 * s, 256 * s + 256)
        g_ref[s] = g[part]
        da_ref[s] = r[part, FFD:].astype(bf16)
        dup = (r[part, 0:FFD] * dgelu_ref[s].astype(f32)).astype(bf16)
        dup_ref[s] = dup
        sum_ref[...] += jnp.sum(dup.astype(f32), axis=0, keepdims=True)


def back_in_kernel(back_ref, *refs):
    token_refs, refs = refs[:8], refs[8:]
    dqkv_ref, dup_ref, w_ref = refs[:3]
    to_right, to_left, *outs = refs[3:11]
    sum_ref, hold_ref = refs[11:]

    @pl.when(pl.program_id(0) == 0)
    def _():
        sum_ref[...] = jnp.zeros_like(sum_ref)

    load_pair(back_ref, token_blocks(token_refs), hold_ref)
    left = [jnp.concatenate([dqkv_ref[s], dup_ref[s]], axis=1) for s in range(2)]
    grad = dot(jnp.concatenate(left, axis=0), w_ref[...], NT)
    low = grad.astype(bf16)
    for half in range(2):
        at = back_ref[2 * pl.program_id(0) + half]
        parts = [low[256 * s + 128 * half : 256 * s + 128 * half + 128] for s in range(2)]
        for block in range(8):

            @pl.when(at == block)
            def _(block=block, parts=parts):
                group, kind = block // 4, block % 4
                if kind == 0:
                    to_right[group] = parts[0]
                    to_left[group] = parts[1]
                else:
                    ref = outs[3 * group + kind - 1]
                    for s in range(2):
                        ref[s] = parts[s]

    normed, _ = norm(hold_ref[...].astype(f32))
    sum_ref[0:1, :] += jnp.sum(grad * normed, axis=0, keepdims=True)
    sum_ref[1:2, :] += jnp.sum(grad, axis=0, keepdims=True)


def fold_kernel(a_ref, b_ref, r0, l0, r1, l1, r0o, l0o, r1o, l1o):
    for g, (r, l, ro, lo) in enumerate(((r0, l0, r0o, l0o), (r1, l1, r1o, l1o))):
        ro[0] = add(r[0], a_ref[g])
        lo[0] = add(l[0], b_ref[g])


def token_grad_kernel(x_ref, g_ref, c_ref, a_ref, b_ref, e_ref, gain_ref, out_ref):
    for s in range(2):
        grad = c_ref[s].astype(f32) + a_ref[s].astype(f32) + b_ref[s].astype(f32) + e_ref[s].astype(f32)
        normed, inverse = norm(x_ref[s].astype(f32))
        n = grad * gain_ref[...]
        inner = n - jnp.mean(n, axis=1, keepdims=True) - normed * jnp.mean(n * normed, axis=1, keepdims=True)
        out_ref[s] = (g_ref[s].astype(f32) + inverse * inner).astype(bf16)


def chunk_kernel(place_ref, mix_ref, up_ref, qkv_ref, vec_ref, mine_ref, other_ref):
    for c in range(2):

        @pl.when(place_ref[2] == c)
        def _(c=c):
            for i in range(16):
                ref, at = (mine_ref if i % 2 == c else other_ref), i // 2
                b, cols = i // 8, slice(128 * (i % 8), 128 * (i % 8) + 128)
                ref[at, :, 0:128] = mix_ref[FFD + 64 * b : FFD + 64 * b + 64, cols]
                for m in range(4):
                    row = 256 * b + 64 * m
                    ref[at, :, 128 + 128 * m : 256 + 128 * m] = mix_ref[row : row + 64, cols]
                ref[at, :, OUT_ROWS : OUT_ROWS + FFD] = up_ref[64 * i : 64 * i + 64, :]
                ref[at, :, OUT_ROWS + FFD : SHARD - 128] = qkv_ref[64 * i : 64 * i + 64, :]
                ref[at, :, SHARD - 128 :] = vec_ref[...]


def pair_sum_kernel(mine_ref, got_ref, out_ref):
    out_ref[...] = add(mine_ref[...], got_ref[...])


def owner_sum_kernel(got_ref, out_ref, rest_ref):
    total = got_ref[0].astype(f32)
    for k in range(1, 8):
        total = total + got_ref[k].astype(f32)
    out_ref[...] = total[:, 0:OUT_ROWS].astype(bf16)
    rest_ref[...] = total[:, OUT_ROWS:].astype(bf16)


def finish_kernel(place_ref, got_ref, qkv_ref, up_ref, out_ref, down_ref, gain_ref, lbias_ref, bqkv_ref, bout_ref, bdown_ref, bup_ref, vec_ref, bq_ref, bu_ref):
    i = place_ref[1]
    total = jnp.zeros((64, 128), f32)
    for k in range(8):
        at = slice(128 * k, 128 * k + 128)
        out_ref[:, at] = got_ref[k, :, 0:128].astype(f32)
        for m in range(4):
            down_ref[64 * m : 64 * m + 64, at] = got_ref[k, :, 128 + 128 * m : 256 + 128 * m].astype(f32)
        up_ref[:, FFD * k : FFD * k + FFD] = got_ref[k, :, OUT_ROWS : OUT_ROWS + FFD].astype(f32)
        for t in range(3):
            start = OUT_ROWS + FFD + 128 * t
            qkv_ref[:, D * t + 128 * k : D * t + 128 * k + 128] = got_ref[k, :, start : start + 128].astype(f32)
        last = got_ref[k, :, SHARD - 128 :].astype(f32)
        for t in range(3):
            bq_ref[8 * t + k : 8 * t + k + 1, :] = last[24 + t : 25 + t, :]
        bu_ref[4 * k : 4 * k + 4, :] = last[27:31, :]
        total = total + last
    vec_ref[...] = total
    odd = i % 2 == 1

    def lanes(row):
        return jnp.where(odd, pltpu.roll(row, 64, 1), row)

    for n, refs in enumerate(((gain_ref,), (lbias_ref,), (bout_ref, bdown_ref))):
        for ref in refs:
            ref[...] = lanes(vec_ref[pl.ds(8 * n + i // 2, 1), :])[:, 0:64]
    start = (3 * i) // 2
    first, second = bq_ref[pl.ds(start, 1), :], bq_ref[pl.ds(start + 1, 1), :]
    lane = lax.broadcasted_iota(jnp.int32, (1, 128), 1)
    turned0, turned1 = pltpu.roll(first, 64, 1), pltpu.roll(second, 64, 1)
    bqkv_ref[:, 0:128] = jnp.where(odd, jnp.where(lane < 64, turned0, turned1), first)
    bqkv_ref[:, 128:192] = jnp.where(odd, turned1, second)[:, 0:64]
    bup_ref[:, 0:128] = bu_ref[pl.ds(2 * i, 1), :]
    bup_ref[:, 128:256] = bu_ref[pl.ds(2 * i + 1, 1), :]


def shape(dims, dtype):
    return jax.ShapeDtypeStruct(dims, dtype)


def rotary_tables():
    frequency = np.float32(10000.0) ** (np.float32(-2.0) * np.arange(HALF, dtype=np.float32) / np.float32(ROTARY))
    angles = np.arange(SEQ, dtype=np.float32)[:, None] * frequency.astype(np.float32)[None, :]
    cosine, sine = np.cos(angles.astype(np.float64)), np.sin(angles.astype(np.float64))
    one = np.ones((SEQ, HEAD_DIM - ROTARY))
    zero = np.zeros((SEQ, HEAD_DIM - ROTARY))
    cos = np.concatenate([cosine, cosine, one] * 2, axis=1)
    sin = np.concatenate([sine, sine, zero] * 2, axis=1)
    return [jnp.asarray(t.astype(np.float32)) for t in (cos, sin)]


def whole(dims):
    return pl.BlockSpec(dims, lambda i, *_: (0,) * len(dims), pipeline_mode=pl.Buffered(1))


def fixed(dims):
    return pl.BlockSpec(dims, lambda i, *_: (0,) * len(dims))


def body(tokens, segments, ln_gain, ln_bias, w_qkv, b_qkv, w_out, b_out, w_up, b_up, w_down, b_down, out_grad):
    j = lax.axis_index("yh") * 4 + lax.axis_index("x")
    i = lax.axis_index("z") * 4 + lax.axis_index("yl") * 2 + lax.axis_index("c")
    place = [j, i, lax.axis_index("c"), lax.axis_index("z"), lax.axis_index("yl")]
    place = jnp.stack(place).astype(jnp.int32)
    back = block_of()
    tokens_n = 2 * SEQ

    rows = lambda n, size=512: pl.BlockSpec((size, n), lambda i, *_: (i, 0))
    at_j = lambda dims, base=0: pl.BlockSpec(dims, lambda i, place: (0, base + place[0]))
    pairs = lambda n: pl.BlockSpec((2, 256, n), lambda i, *_: (0, i, 0))
    by_seq = lambda n: pl.BlockSpec((n, 1, 128, D), lambda i: (0, i, 0, 0))
    own_seq = pl.BlockSpec((1, 128, D), lambda i: (i, 0, 0))
    own_block = shape((2, 128, D), bf16)
    flat = lambda a: a.reshape(tokens_n, -1)
    line = lambda a: a

    other = shift(tokens, "yh", 1)
    left = shift(tokens, "x", 1)
    right = shift(tokens, "x", -1)
    g_sum = jnp.sum(out_grad.astype(f32), axis=(0, 1))
    piece = call(
        piece_kernel,
        "piece",
        (1,),
        [at_j((64, 128)), at_j((256, 128))],
        fixed((64, OUT_ROWS)),
        shape((64, OUT_ROWS), bf16),
        prefetch=1,
    )(place, w_out, w_down)
    piece = lax.ppermute(piece, ALL, out_pairs(False))
    shard = call(
        shard_kernel,
        "shard",
        (1,),
        [at_j((64, 128)), at_j((64, 128), 8), at_j((64, 128), 16), at_j((64, FFD)), whole((64, OUT_ROWS))]
        + [whole((n,)) for n in (64, 64, 192, 64, 256, 64)],
        fixed((64, SHARD)),
        shape((64, SHARD), bf16),
        prefetch=1,
    )(place, w_qkv, w_qkv, w_qkv, w_up, after(piece, left, right, other, g_sum, back), *[line(a) for a in (ln_gain, ln_bias, b_qkv, b_out, b_up, b_down)])
    w_all = lax.all_gather(shard, ("z", "yl", "c"), axis=0, tiled=True)

    g_other = shift(after(out_grad, left, right, other), "yh", 1)
    left3 = shift(jnp.concatenate([other, left[0:1]]), "x", 1)
    right3 = shift(jnp.concatenate([other, right[1:2]]), "x", -1)
    far0 = shift(after(left3, g_other)[0:1], "x", 1)
    far1 = shift(after(right3, g_other)[1:2], "x", -1)
    token_refs = (tokens, other, left, right, left3, right3, far0, far1)
    token_specs = [whole(a.shape) for a in token_refs]


    g_both = after(jnp.concatenate([out_grad, g_other]), far0, far1)
    g_left = shift(g_both, "x", 1)
    g_right = shift(g_both, "x", -1)

    cos, sin = rotary_tables()
    seg_row = segments[:, None, :]
    table = whole((SEQ, PAIR))

    hidden, qkv, activated, dgelu, small = call(
        project_kernel,
        "project",
        (4,),
        token_specs
        + [whole((D, IN_COLS)), pl.BlockSpec((D, 128), lambda i, *_: (0, 12))]
        + [pl.BlockSpec((256, PAIR), lambda i, *_: (i, 0))] * 2,
        [pairs(n) for n in (D, QKV, FFD, FFD)] + [fixed((1, 39 * 128))],
        [pltpu.HBM((2, SEQ, n), bf16) for n in (D, QKV, OUT_ROWS, FFD)] + [shape((1, 39 * 128), f32)],
        scratch=[pltpu.VMEM((512, D), bf16)],
        prefetch=1,
    )(back, *token_refs, w_all, w_all, cos, sin)

    seg_row_spec = pl.BlockSpec((1, 1, SEQ), lambda i: (i, 0, 0))
    lse_spec = pl.BlockSpec((1, 2, SEQ), lambda i: (i, 0, 0))
    act_att, lse = call(
        attend_kernel,
        "attend",
        (2,),
        [rows(QKV, SEQ), seg_row_spec, pl.BlockSpec(memory_space=pl.ANY)],
        [pl.BlockSpec((SEQ, PAIR), lambda i: (i, FFD // PAIR)), lse_spec],
        [pltpu.HBM((tokens_n, OUT_ROWS), bf16), shape((2, 2, SEQ), f32)],
        alias={2: 0},
    )(flat(qkv), seg_row, flat(activated))

    part = lambda first: pl.BlockSpec((1, 128, D), lambda i: (first + i, 0, 0))
    far_own, far_other = call(
        far_kernel,
        "far",
        (2,),
        [part(0), part(2)],
        [part(0)] * 2,
        [shape((2, 128, D), bf16)] * 2,
    )(after(g_left, act_att), after(g_right, act_att))
    far_own, far_other = shift(far_own, "x", 1), shift(far_other, "x", -1)
    grad_refs = (out_grad, g_other, g_left, g_right, far_own, far_other)

    w_mix, w_mix_turned = call(
        assemble_kernel,
        "assemble",
        (1,),
        [pl.BlockSpec((D, 128), functools.partial(lambda m, i: (0, m), 7 + m)) for m in range(5)],
        [fixed((OUT_ROWS, D)), fixed((D, OUT_ROWS))],
        [shape((OUT_ROWS, D), bf16), shape((D, OUT_ROWS), bf16)],
    )(*[w_all] * 5)
    parts = call(
        mix_kernel,
        "mix",
        (4,),
        [rows(OUT_ROWS), whole((OUT_ROWS, D))],
        pl.BlockSpec((4, 1, 128, D), lambda i: (i % 2, i // 2, 0, 0)),
        pltpu.HBM((8, 2, 128, D), bf16),
    )(act_att, w_mix)
    summed = lax.psum_scatter(parts, ("yh", "x"), scatter_dimension=0, tiled=True)[0]
    mixed = tokens.astype(f32) + summed.astype(f32) + (small[0, 2 * D : 3 * D] + small[0, 3 * D : 4 * D])
    mixed = mixed.astype(bf16)
    grad_attended, grad_up, g_rows, up_sums = call(
        back_out_kernel,
        "back_out",
        (4,),
        [whole(a.shape) for a in grad_refs] + [whole((D, OUT_ROWS)), pairs(FFD)],
        [pairs(PAIR), pairs(FFD), pairs(D), fixed((1, FFD))],
        [shape((2, SEQ, n), bf16) for n in (PAIR, FFD)] + [pltpu.HBM((2, SEQ, D), bf16)] + [shape((1, FFD), f32)],
        scratch=[pltpu.VMEM((512, D), bf16)],
        prefetch=1,
    )(after(back, parts), *grad_refs, w_mix_turned, dgelu)

    grad_qkv, qkv_sums = call(
        attend_back_kernel,
        "attend_back",
        (2,),
        [rows(QKV, SEQ), rows(PAIR, SEQ), lse_spec, seg_row_spec, table, table],
        [rows(QKV, SEQ), pl.BlockSpec((1, 1, QKV), lambda i: (i, 0, 0))],
        [shape((tokens_n, QKV), bf16), shape((2, 1, QKV), f32)],
        scratch=[pltpu.VMEM((SEQ, PAIR), f32), pltpu.VMEM((SEQ, PAIR), f32)],
    )(flat(qkv), flat(grad_attended), lse, seg_row, cos, sin)

    block = shape((2, 128, D), bf16)
    *sent, ln_sums = call(
        back_in_kernel,
        "back_in",
        (4,),
        token_specs + [pairs(QKV), pairs(FFD), whole((D, IN_COLS))],
        [fixed((2, 128, D))] * 8 + [fixed((2, D))],
        [pltpu.HBM((2, 128, D), bf16)] * 8 + [shape((2, D), f32)],
        scratch=[pltpu.VMEM((512, D), bf16)],
        prefetch=1,
    )(back, *token_refs, grad_qkv.reshape(2, SEQ, QKV), grad_up, w_all)

    to_right, to_left, right0, left0, own0, right1, left1, own1 = sent
    a = shift(to_right, "x", 1)
    b = shift(to_left, "x", -1)
    first = pl.BlockSpec((1, 128, D), lambda i: (0, 0, 0))
    second = pl.BlockSpec((1, 128, D), lambda i: (1, 0, 0))
    right0, left0, right1, left1 = call(
        fold_kernel,
        "fold",
        (1,),
        [whole((2, 128, D))] * 2 + [first, second, first, second],
        [first, second, first, second],
        [block] * 4,
        alias={2: 0, 3: 1, 4: 2, 5: 3},
    )(a, b, right0, left0, right1, left1)
    from_left0 = shift(right0, "x", 1)
    from_right0 = shift(left0, "x", -1)
    from_left1 = shift(right1, "x", 1)
    from_right1 = shift(left1, "x", -1)
    total = own0.astype(f32) + from_left0.astype(f32) + from_right0.astype(f32)
    from_other = shift(total.astype(bf16), "yh", 1)
    grad_tokens = call(
        token_grad_kernel,
        "token_grad",
        (1,),
        [whole((2, 128, D))] * 6 + [pl.BlockSpec((1, D), lambda i: (0, 0))],
        fixed((2, 128, D)),
        block,
    )(tokens, out_grad, own1, from_left1, from_right1, from_other, small)

    g_rows = after(flat(g_rows), to_right)
    hidden = after(flat(hidden), to_right)
    grad_mix = dot(act_att, g_rows, TN).astype(bf16)
    grad_w_up = dot(hidden, flat(grad_up), TN).astype(bf16)
    grad_w_qkv = dot(hidden, grad_qkv, TN).astype(bf16)
    vec = [ln_sums.reshape(16, 128), g_sum.reshape(8, 128), jnp.sum(qkv_sums, axis=0).reshape(3, 128), up_sums.reshape(4, 128)]
    vec = jnp.pad(jnp.concatenate(vec).astype(bf16), ((0, 33), (0, 0)))
    halves = shape((8, 64, SHARD), bf16)
    own_half, other_half = call(
        chunk_kernel,
        "chunk",
        (1,),
        [whole((OUT_ROWS, D)), whole((D, FFD)), whole((D, QKV)), whole((64, 128))],
        [fixed(halves.shape)] * 2,
        [halves] * 2,
        prefetch=1,
    )(place, after(grad_mix, a, b), grad_w_up, grad_w_qkv, vec)
    got = shift(other_half, "c", 1)
    quarter = pl.BlockSpec((2, 64, SHARD), lambda i: (i, 0, 0))
    chip_half = call(pair_sum_kernel, "pair_sum", (4,), [quarter] * 2, quarter, halves)(own_half, got)
    got = lax.all_to_all(after(chip_half, right0, left0), ("z", "yl"), 0, 0, tiled=True)
    out_owned, rest_owned = call(
        owner_sum_kernel,
        "owner_sum",
        (1,),
        [whole(halves.shape)],
        [fixed((64, OUT_ROWS)), fixed((64, SHARD - OUT_ROWS))],
        [shape((64, OUT_ROWS), bf16), shape((64, SHARD - OUT_ROWS), bf16)],
    )(got)
    out_owned = lax.ppermute(out_owned, ALL, out_pairs(True))

    def spread_ctx(a):
        return lax.all_to_all(jnp.broadcast_to(a[None], (8,) + a.shape), ("yh", "x"), 0, 0, tiled=True)

    both = spread_ctx(after(jnp.concatenate([out_owned, rest_owned], axis=1), from_left1, from_right1, from_other))
    sizes = [(64, 3 * D), (64, 4 * D), (64, D), (256, D), (1, 64), (1, 64), (1, 192), (1, 64), (1, 64), (1, 256)]
    done = call(
        finish_kernel,
        "finish",
        (1,),
        [fixed((8, 64, SHARD))],
        [fixed(dims) for dims in sizes],
        [shape(dims, f32) for dims in sizes],
        scratch=[pltpu.VMEM((64, 128), f32), pltpu.VMEM((32, 128), f32), pltpu.VMEM((32, 128), f32)],
        prefetch=1,
    )(place, after(both, mixed))
    grad_w_qkv, grad_w_up, grad_w_out, grad_w_down = done[:4]
    grad_gain, grad_lbias, grad_bqkv, grad_bout, grad_bdown, grad_bup = [a.reshape(-1) for a in done[4:]]
    return (
        mixed,
        grad_tokens,
        grad_gain,
        grad_lbias,
        grad_w_qkv,
        grad_bqkv,
        grad_w_out,
        grad_bout,
        grad_w_up,
        grad_bup,
        grad_w_down,
        grad_bdown,
    )


def solution(mesh):
    fine = Mesh(mesh.devices.reshape(4, 2, 2, 2, 4), ALL)
    dp = ("z", "yl", "c")
    ctx = ("yh", "x")
    in_specs = (
        P(dp, ctx, None),
        P(dp, None),
        P(dp),
        P(dp),
        P(dp, None),
        P(dp),
        P(dp, None),
        P(dp),
        P(dp, None),
        P(dp),
        P(dp, None),
        P(dp),
        P(dp, ctx, None),
    )
    out_specs = (
        P(dp, ctx, None),
        P(dp, ctx, None),
        P(dp),
        P(dp),
        P(dp, None),
        P(dp),
        P(dp, None),
        P(dp),
        P(dp, None),
        P(dp),
        P(dp, None),
        P(dp),
    )
    return jax.shard_map(body, mesh=fine, in_specs=in_specs, out_specs=out_specs, check_vma=False)
```

```python
import functools

import jax
import jax.numpy as jnp
import numpy as np
from jax import lax
from jax.experimental import pallas as pl
from jax.experimental.pallas import tpu as pltpu
from jax.sharding import Mesh
from jax.sharding import PartitionSpec as P

HEAD_DIM = 64
ROTARY = 32
HALF = ROTARY // 2
SEQ = 1024
D = 1024
PAIR = 128
FFD = 512
QKV = 3 * PAIR
IN_COLS = QKV + FFD
OUT_ROWS = PAIR + FFD
QB = 256

norm_epsilon = 1e-05
masked_score = -1e30
f32 = jnp.float32
bf16 = jnp.bfloat16
NT = (((1,), (1,)), ((), ()))
NN = (((1,), (0,)), ((), ()))
VMEM_LIMIT = 30 * 1024 * 1024
MIB = dict(shard=60, piece=60, project=60, attend=52, assemble=16, mix=16, back_out=60, attend_back=20, back_in=20, chunk=16, fold=16, column_sum=16, far=16, pair_sum=16, owner_sum=16, finish=16, token_grad=16)
TN = (((0,), (0,)), ((), ()))
SHARD = IN_COLS + OUT_ROWS + 128
SCALE = 0.3
COST = dict(shard=2, piece=1, project=13, attend=11, assemble=3, mix=6, back_out=9, attend_back=13, back_in=14, fold=2, token_grad=3, chunk=4, pair_sum=3, owner_sum=2, finish=3)


def dot(a, b, dims=NN):
    return lax.dot_general(a, b, dims, preferred_element_type=f32)


def call(kernel, name, grid, in_specs, out_specs, out_shape, scratch=(), prefetch=0, alias=None):
    return pl.pallas_call(
        kernel,
        name=name,
        grid_spec=pltpu.PrefetchScalarGridSpec(
            num_scalar_prefetch=prefetch,
            grid=grid,
            in_specs=in_specs,
            out_specs=out_specs,
            scratch_shapes=scratch,
        ),
        out_shape=out_shape,
        input_output_aliases=alias or {},
        compiler_params=pltpu.CompilerParams(
            dimension_semantics=("arbitrary",) * len(grid), vmem_limit_bytes=int(MIB.get(name, 52) * 1024 * 1024)
        ),
        cost_estimate=pl.CostEstimate(flops=int(COST.get(name, 1) * 1e9 * SCALE), bytes_accessed=int(COST.get(name, 1) * 1000000 * SCALE), transcendentals=0),
    )


ALL = ("z", "yl", "c", "yh", "x")


def shift(x, axis, by):
    count = lax.axis_size(axis)
    return lax.ppermute(x, axis, [(i, (i + by) % count) for i in range(count)])


def after(x, *others):
    return lax.optimization_barrier((x,) + others)[0]


def add(a, b):
    return (a.astype(f32) + b.astype(f32)).astype(bf16)


def block_of():
    at = jnp.arange(8, dtype=jnp.int32)
    same = (at // 4) == lax.axis_index("yh")
    step = (at % 4 - lax.axis_index("x")) % 4
    kind = jnp.where(step == 0, 3, jnp.where(step == 1, 1, jnp.where(step == 2, 0, 2)))
    return (jnp.where(same, 4, 0) + kind).astype(jnp.int32)


def out_pairs(back):
    pairs = []
    for j in range(8):
        for b in range(2):
            for k in range(8):
                pairs.append(((2 * j + b) * 8 + k, (8 * b + k) * 8 + j))
    return [(t, s) for s, t in pairs] if back else pairs


def turn(v, cosine, sine):
    lane = lax.broadcasted_iota(jnp.int32, (1, PAIR), 1) % HEAD_DIM
    crossed = jnp.where(lane < HALF, -pltpu.roll(v, PAIR - HALF, 1), pltpu.roll(v, HALF, 1))
    return v * cosine + crossed * sine


def norm(x):
    center = x - jnp.mean(x, axis=1, keepdims=True)
    inverse = lax.rsqrt(jnp.mean(center * center, axis=1, keepdims=True) + norm_epsilon)
    return center * inverse, inverse


def piece_kernel(place_ref, out_ref, down_ref, piece_ref):
    piece_ref[:, 0:128] = out_ref[...]
    for m in range(4):
        piece_ref[:, 128 + 128 * m : 256 + 128 * m] = down_ref[64 * m : 64 * m + 64, :]


def spread(row, size, offset):
    n = row.shape[0]
    row = row.reshape(1, n)
    v = lax.broadcasted_iota(jnp.int32, (n, size), 0)
    t = lax.broadcasted_iota(jnp.int32, (n, size), 1)
    return dot(row, jnp.where(offset(t) == v, 1.0, 0.0).astype(bf16))


def shard_kernel(place_ref, q_ref, k_ref, v_ref, up_ref, piece_ref, gain_ref, lbias_ref, bqkv_ref, bout_ref, bup_ref, bdown_ref, shard_ref):
    j, i = place_ref[0], place_ref[1]
    shard_ref[:, 0:128] = q_ref[...]
    shard_ref[:, 128:256] = k_ref[...]
    shard_ref[:, 256:384] = v_ref[...]
    shard_ref[:, QKV:IN_COLS] = up_ref[...]
    shard_ref[:, IN_COLS : IN_COLS + OUT_ROWS] = piece_ref[...]
    rows = []
    for ref in (gain_ref, lbias_ref, bout_ref, bdown_ref):
        rows.append(spread(ref[...], D, lambda t: t - 64 * i))
    rows.append(spread(bqkv_ref[...], QKV, lambda t: (t // 128) * D + 128 * j + t % 128 - 192 * i))
    rows.append(spread(bup_ref[...], FFD, lambda t: t + FFD * j - 256 * i))
    row = jnp.concatenate(rows, axis=1)
    count = row.shape[1] // 128
    table = jnp.concatenate([row[:, 128 * r : 128 * r + 128] for r in range(count)] + [jnp.zeros((64 - count, 128), f32)], axis=0)
    shard_ref[:, IN_COLS + OUT_ROWS :] = table.astype(bf16)


def assemble_kernel(g0, g1, g2, g3, g4, out_ref, turned_ref):
    for i in range(16):
        b, k = i // 8, i % 8
        rows = pl.ds(64 * i, 64)
        at = pl.ds(128 * k, 128)
        for m, g_ref in enumerate((g0, g1, g2, g3, g4)):
            row = FFD + 64 * b if m == 0 else 256 * b + 64 * (m - 1)
            out_ref[pl.ds(row, 64), at] = g_ref[rows, :]
    turned_ref[...] = out_ref[...].T


def token_blocks(refs):
    own, other, left, right, left3, right3, far0, far1 = refs
    return [
        ((far0, 0), (far1, 0)),
        ((right3, 0), (right3, 1)),
        ((left3, 0), (left3, 1)),
        ((other, 0), (other, 1)),
        ((left3, 2), (right3, 2)),
        ((right, 0), (right, 1)),
        ((left, 0), (left, 1)),
        ((own, 0), (own, 1)),
    ]


def grad_blocks(refs):
    own, other, left, right, far_own, far_other = refs
    return [
        ((far_other, 0), (far_other, 1)),
        ((right, 2), (right, 3)),
        ((left, 2), (left, 3)),
        ((other, 0), (other, 1)),
        ((far_own, 0), (far_own, 1)),
        ((right, 0), (right, 1)),
        ((left, 0), (left, 1)),
        ((own, 0), (own, 1)),
    ]


def load_pair(back_ref, blocks, hold_ref):
    for half in range(2):
        want = back_ref[2 * pl.program_id(0) + half]
        for block, pair in enumerate(blocks):

            @pl.when(want == block)
            def _(pair=pair):
                for s, (ref, row) in enumerate(pair):
                    hold_ref[256 * s + 128 * half : 256 * s + 128 * half + 128, :] = ref[row]


def project_kernel(back_ref, *refs):
    token_refs, refs = refs[:8], refs[8:]
    w_ref, vec_ref, cos_ref, sin_ref = refs[:4]
    hid_ref, qkv_ref, act_ref, dgelu_ref, small_ref, hold_ref = refs[4:]

    @pl.when(pl.program_id(0) == 0)
    def _():
        total = vec_ref[0:64, :].astype(f32)
        for i in range(1, 16):
            total = total + vec_ref[64 * i : 64 * i + 64, :].astype(f32)
        small_ref[...] = jnp.concatenate([total[r : r + 1, :] for r in range(39)], axis=1)

    load_pair(back_ref, token_blocks(token_refs), hold_ref)
    gain, lbias = small_ref[:, 0:D], small_ref[:, D : 2 * D]
    bias = small_ref[:, 4 * D :]
    cosine, sine = cos_ref[...], sin_ref[...]
    for s in range(2):
        normed, _ = norm(hold_ref[256 * s : 256 * s + 256, :].astype(f32))
        hidden = (normed * gain + lbias).astype(bf16)
        proj = dot(hidden, w_ref[...]) + bias
        hid_ref[s] = hidden
        qkv_ref[s, :, 0:PAIR] = turn(proj[:, 0:PAIR], cosine, sine).astype(bf16)
        qkv_ref[s, :, PAIR : 2 * PAIR] = turn(proj[:, PAIR : 2 * PAIR], cosine, sine).astype(bf16)
        qkv_ref[s, :, 2 * PAIR : QKV] = proj[:, 2 * PAIR : QKV].astype(bf16)
        up = proj[:, QKV:]
        cdf = 0.5 * (1.0 + lax.erf(up * 0.7071067811865476))
        density = jnp.exp(-0.5 * up * up) * 0.3989422804014327
        act_ref[s] = (up * cdf).astype(bf16)
        dgelu_ref[s] = (cdf + up * density).astype(bf16)


def head_lanes(h):
    lane = lax.broadcasted_iota(jnp.int32, (1, PAIR), 1)
    return (lane < HEAD_DIM) if h == 0 else (lane >= HEAD_DIM)


def document_numbers(seg_row_ref):
    row = seg_row_ref[0].astype(f32)
    return row, jnp.broadcast_to(row, (PAIR, SEQ)).T[:, 0:1]


def allowed_mask(seg_row, seg_col, b, keys):
    key_pos = lax.broadcasted_iota(jnp.int32, (keys, QB), 0)
    query_pos = lax.broadcasted_iota(jnp.int32, (keys, QB), 1) + b * QB
    same = seg_col[0:keys] == seg_row[:, b * QB : (b + 1) * QB]
    return (key_pos <= query_pos) & same


def attend_kernel(qkv_ref, seg_row_ref, both_ref, att_ref, lse_ref):
    seg_row, seg_col = document_numbers(seg_row_ref)
    value_t = qkv_ref[:, 2 * PAIR : QKV].astype(f32).T.astype(bf16)
    for b in range(SEQ // QB):
        keys = (b + 1) * QB
        rows = slice(b * QB, (b + 1) * QB)
        allowed = allowed_mask(seg_row, seg_col, b, keys)
        query = qkv_ref[rows, 0:PAIR]
        mixed = []
        for h in range(2):
            q = jnp.where(head_lanes(h), query * 0.125, jnp.zeros_like(query))
            s = jnp.where(allowed, dot(qkv_ref[0:keys, PAIR : 2 * PAIR], q, NT), masked_score)
            top = jnp.max(s, axis=0, keepdims=True)
            e = jnp.exp(s - top)
            total = jnp.sum(e, axis=0, keepdims=True)
            p = (e * (1.0 / total)).astype(bf16)
            lse_ref[0, h : h + 1, rows] = top + jnp.log(total)
            mixed.append(dot(value_t[h * HEAD_DIM : (h + 1) * HEAD_DIM, 0:keys], p))
        att_ref[rows, :] = jnp.concatenate(mixed, axis=0).T.astype(bf16)


def attend_back_kernel(
    qkv_ref, da_ref, lse_ref, seg_row_ref, cos_ref, sin_ref, out_ref, sum_ref, dk_ref, dv_ref
):
    seg_row, seg_col = document_numbers(seg_row_ref)
    key_t = qkv_ref[:, PAIR : 2 * PAIR].astype(f32).T.astype(bf16)
    dk_ref[...] = jnp.zeros_like(dk_ref)
    dv_ref[...] = jnp.zeros_like(dv_ref)
    sums = jnp.zeros((1, PAIR), f32)
    for b in range(SEQ // QB):
        keys = (b + 1) * QB
        rows = slice(b * QB, (b + 1) * QB)
        allowed = allowed_mask(seg_row, seg_col, b, keys)
        query = qkv_ref[rows, 0:PAIR]
        grad = da_ref[rows, :]
        dq = []
        for h in range(2):
            q = jnp.where(head_lanes(h), query * 0.125, jnp.zeros_like(query))
            g = jnp.where(head_lanes(h), grad, jnp.zeros_like(grad))
            s = jnp.where(allowed, dot(qkv_ref[0:keys, PAIR : 2 * PAIR], q, NT), masked_score)
            soft = jnp.exp(s - lse_ref[0, h : h + 1, rows])
            dp = dot(qkv_ref[0:keys, 2 * PAIR : QKV], g, NT)
            t = soft * dp
            inner = jnp.sum(t, axis=0, keepdims=True)
            ds = (t - soft * inner).astype(bf16)
            dv_ref[0:keys, :] += dot(soft.astype(bf16), g)
            dk_ref[0:keys, :] += dot(ds, q)
            dq.append(dot(key_t[h * HEAD_DIM : (h + 1) * HEAD_DIM, 0:keys], ds))
        dq = jnp.concatenate(dq, axis=0).T * 0.125
        dq = turn(dq, cos_ref[rows, :], -sin_ref[rows, :]).astype(bf16)
        out_ref[rows, 0:PAIR] = dq
        sums += jnp.sum(dq.astype(f32), axis=0, keepdims=True)
    dk = turn(dk_ref[...], cos_ref[...], -sin_ref[...]).astype(bf16)
    dv = dv_ref[...].astype(bf16)
    out_ref[:, PAIR : 2 * PAIR] = dk
    out_ref[:, 2 * PAIR : QKV] = dv
    sum_ref[0, :, 0:PAIR] = sums
    sum_ref[0, :, PAIR : 2 * PAIR] = jnp.sum(dk.astype(f32), axis=0, keepdims=True)
    sum_ref[0, :, 2 * PAIR : QKV] = jnp.sum(dv.astype(f32), axis=0, keepdims=True)


def mix_kernel(left_ref, w_ref, out_ref):
    part = dot(left_ref[...], w_ref[...]).astype(bf16)
    out_ref[:, 0] = part.reshape(4, 128, D)


def far_kernel(left_ref, right_ref, own_ref, other_ref):
    own_ref[...] = left_ref[...]
    other_ref[...] = right_ref[...]


def back_out_kernel(back_ref, *refs):
    grad_refs, refs = refs[:6], refs[6:]
    w_ref, dgelu_ref, da_ref, dup_ref, g_ref, sum_ref, hold_ref = refs

    @pl.when(pl.program_id(0) == 0)
    def _():
        sum_ref[...] = jnp.zeros_like(sum_ref)

    load_pair(back_ref, grad_blocks(grad_refs), hold_ref)
    g = hold_ref[...]
    r = dot(g, w_ref[...])
    for s in range(2):
        part = slice(256 * s, 256 * s + 256)
        g_ref[s] = g[part]
        da_ref[s] = r[part, FFD:].astype(bf16)
        dup = (r[part, 0:FFD] * dgelu_ref[s].astype(f32)).astype(bf16)
        dup_ref[s] = dup
        sum_ref[...] += jnp.sum(dup.astype(f32), axis=0, keepdims=True)


def back_in_kernel(back_ref, *refs):
    token_refs, refs = refs[:8], refs[8:]
    dqkv_ref, dup_ref, w_ref = refs[:3]
    to_right, to_left, *outs = refs[3:11]
    sum_ref, hold_ref = refs[11:]

    @pl.when(pl.program_id(0) == 0)
    def _():
        sum_ref[...] = jnp.zeros_like(sum_ref)

    load_pair(back_ref, token_blocks(token_refs), hold_ref)
    left = [jnp.concatenate([dqkv_ref[s], dup_ref[s]], axis=1) for s in range(2)]
    grad = dot(jnp.concatenate(left, axis=0), w_ref[...], NT)
    low = grad.astype(bf16)
    for half in range(2):
        at = back_ref[2 * pl.program_id(0) + half]
        parts = [low[256 * s + 128 * half : 256 * s + 128 * half + 128] for s in range(2)]
        for block in range(8):

            @pl.when(at == block)
            def _(block=block, parts=parts):
                group, kind = block // 4, block % 4
                if kind == 0:
                    to_right[group] = parts[0]
                    to_left[group] = parts[1]
                else:
                    ref = outs[3 * group + kind - 1]
                    for s in range(2):
                        ref[s] = parts[s]

    normed, _ = norm(hold_ref[...].astype(f32))
    sum_ref[0:1, :] += jnp.sum(grad * normed, axis=0, keepdims=True)
    sum_ref[1:2, :] += jnp.sum(grad, axis=0, keepdims=True)


def fold_kernel(a_ref, b_ref, r0, l0, r1, l1, r0o, l0o, r1o, l1o):
    for g, (r, l, ro, lo) in enumerate(((r0, l0, r0o, l0o), (r1, l1, r1o, l1o))):
        ro[0] = add(r[0], a_ref[g])
        lo[0] = add(l[0], b_ref[g])


def column_sum_kernel(own_ref, left_ref, right_ref, out_ref):
    out_ref[...] = (own_ref[...].astype(f32) + left_ref[...].astype(f32) + right_ref[...].astype(f32)).astype(bf16)


def token_grad_kernel(x_ref, g_ref, c_ref, a_ref, b_ref, e_ref, gain_ref, out_ref):
    for s in range(2):
        grad = c_ref[s].astype(f32) + a_ref[s].astype(f32) + b_ref[s].astype(f32) + e_ref[s].astype(f32)
        normed, inverse = norm(x_ref[s].astype(f32))
        n = grad * gain_ref[...]
        inner = n - jnp.mean(n, axis=1, keepdims=True) - normed * jnp.mean(n * normed, axis=1, keepdims=True)
        out_ref[s] = (g_ref[s].astype(f32) + inverse * inner).astype(bf16)


def chunk_kernel(place_ref, mix_ref, up_ref, qkv_ref, vec_ref, mine_ref, other_ref):
    for c in range(2):

        @pl.when(place_ref[2] == c)
        def _(c=c):
            for i in range(16):
                ref, at = (mine_ref if i % 2 == c else other_ref), i // 2
                b, cols = i // 8, slice(128 * (i % 8), 128 * (i % 8) + 128)
                ref[at, :, 0:128] = mix_ref[FFD + 64 * b : FFD + 64 * b + 64, cols]
                for m in range(4):
                    row = 256 * b + 64 * m
                    ref[at, :, 128 + 128 * m : 256 + 128 * m] = mix_ref[row : row + 64, cols]
                ref[at, :, OUT_ROWS : OUT_ROWS + FFD] = up_ref[64 * i : 64 * i + 64, :]
                ref[at, :, OUT_ROWS + FFD : SHARD - 128] = qkv_ref[64 * i : 64 * i + 64, :]
                ref[at, :, SHARD - 128 :] = vec_ref[...]


def pair_sum_kernel(mine_ref, got_ref, out_ref):
    out_ref[...] = add(mine_ref[...], got_ref[...])


def owner_sum_kernel(got_ref, out_ref, rest_ref):
    total = got_ref[0].astype(f32)
    for k in range(1, 8):
        total = total + got_ref[k].astype(f32)
    out_ref[...] = total[:, 0:OUT_ROWS].astype(bf16)
    rest_ref[...] = total[:, OUT_ROWS:].astype(bf16)


def finish_kernel(place_ref, got_ref, qkv_ref, up_ref, out_ref, down_ref, gain_ref, lbias_ref, bqkv_ref, bout_ref, bdown_ref, bup_ref, vec_ref, bq_ref, bu_ref):
    i = place_ref[1]
    total = jnp.zeros((64, 128), f32)
    for k in range(8):
        at = slice(128 * k, 128 * k + 128)
        out_ref[:, at] = got_ref[k, :, 0:128].astype(f32)
        for m in range(4):
            down_ref[64 * m : 64 * m + 64, at] = got_ref[k, :, 128 + 128 * m : 256 + 128 * m].astype(f32)
        up_ref[:, FFD * k : FFD * k + FFD] = got_ref[k, :, OUT_ROWS : OUT_ROWS + FFD].astype(f32)
        for t in range(3):
            start = OUT_ROWS + FFD + 128 * t
            qkv_ref[:, D * t + 128 * k : D * t + 128 * k + 128] = got_ref[k, :, start : start + 128].astype(f32)
        last = got_ref[k, :, SHARD - 128 :].astype(f32)
        for t in range(3):
            bq_ref[8 * t + k : 8 * t + k + 1, :] = last[24 + t : 25 + t, :]
        bu_ref[4 * k : 4 * k + 4, :] = last[27:31, :]
        total = total + last
    vec_ref[...] = total
    odd = i % 2 == 1

    def lanes(row):
        return jnp.where(odd, pltpu.roll(row, 64, 1), row)

    for n, refs in enumerate(((gain_ref,), (lbias_ref,), (bout_ref, bdown_ref))):
        for ref in refs:
            ref[...] = lanes(vec_ref[pl.ds(8 * n + i // 2, 1), :])[:, 0:64]
    start = (3 * i) // 2
    first, second = bq_ref[pl.ds(start, 1), :], bq_ref[pl.ds(start + 1, 1), :]
    lane = lax.broadcasted_iota(jnp.int32, (1, 128), 1)
    turned0, turned1 = pltpu.roll(first, 64, 1), pltpu.roll(second, 64, 1)
    bqkv_ref[:, 0:128] = jnp.where(odd, jnp.where(lane < 64, turned0, turned1), first)
    bqkv_ref[:, 128:192] = jnp.where(odd, turned1, second)[:, 0:64]
    bup_ref[:, 0:128] = bu_ref[pl.ds(2 * i, 1), :]
    bup_ref[:, 128:256] = bu_ref[pl.ds(2 * i + 1, 1), :]


def shape(dims, dtype):
    return jax.ShapeDtypeStruct(dims, dtype)


def rotary_tables():
    frequency = np.float32(10000.0) ** (np.float32(-2.0) * np.arange(HALF, dtype=np.float32) / np.float32(ROTARY))
    angles = np.arange(SEQ, dtype=np.float32)[:, None] * frequency.astype(np.float32)[None, :]
    cosine, sine = np.cos(angles.astype(np.float64)), np.sin(angles.astype(np.float64))
    one = np.ones((SEQ, HEAD_DIM - ROTARY))
    zero = np.zeros((SEQ, HEAD_DIM - ROTARY))
    cos = np.concatenate([cosine, cosine, one] * 2, axis=1)
    sin = np.concatenate([sine, sine, zero] * 2, axis=1)
    return [jnp.asarray(t.astype(np.float32)) for t in (cos, sin)]


def whole(dims):
    return pl.BlockSpec(dims, lambda i, *_: (0,) * len(dims), pipeline_mode=pl.Buffered(1))


def fixed(dims):
    return pl.BlockSpec(dims, lambda i, *_: (0,) * len(dims))


def body(tokens, segments, ln_gain, ln_bias, w_qkv, b_qkv, w_out, b_out, w_up, b_up, w_down, b_down, out_grad):
    j = lax.axis_index("yh") * 4 + lax.axis_index("x")
    i = lax.axis_index("z") * 4 + lax.axis_index("yl") * 2 + lax.axis_index("c")
    place = [j, i, lax.axis_index("c"), lax.axis_index("z"), lax.axis_index("yl")]
    place = jnp.stack(place).astype(jnp.int32)
    back = block_of()
    tokens_n = 2 * SEQ

    rows = lambda n, size=512: pl.BlockSpec((size, n), lambda i, *_: (i, 0))
    at_j = lambda dims, base=0: pl.BlockSpec(dims, lambda i, place: (0, base + place[0]))
    pairs = lambda n: pl.BlockSpec((2, 256, n), lambda i, *_: (0, i, 0))
    by_seq = lambda n: pl.BlockSpec((n, 1, 128, D), lambda i: (0, i, 0, 0))
    own_seq = pl.BlockSpec((1, 128, D), lambda i: (i, 0, 0))
    own_block = shape((2, 128, D), bf16)
    flat = lambda a: a.reshape(tokens_n, -1)
    line = lambda a: a

    other = shift(tokens, "yh", 1)
    left = shift(tokens, "x", 1)
    right = shift(tokens, "x", -1)
    g_sum = jnp.sum(out_grad.astype(f32), axis=(0, 1))
    piece = call(
        piece_kernel,
        "piece",
        (1,),
        [at_j((64, 128)), at_j((256, 128))],
        fixed((64, OUT_ROWS)),
        shape((64, OUT_ROWS), bf16),
        prefetch=1,
    )(place, w_out, w_down)
    piece = lax.ppermute(piece, ALL, out_pairs(False))
    shard = call(
        shard_kernel,
        "shard",
        (1,),
        [at_j((64, 128)), at_j((64, 128), 8), at_j((64, 128), 16), at_j((64, FFD)), whole((64, OUT_ROWS))]
        + [whole((n,)) for n in (64, 64, 192, 64, 256, 64)],
        fixed((64, SHARD)),
        shape((64, SHARD), bf16),
        prefetch=1,
    )(place, w_qkv, w_qkv, w_qkv, w_up, after(piece, left, right, other, g_sum, back), *[line(a) for a in (ln_gain, ln_bias, b_qkv, b_out, b_up, b_down)])
    w_all = lax.all_gather(shard, ("z", "yl", "c"), axis=0, tiled=True)

    g_other = shift(after(out_grad, left, right, other), "yh", 1)
    left3 = shift(jnp.concatenate([other, left[0:1]]), "x", 1)
    right3 = shift(jnp.concatenate([other, right[1:2]]), "x", -1)
    far0 = shift(after(left3, g_other)[0:1], "x", 1)
    far1 = shift(after(right3, g_other)[1:2], "x", -1)
    token_refs = (tokens, other, left, right, left3, right3, far0, far1)
    token_specs = [whole(a.shape) for a in token_refs]


    g_both = after(jnp.concatenate([out_grad, g_other]), far0, far1)
    g_left = shift(g_both, "x", 1)
    g_right = shift(g_both, "x", -1)

    cos, sin = rotary_tables()
    seg_row = segments[:, None, :]
    table = whole((SEQ, PAIR))

    hidden, qkv, activated, dgelu, small = call(
        project_kernel,
        "project",
        (4,),
        token_specs
        + [whole((D, IN_COLS)), pl.BlockSpec((D, 128), lambda i, *_: (0, 12))]
        + [pl.BlockSpec((256, PAIR), lambda i, *_: (i, 0))] * 2,
        [pairs(n) for n in (D, QKV, FFD, FFD)] + [fixed((1, 39 * 128))],
        [pltpu.HBM((2, SEQ, n), bf16) for n in (D, QKV, OUT_ROWS, FFD)] + [shape((1, 39 * 128), f32)],
        scratch=[pltpu.VMEM((512, D), bf16)],
        prefetch=1,
    )(back, *token_refs, w_all, w_all, cos, sin)

    seg_row_spec = pl.BlockSpec((1, 1, SEQ), lambda i: (i, 0, 0))
    lse_spec = pl.BlockSpec((1, 2, SEQ), lambda i: (i, 0, 0))
    act_att, lse = call(
        attend_kernel,
        "attend",
        (2,),
        [rows(QKV, SEQ), seg_row_spec, pl.BlockSpec(memory_space=pl.ANY)],
        [pl.BlockSpec((SEQ, PAIR), lambda i: (i, FFD // PAIR)), lse_spec],
        [pltpu.HBM((tokens_n, OUT_ROWS), bf16), shape((2, 2, SEQ), f32)],
        alias={2: 0},
    )(flat(qkv), seg_row, flat(activated))

    part = lambda first: pl.BlockSpec((1, 128, D), lambda i: (first + i, 0, 0))
    far_own, far_other = call(
        far_kernel,
        "far",
        (2,),
        [part(0), part(2)],
        [part(0)] * 2,
        [shape((2, 128, D), bf16)] * 2,
    )(after(g_left, act_att), after(g_right, act_att))
    far_own, far_other = shift(far_own, "x", 1), shift(far_other, "x", -1)
    grad_refs = (out_grad, g_other, g_left, g_right, far_own, far_other)

    w_mix, w_mix_turned = call(
        assemble_kernel,
        "assemble",
        (1,),
        [pl.BlockSpec((D, 128), functools.partial(lambda m, i: (0, m), 7 + m)) for m in range(5)],
        [fixed((OUT_ROWS, D)), fixed((D, OUT_ROWS))],
        [shape((OUT_ROWS, D), bf16), shape((D, OUT_ROWS), bf16)],
    )(*[w_all] * 5)
    parts = call(
        mix_kernel,
        "mix",
        (4,),
        [rows(OUT_ROWS), whole((OUT_ROWS, D))],
        pl.BlockSpec((4, 1, 128, D), lambda i: (i % 2, i // 2, 0, 0)),
        pltpu.HBM((8, 2, 128, D), bf16),
    )(act_att, w_mix)
    summed = lax.psum_scatter(parts, ("yh", "x"), scatter_dimension=0, tiled=True)[0]
    mixed = tokens.astype(f32) + summed.astype(f32) + (small[0, 2 * D : 3 * D] + small[0, 3 * D : 4 * D])
    mixed = mixed.astype(bf16)
    grad_attended, grad_up, g_rows, up_sums = call(
        back_out_kernel,
        "back_out",
        (4,),
        [whole(a.shape) for a in grad_refs] + [whole((D, OUT_ROWS)), pairs(FFD)],
        [pairs(PAIR), pairs(FFD), pairs(D), fixed((1, FFD))],
        [shape((2, SEQ, n), bf16) for n in (PAIR, FFD)] + [pltpu.HBM((2, SEQ, D), bf16)] + [shape((1, FFD), f32)],
        scratch=[pltpu.VMEM((512, D), bf16)],
        prefetch=1,
    )(after(back, parts), *grad_refs, w_mix_turned, dgelu)

    grad_qkv, qkv_sums = call(
        attend_back_kernel,
        "attend_back",
        (2,),
        [rows(QKV, SEQ), rows(PAIR, SEQ), lse_spec, seg_row_spec, table, table],
        [rows(QKV, SEQ), pl.BlockSpec((1, 1, QKV), lambda i: (i, 0, 0))],
        [shape((tokens_n, QKV), bf16), shape((2, 1, QKV), f32)],
        scratch=[pltpu.VMEM((SEQ, PAIR), f32), pltpu.VMEM((SEQ, PAIR), f32)],
    )(flat(qkv), flat(grad_attended), lse, seg_row, cos, sin)

    block = shape((2, 128, D), bf16)
    *sent, ln_sums = call(
        back_in_kernel,
        "back_in",
        (4,),
        token_specs + [pairs(QKV), pairs(FFD), whole((D, IN_COLS))],
        [fixed((2, 128, D))] * 8 + [fixed((2, D))],
        [pltpu.HBM((2, 128, D), bf16)] * 8 + [shape((2, D), f32)],
        scratch=[pltpu.VMEM((512, D), bf16)],
        prefetch=1,
    )(back, *token_refs, grad_qkv.reshape(2, SEQ, QKV), grad_up, w_all)

    to_right, to_left, right0, left0, own0, right1, left1, own1 = sent
    a = shift(to_right, "x", 1)
    b = shift(to_left, "x", -1)
    first = pl.BlockSpec((1, 128, D), lambda i: (0, 0, 0))
    second = pl.BlockSpec((1, 128, D), lambda i: (1, 0, 0))
    right0, left0, right1, left1 = call(
        fold_kernel,
        "fold",
        (1,),
        [whole((2, 128, D))] * 2 + [first, second, first, second],
        [first, second, first, second],
        [block] * 4,
        alias={2: 0, 3: 1, 4: 2, 5: 3},
    )(a, b, right0, left0, right1, left1)
    from_left0 = shift(right0, "x", 1)
    from_right0 = shift(left0, "x", -1)
    from_left1 = shift(right1, "x", 1)
    from_right1 = shift(left1, "x", -1)
    one_seq = pl.BlockSpec((1, 128, D), lambda i: (i, 0, 0))
    total = call(column_sum_kernel, "column_sum", (2,), [one_seq] * 3, one_seq, block)(own0, from_left0, from_right0)
    from_other = shift(total, "yh", 1)
    grad_tokens = call(
        token_grad_kernel,
        "token_grad",
        (1,),
        [whole((2, 128, D))] * 6 + [pl.BlockSpec((1, D), lambda i: (0, 0))],
        fixed((2, 128, D)),
        block,
    )(tokens, out_grad, own1, from_left1, from_right1, from_other, small)

    g_rows = after(flat(g_rows), to_right)
    hidden = after(flat(hidden), to_right)
    grad_mix = dot(act_att, g_rows, TN).astype(bf16)
    grad_w_up = dot(hidden, flat(grad_up), TN).astype(bf16)
    grad_w_qkv = dot(hidden, grad_qkv, TN).astype(bf16)
    vec = [ln_sums.reshape(16, 128), g_sum.reshape(8, 128), jnp.sum(qkv_sums, axis=0).reshape(3, 128), up_sums.reshape(4, 128)]
    vec = jnp.pad(jnp.concatenate(vec).astype(bf16), ((0, 33), (0, 0)))
    halves = shape((8, 64, SHARD), bf16)
    own_half, other_half = call(
        chunk_kernel,
        "chunk",
        (1,),
        [whole((OUT_ROWS, D)), whole((D, FFD)), whole((D, QKV)), whole((64, 128))],
        [fixed(halves.shape)] * 2,
        [halves] * 2,
        prefetch=1,
    )(place, after(grad_mix, a, b), grad_w_up, grad_w_qkv, vec)
    got = shift(other_half, "c", 1)
    quarter = pl.BlockSpec((2, 64, SHARD), lambda i: (i, 0, 0))
    chip_half = call(pair_sum_kernel, "pair_sum", (4,), [quarter] * 2, quarter, halves)(own_half, got)
    got = lax.all_to_all(after(chip_half, right0, left0), ("z", "yl"), 0, 0, tiled=True)
    out_owned, rest_owned = call(
        owner_sum_kernel,
        "owner_sum",
        (1,),
        [whole(halves.shape)],
        [fixed((64, OUT_ROWS)), fixed((64, SHARD - OUT_ROWS))],
        [shape((64, OUT_ROWS), bf16), shape((64, SHARD - OUT_ROWS), bf16)],
    )(got)
    out_owned = lax.ppermute(out_owned, ALL, out_pairs(True))

    def spread_ctx(a):
        return lax.all_to_all(jnp.broadcast_to(a[None], (8,) + a.shape), ("yh", "x"), 0, 0, tiled=True)

    both = spread_ctx(after(jnp.concatenate([out_owned, rest_owned], axis=1), from_left1, from_right1, from_other))
    sizes = [(64, 3 * D), (64, 4 * D), (64, D), (256, D), (1, 64), (1, 64), (1, 192), (1, 64), (1, 64), (1, 256)]
    done = call(
        finish_kernel,
        "finish",
        (1,),
        [fixed((8, 64, SHARD))],
        [fixed(dims) for dims in sizes],
        [shape(dims, f32) for dims in sizes],
        scratch=[pltpu.VMEM((64, 128), f32), pltpu.VMEM((32, 128), f32), pltpu.VMEM((32, 128), f32)],
        prefetch=1,
    )(place, after(both, mixed))
    grad_w_qkv, grad_w_up, grad_w_out, grad_w_down = done[:4]
    grad_gain, grad_lbias, grad_bqkv, grad_bout, grad_bdown, grad_bup = [a.reshape(-1) for a in done[4:]]
    return (
        mixed,
        grad_tokens,
        grad_gain,
        grad_lbias,
        grad_w_qkv,
        grad_bqkv,
        grad_w_out,
        grad_bout,
        grad_w_up,
        grad_bup,
        grad_w_down,
        grad_bdown,
    )


def solution(mesh):
    fine = Mesh(mesh.devices.reshape(4, 2, 2, 2, 4), ALL)
    dp = ("z", "yl", "c")
    ctx = ("yh", "x")
    in_specs = (
        P(dp, ctx, None),
        P(dp, None),
        P(dp),
        P(dp),
        P(dp, None),
        P(dp),
        P(dp, None),
        P(dp),
        P(dp, None),
        P(dp),
        P(dp, None),
        P(dp),
        P(dp, ctx, None),
    )
    out_specs = (
        P(dp, ctx, None),
        P(dp, ctx, None),
        P(dp),
        P(dp),
        P(dp, None),
        P(dp),
        P(dp, None),
        P(dp),
        P(dp, None),
        P(dp),
        P(dp, None),
        P(dp),
    )
    return jax.shard_map(body, mesh=fine, in_specs=in_specs, out_specs=out_specs, check_vma=False)
```
